256 devices in a mesh: dp: 8 (over z), mp: 32 (over y, x, core).
Axes of the slice: x: 4, y: 4, z: 8, core: 2. Of those that a mesh axis runs over, the one named last changes fastest.
Arguments:
- grads: bfloat16 [8, 8, 1024, 1024], P('dp', None, 'mp'), may hold values from -0.15625 to 0.15625
- block_slot: int32 [8], replicated, may hold values from 0 to 15, as said below
- left_stats: float32 [16, 1024, 1024], P('dp', 'mp'), as said below
- right_stats: float32 [16, 1024, 1024], P('dp', 'mp'), as said below
- left_basis: bfloat16 [16, 1024, 1024], P('dp', 'mp'), as said below
- right_basis: bfloat16 [16, 1024, 1024], P('dp', 'mp'), as said below
- first_moment: float32 [16, 1024, 1024], P('dp', 'mp'), may hold values from -0.125 to 0.125
- second_moment: float32 [16, 1024, 1024], P('dp', 'mp'), may hold values from 4.8828126e-05 to 0.001953125
Outputs:
- update: bfloat16 [8, 1024, 1024], P('dp')
- new_left_stats: float32 [16, 1024, 1024], P('dp', 'mp')
- new_right_stats: float32 [16, 1024, 1024], P('dp', 'mp')
- new_left_basis: bfloat16 [16, 1024, 1024], P('dp', 'mp')
- new_right_basis: bfloat16 [16, 1024, 1024], P('dp', 'mp')
The draws below stay inside these ranges and needn't reach their ends.
Inputs may be any that keep to these rules, and one draw needn't show every extreme that they name: `block_slot`: distinct blocks name distinct slots; slot s belongs to index s // 2 of dp, and some index of dp holds 2 blocks in every draw. `left_stats`: every slot is symmetric positive definite. `right_stats`: every slot is symmetric positive definite. `left_basis`: every slot is invertible. `right_basis`: every slot is invertible.
All inputs are finite; a program needn't handle non-finite values.
Results may differ from the reference program's by a relative error of at most 0.022.
Values may be sent and summed in bfloat16 or wider, within the bound.
A program may use at most 192 MiB of HBM per device.

```python
import math
import jax
import jax.numpy as jnp
from jax import lax

B = 1024
CAP = 2
NBLK = 8
SLOTS = 16
N_DP = 8


def draw_block_slot(key, part):
    key_owner, key_rest, key_shuffle = jax.random.split(jax.random.fold_in(key, 7), 3)
    owner_count = SLOTS // CAP
    fullest = jax.random.randint(key_owner, (), 0, owner_count).astype(jnp.int32)
    spare_slots = jax.random.permutation(key_rest, SLOTS - CAP)[:NBLK - CAP].astype(jnp.int32)
    spare_slots = spare_slots + CAP * (spare_slots >= fullest * CAP).astype(jnp.int32)
    packed = jnp.concatenate([fullest * CAP + jnp.arange(CAP, dtype=jnp.int32), spare_slots])
    shuffle = jax.random.permutation(key_shuffle, NBLK)
    return packed[shuffle].astype(jnp.int32)


def definite_blocks(key):
    key_factor, key_scale = jax.random.split(key)
    factor = jax.random.normal(key_factor, (SLOTS, B, B), jnp.float32)
    row_scale = jax.random.uniform(key_scale, (SLOTS, B), jnp.float32, 0.8, 1.2)
    ridge = 0.25
    factor = factor * row_scale[:, :, None]
    product = jnp.einsum('sik,sjk->sij', factor, factor, precision=lax.Precision.HIGHEST, preferred_element_type=jnp.float32) * (0.5 / B)
    symmetric = 0.5 * (product + jnp.swapaxes(product, 1, 2))
    identity = jnp.eye(B, dtype=jnp.float32)
    return symmetric + ridge * identity


def dense_basis(key):
    key_matrix, key_sign, key_scale = jax.random.split(key, 3)
    matrix = jax.random.normal(key_matrix, (SLOTS, B, B), jnp.float32) * (0.3 / math.sqrt(B))
    column_scale = jax.random.uniform(key_scale, (SLOTS, B), jnp.float32, 0.8, 1.2)
    signs = jnp.where(jax.random.bernoulli(key_sign, 0.5, (SLOTS, B)), 1.0, -1.0).astype(jnp.float32)
    identity = jnp.eye(B, dtype=jnp.float32)
    dense = matrix * (1.0 - identity) + identity * signs[:, None, :]
    return (dense * column_scale[:, None, :]).astype(jnp.bfloat16)


def draw_left_stats(key, part):
    return definite_blocks(jax.random.fold_in(key, 11))


def draw_right_stats(key, part):
    return definite_blocks(jax.random.fold_in(key, 12))


def draw_left_basis(key, part):
    return dense_basis(jax.random.fold_in(key, 21))


def draw_right_basis(key, part):
    return dense_basis(jax.random.fold_in(key, 22))


def level_of(rng, shape, cuts, least, largest):
    gain, own = 1.0, jax.random.fold_in(rng, 6)
    for dim, shards_of in cuts:
        heights = jnp.exp(jax.random.uniform(jax.random.fold_in(own, dim), (shards_of,), jnp.float32, least / len(cuts), largest / len(cuts)))
        gain = gain * jnp.repeat(heights, shape[dim] // shards_of).reshape([-1 if axis == dim else 1 for axis in range(len(shape))])
    return gain


def normal_values(stream_key, shape, scale, bound, cuts=(), kind=jnp.bfloat16):
    loudness = level_of(stream_key, shape, cuts, -0.22, 0.18) if cuts else 1.0
    drawn = jax.random.normal(stream_key, shape, jnp.float32) * scale * loudness
    return jnp.minimum(jnp.maximum(drawn, -bound), bound).astype(kind)


def setup_inputs(seed: int = 0) -> dict:
    seeds = jax.random.split(jax.random.key(seed), 9)
    grads = normal_values(seeds[0], (N_DP, NBLK, B, B), (0.35 * B ** -0.5), 0.15625, ((0, 8), (2, 32)))
    block_slot = draw_block_slot(jax.random.fold_in(seeds[8], 71), 0)
    left_stats = draw_left_stats(jax.random.fold_in(seeds[8], 71), 0)
    right_stats = draw_right_stats(jax.random.fold_in(seeds[8], 71), 0)
    left_basis = draw_left_basis(jax.random.fold_in(seeds[8], 71), 0)
    right_basis = draw_right_basis(jax.random.fold_in(seeds[8], 71), 0)
    first_moment = normal_values(seeds[6], (SLOTS, B, B), (0.3 * B ** -0.5), 0.125, ((0, 8), (1, 32)), jnp.float32)
    second_moment = jnp.clip(jnp.exp(math.log(0.001953125) - 3.6888794 * jax.random.uniform(seeds[7], (SLOTS, B, B), jnp.float32) ** level_of(seeds[7], (SLOTS, B, B), ((0, 8), (1, 32)), -0.2, 0.2)), 4.882812572759576e-05, 0.001953125)
    return {"grads": grads, "block_slot": block_slot, "left_stats": left_stats, "right_stats": right_stats, "left_basis": left_basis, "right_basis": right_basis, "first_moment": first_moment, "second_moment": second_moment}


BETA_STATS = 0.95
BETA_FIRST = 0.9
BETA_SECOND = 0.95
EPSILON = 1e-08
highest = lax.Precision.HIGHEST

def lower_solve(factor, right_side, transpose):
    return jax.scipy.linalg.solve_triangular(factor, right_side, trans=transpose, lower=True)

def one_block(grad, left_stat, right_stat, left_old, right_old, first_old, second_old):
    left_next = BETA_STATS * left_stat + (1.0 - BETA_STATS) * jnp.dot(grad.astype(jnp.float32), grad.T.astype(jnp.float32), preferred_element_type=jnp.float32)
    right_next = BETA_STATS * right_stat + (1.0 - BETA_STATS) * jnp.dot(grad.T.astype(jnp.float32), grad.astype(jnp.float32), preferred_element_type=jnp.float32)
    left_power = jnp.dot(left_next.astype(jnp.bfloat16).astype(jnp.float32), left_old.astype(jnp.float32), preferred_element_type=jnp.float32).astype(jnp.bfloat16)
    right_power = jnp.dot(right_next.astype(jnp.bfloat16).astype(jnp.float32), right_old.astype(jnp.float32), preferred_element_type=jnp.float32).astype(jnp.bfloat16)
    left_factor = jnp.linalg.cholesky(jnp.dot(left_power.T.astype(jnp.float32), left_power.astype(jnp.float32), preferred_element_type=jnp.float32))
    right_factor = jnp.linalg.cholesky(jnp.dot(right_power.T.astype(jnp.float32), right_power.astype(jnp.float32), preferred_element_type=jnp.float32))
    left_q = lower_solve(left_factor, left_power.astype(jnp.float32).T, 0).T
    right_q = lower_solve(right_factor, right_power.astype(jnp.float32).T, 0).T
    moved_rows = jnp.dot(left_q.T.astype(jnp.float32), grad.astype(jnp.float32), precision=highest, preferred_element_type=jnp.float32)
    rotated = jnp.dot(moved_rows.astype(jnp.float32), right_q.astype(jnp.float32), precision=highest, preferred_element_type=jnp.float32)
    first_next = BETA_FIRST * first_old + (1.0 - BETA_FIRST) * rotated
    second_next = BETA_SECOND * second_old + (1.0 - BETA_SECOND) * rotated * rotated
    normed = first_next / (jnp.sqrt(second_next) + EPSILON)
    half = jnp.dot(normed.astype(jnp.float32), right_q.T.astype(jnp.float32), precision=highest, preferred_element_type=jnp.float32).astype(jnp.bfloat16)
    update = jnp.dot(left_q.astype(jnp.float32), half.astype(jnp.float32), precision=highest, preferred_element_type=jnp.float32).astype(jnp.bfloat16)
    return (update, left_next, right_next, left_q.astype(jnp.bfloat16), right_q.astype(jnp.bfloat16))

def reference(grads, block_slot, left_stats, right_stats, left_basis, right_basis, first_moment, second_moment):
    summed = lax.optimization_barrier(jnp.sum(grads.astype(jnp.float32), axis=0)).astype(jnp.bfloat16)

    def step_block(block_index):
        slot_index = block_slot[block_index]
        return one_block(summed[block_index], left_stats[slot_index], right_stats[slot_index], left_basis[slot_index], right_basis[slot_index], first_moment[slot_index], second_moment[slot_index])
    update, left_next, right_next, left_new, right_new = lax.map(step_block, jnp.arange(NBLK, dtype=jnp.int32))
    new_left_stats = left_stats.at[block_slot].set(left_next)
    new_right_stats = right_stats.at[block_slot].set(right_next)
    new_left_basis = left_basis.at[block_slot].set(left_new)
    new_right_basis = right_basis.at[block_slot].set(right_new)
    return (update, new_left_stats, new_right_stats, new_left_basis, new_right_basis)
```

```python
import functools

import jax
import jax.numpy as jnp
from jax import lax
from jax.experimental import pallas as pl
from jax.experimental.pallas import tpu as pltpu
from jax.sharding import Mesh
from jax.sharding import PartitionSpec as P

BETA_STATS = 0.95
BETA_FIRST = 0.9
BETA_SECOND = 0.95
EPSILON = 1e-08
F32 = jnp.float32
BF = jnp.bfloat16
T = 128
MP = ("y", "h", "s", "c")
QUAD = ("s", "c")
RING = ("y", "h")


def split(x):
    high = x.astype(BF)
    return high, (x - high.astype(F32)).astype(BF)


def dot3(a_parts, b_parts, dims):
    (ah, al), (bh, bl) = a_parts, b_parts
    dot = functools.partial(
        lax.dot_general, dimension_numbers=(dims, ((), ())), preferred_element_type=F32
    )
    return dot(ah, bh) + (dot(ah, bl) + dot(al, bh))


def base_factor(block):
    sub = lax.broadcasted_iota(jnp.int32, (8, T), 0)
    lane = lax.broadcasted_iota(jnp.int32, (8, T), 1)
    groups = T // 8
    rows = [block[8 * g : 8 * g + 8, :] for g in range(groups)]
    inv = [(lane == sub + 8 * g).astype(F32) for g in range(groups)]

    def spread(x, q):
        return jnp.broadcast_to(x[q : q + 1, :], (8, T))

    for g in range(groups):
        r, e = rows[g], inv[g]
        cols = [jnp.broadcast_to(r[:, 8 * g + q : 8 * g + q + 1], (8, T)) for q in range(8)]
        scale = jnp.zeros((8, T), F32)
        for q in range(8):
            pivot = spread(cols[q], q)
            scale = jnp.where(sub == q, pivot, scale)
            if q < 7:
                mult = jnp.where(sub > q, cols[q] / pivot, 0.0)
                r = r - mult * spread(r, q)
                e = e - mult * spread(e, q)
                for p in range(q + 1, 8):
                    cols[p] = cols[p] - mult * spread(cols[p], q)
        scale = lax.rsqrt(scale)
        r, e = r * scale, e * scale
        inv[g] = e
        if g < groups - 1:
            turned = r.T
            r_rows = [spread(r, q) for q in range(8)]
            e_rows = [spread(e, q) for q in range(8)]
            for h in range(g + 1, groups):
                x, y = rows[h], inv[h]
                for q in range(8):
                    m = jnp.broadcast_to(turned[8 * h : 8 * h + 8, q : q + 1], (8, T))
                    x = x - m * r_rows[q]
                    y = y - m * e_rows[q]
                rows[h], inv[h] = x, y
    return jnp.concatenate(inv, axis=0)


def factor_kernel(gram_ref, power_ref, q_ref, a, high, low):
    width = gram_ref.shape[0]
    left, right = slice(0, width), slice(width, 2 * width)
    a[...] = gram_ref[...]
    q_ref[...] = power_ref[...].astype(F32)

    def panel(i, carry):
        here = pl.ds(pl.multiple_of(i * T, T), T)
        inverse = split(base_factor(a[here, here]))
        u = dot3(inverse, split(a[here, :]), ((1,), (0,)))
        w = dot3(inverse, split(q_ref[here, :]), ((1,), (0,)))
        q_ref[here, :] = w
        high[:, left], low[:, left] = split(u)
        high[:, right], low[:, right] = split(w)

        def trail(j, inner):
            there = pl.ds(pl.multiple_of(j * T, T), T)
            m = (high[:, there], low[:, there])
            a[there, :] -= dot3(m, (high[:, left], low[:, left]), ((0,), (0,)))
            q_ref[there, :] -= dot3(m, (high[:, right], low[:, right]), ((0,), (0,)))
            return inner

        lax.fori_loop(i + 1, width // T, trail, 0)
        return carry

    lax.fori_loop(0, width // T, panel, 0)


def orthogonal(gram, power_t):
    width = gram.shape[0]
    return pl.pallas_call(
        factor_kernel,
        out_shape=jax.ShapeDtypeStruct((width, width), F32),
        in_specs=[pl.BlockSpec(memory_space=pltpu.VMEM)] * 2,
        out_specs=pl.BlockSpec(memory_space=pltpu.VMEM),
        scratch_shapes=[
            pltpu.VMEM((width, width), F32),
            pltpu.VMEM((T, 2 * width), BF),
            pltpu.VMEM((T, 2 * width), BF),
        ],
        compiler_params=pltpu.CompilerParams(vmem_limit_bytes=40 * 2**20),
    )(gram, power_t)


def dot(a, b, a_dim, b_dim):
    return lax.dot_general(a, b, (((a_dim,), (b_dim,)), ((), ())), preferred_element_type=F32)


def quad_exchange(pieces):
    return lax.all_to_all(pieces, QUAD, split_axis=0, concat_axis=0, tiled=True)


def per_device(
    grads, block_slot, left_stats, right_stats, left_basis, right_basis, first_moment, second_moment
):
    capacity, row_count, width = left_stats.shape
    group_size = lax.axis_size("dp")
    owner_index = lax.axis_index("dp")
    block_total = block_slot.shape[0]
    slot_total = capacity * group_size
    side, core = lax.axis_index("s"), lax.axis_index("c")
    ring_index = lax.axis_index(RING)
    local_grads = grads[0]
    slot_ids = owner_index * capacity + jnp.arange(capacity, dtype=jnp.int32)
    held = jnp.any(block_slot[:, None] == slot_ids[None, :], axis=0)
    local_index = block_slot - owner_index * capacity
    owned = (local_index >= 0) & (local_index < capacity)
    safe_index = jnp.clip(local_index, 0, capacity - 1)

    sent = jnp.concatenate(
        [
            jnp.concatenate([left_stats, right_stats], axis=0).astype(BF),
            jnp.concatenate([left_basis, right_basis], axis=0),
        ],
        axis=1,
    )
    got = quad_exchange(sent)
    got = got.reshape(4, 2, row_count, width).transpose(1, 0, 2, 3).reshape(2, 4 * row_count, width)
    old = lax.all_gather(got, RING, axis=1, tiled=True)
    old_stat, old_basis = old[0], old[1]
    moments = jnp.concatenate([first_moment, second_moment], axis=1).astype(BF)
    moments = quad_exchange(jnp.concatenate([moments, moments], axis=0))
    moments = moments.reshape(4, 2, row_count, width).astype(F32)
    first_old = moments[:, 0].reshape(4 * row_count, width)
    second_old = moments[:, 1].reshape(4 * row_count, width)

    placing = (
        block_slot[:, None] == lax.broadcasted_iota(jnp.int32, (block_total, slot_total), 1)
    ).astype(BF)
    slot_grads = jnp.einsum("bs,brc->src", placing, local_grads, preferred_element_type=F32)
    grad_rows = lax.psum_scatter(slot_grads.astype(BF), "dp", scatter_dimension=0, tiled=True)
    mine = jnp.where(core == 0, grad_rows[0], grad_rows[1])
    other = jnp.where(core == 0, grad_rows[1], grad_rows[0])
    came = lax.ppermute(other, "c", [(0, 1), (1, 0)])
    pair = jnp.where(core == 0, jnp.stack([mine, came]), jnp.stack([came, mine]))
    grad = lax.all_gather(
        pair.reshape(2 * row_count, width), ("y", "h", "s"), axis=0, tiled=True
    )

    term = lax.cond(
        side == 0, lambda g: dot(g, g, 1, 1), lambda g: dot(g, g, 0, 0), grad
    )
    stat = (BETA_STATS * old_stat.astype(F32) + (1.0 - BETA_STATS) * term).astype(BF)
    power_t = dot(old_basis, stat, 0, 0).astype(BF)
    gram = dot(power_t, power_t, 1, 1)
    q_t = orthogonal(gram, power_t)
    q_half = q_t.astype(BF)

    term_rows = lax.dynamic_slice_in_dim(term, ring_index * 4 * row_count, 4 * row_count, 0)
    terms = quad_exchange(term_rows.reshape(4, row_count, width))
    held_mask = held[:, None, None]
    new_left_stats = jnp.where(
        held_mask, BETA_STATS * left_stats + (1.0 - BETA_STATS) * terms[:2], left_stats
    )
    new_right_stats = jnp.where(
        held_mask, BETA_STATS * right_stats + (1.0 - BETA_STATS) * terms[2:], right_stats
    )

    q_cols = lax.dynamic_slice_in_dim(q_half, ring_index * 4 * row_count, 4 * row_count, 1)
    q_part = lax.dynamic_slice_in_dim(q_half, ring_index * 4 * row_count, 4 * row_count, 0)
    both = jnp.concatenate(
        [q_cols.T.reshape(4, row_count, width), q_part.reshape(4, row_count, width)], axis=1
    )
    both = quad_exchange(both)
    bases = both[:, :row_count]
    new_left_basis = jnp.where(held_mask, bases[:2], left_basis)
    new_right_basis = jnp.where(held_mask, bases[2:], right_basis)

    def to_home(slot_rows):
        picked = jnp.take(slot_rows, safe_index, axis=0)
        arrived = lax.all_to_all(
            jnp.where(owned[:, None, None], picked, jnp.zeros_like(picked)),
            "dp",
            split_axis=0,
            concat_axis=0,
            tiled=True,
        )
        return lax.all_gather(jnp.sum(arrived, axis=0), MP, axis=0, tiled=True)

    q_home = to_home(both[:2, row_count:])

    left_part = lax.ppermute(q_part, "s", [(0, 1), (1, 0)])
    moved = dot(grad, q_half, 1, 1).astype(BF)
    rotated = dot(left_part, moved, 1, 0)
    first_next = BETA_FIRST * first_old + (1.0 - BETA_FIRST) * rotated
    second_next = BETA_SECOND * second_old + (1.0 - BETA_SECOND) * rotated * rotated
    normed = first_next / (jnp.sqrt(second_next) + EPSILON)
    half = dot(normed.astype(BF), q_half, 1, 0).astype(BF)
    halves = quad_exchange(half.reshape(4, row_count, width))[2:]
    half_home = to_home(halves)
    update = dot(q_home, half_home, 0, 0).astype(BF)
    return (update[None], new_left_stats, new_right_stats, new_left_basis, new_right_basis)


def solution(mesh):
    groups = mesh.shape["dp"]
    fine = Mesh(mesh.devices.reshape(groups, 4, 2, 2, 2), ("dp",) + MP)
    rows = P("dp", MP, None)
    return jax.shard_map(
        per_device,
        mesh=fine,
        in_specs=(P("dp", None, MP, None), P()) + (rows,) * 6,
        out_specs=(P("dp", None, None),) + (rows,) * 4,
        check_vma=False,
    )
```

```python
import functools

import jax
import jax.numpy as jnp
from jax import lax
from jax.experimental import pallas as pl
from jax.experimental.pallas import tpu as pltpu
from jax.sharding import Mesh
from jax.sharding import PartitionSpec as P

BETA_STATS = 0.95
BETA_FIRST = 0.9
BETA_SECOND = 0.95
EPSILON = 1e-08
F32 = jnp.float32
BF = jnp.bfloat16
T = 128
MP = ("yh", "k", "xh", "s", "c")
MESH = pl.DeviceIdType.MESH
ANY = pl.BlockSpec(memory_space=pl.ANY)


def split(x):
    high = x.astype(BF)
    return high, (x - high.astype(F32)).astype(BF)


def dot3(a_parts, b_parts, dims):
    (ah, al), (bh, bl) = a_parts, b_parts
    dot = functools.partial(
        lax.dot_general, dimension_numbers=(dims, ((), ())), preferred_element_type=F32
    )
    return dot(ah, bh) + (dot(ah, bl) + dot(al, bh))


def base_factor(block):
    sub = lax.broadcasted_iota(jnp.int32, (8, T), 0)
    lane = lax.broadcasted_iota(jnp.int32, (8, T), 1)
    groups = T // 8
    rows = [block[8 * g : 8 * g + 8, :] for g in range(groups)]
    inv = [(lane == sub + 8 * g).astype(F32) for g in range(groups)]

    def spread(x, q):
        return jnp.broadcast_to(x[q : q + 1, :], (8, T))

    for g in range(groups):
        r, e = rows[g], inv[g]
        cols = [jnp.broadcast_to(r[:, 8 * g + q : 8 * g + q + 1], (8, T)) for q in range(8)]
        scale = jnp.zeros((8, T), F32)
        for q in range(8):
            pivot = spread(cols[q], q)
            scale = jnp.where(sub == q, pivot, scale)
            if q < 7:
                mult = jnp.where(sub > q, cols[q] / pivot, 0.0)
                r = r - mult * spread(r, q)
                e = e - mult * spread(e, q)
                for p in range(q + 1, 8):
                    cols[p] = cols[p] - mult * spread(cols[p], q)
        scale = lax.rsqrt(scale)
        r, e = r * scale, e * scale
        inv[g] = e
        if g < groups - 1:
            turned = r.T
            r_rows = [spread(r, q) for q in range(8)]
            e_rows = [spread(e, q) for q in range(8)]
            for h in range(g + 1, groups):
                x, y = rows[h], inv[h]
                for q in range(8):
                    m = jnp.broadcast_to(turned[8 * h : 8 * h + 8, q : q + 1], (8, T))
                    x = x - m * r_rows[q]
                    y = y - m * e_rows[q]
                rows[h], inv[h] = x, y
    return jnp.concatenate(inv, axis=0)


def factor_kernel(gram_ref, power_ref, q_ref, a, high, low):
    width = gram_ref.shape[0]
    left, right = slice(0, width), slice(width, 2 * width)
    a[...] = gram_ref[...]
    q_ref[...] = power_ref[...].astype(F32)

    def panel(i, carry):
        here = pl.ds(pl.multiple_of(i * T, T), T)
        inverse = split(base_factor(a[here, here]))
        u = dot3(inverse, split(a[here, :]), ((1,), (0,)))
        w = dot3(inverse, split(q_ref[here, :]), ((1,), (0,)))
        q_ref[here, :] = w
        high[:, left], low[:, left] = split(u)
        high[:, right], low[:, right] = split(w)

        def trail(j, inner):
            there = pl.ds(pl.multiple_of(j * T, T), T)
            m = (high[:, there], low[:, there])
            a[there, :] -= dot3(m, (high[:, left], low[:, left]), ((0,), (0,)))
            q_ref[there, :] -= dot3(m, (high[:, right], low[:, right]), ((0,), (0,)))
            return inner

        lax.fori_loop(i + 1, width // T, trail, 0)
        return carry

    lax.fori_loop(0, width // T, panel, 0)


def orthogonal(gram, power_t):
    width = gram.shape[0]
    return pl.pallas_call(
        factor_kernel,
        out_shape=jax.ShapeDtypeStruct((width, width), F32),
        in_specs=[pl.BlockSpec(memory_space=pltpu.VMEM)] * 2,
        out_specs=pl.BlockSpec(memory_space=pltpu.VMEM),
        scratch_shapes=[
            pltpu.VMEM((width, width), F32),
            pltpu.VMEM((T, 2 * width), BF),
            pltpu.VMEM((T, 2 * width), BF),
        ],
        compiler_params=pltpu.CompilerParams(vmem_limit_bytes=40 * 2**20),
    )(gram, power_t)


def dot(a, b, a_dim, b_dim):
    return lax.dot_general(a, b, (((a_dim,), (b_dim,)), ((), ())), preferred_element_type=F32)


def chip_coords(t):
    return {"yh": t // 8, "k": (t // 4) % 2, "xh": (t // 2) % 2, "s": t % 2}


def place():
    yh, k, xh, s, c = (lax.axis_index(a) for a in MP)
    return ((yh * 2 + k) * 2 + xh) * 2 + s, c


def remote(src, dst, send, recv, coords):
    return pltpu.make_async_remote_copy(
        src_ref=src, dst_ref=dst, send_sem=send, recv_sem=recv, device_id=coords, device_id_type=MESH
    )


def greet(me, chip, core):
    barrier = pltpu.get_barrier_semaphore()

    def to_dp(j, carry):
        pl.semaphore_signal(barrier, inc=1, device_id={"dp": (me + j) % 8}, device_id_type=MESH)
        return carry

    def to_chip(j, carry):
        pl.semaphore_signal(
            barrier, inc=1, device_id=chip_coords((chip + j) % 16), device_id_type=MESH
        )
        return carry

    lax.fori_loop(1, 8, to_dp, 0)
    lax.fori_loop(1, 16, to_chip, 0)
    pl.semaphore_signal(barrier, inc=1, device_id={"c": 1 - core}, device_id_type=MESH)
    pl.semaphore_wait(barrier, 7 + 15 + 1)


def loop(low, high, body):
    def step(j, carry):
        body(j)
        return carry

    lax.fori_loop(low, high, step, 0)


def gather_kernel(
    slot_grads, state, moments, grad_out, stat_out, basis_out, moments_out,
    parts, total, dp_send, dp_recv, state_send, state_recv, quad_send, quad_recv,
    grad_send, grad_recv, pair_send, pair_recv, own,
):
    me = lax.axis_index("dp")
    chip, core = place()
    quad_base = chip - 4 * ((chip // 4) % 2) - chip % 2
    local = 2 * ((chip // 4) % 2) + chip % 2
    pair = {"c": 1 - core}
    greet(me, chip, core)

    def dp_copy(j, source):
        there = (me + j) % 8
        return remote(
            slot_grads.at[there], parts.at[source], dp_send.at[there], dp_recv.at[source], {"dp": there}
        )

    def state_copy(which, out, j, source):
        there = (chip + j) % 16
        return remote(
            state.at[(there // 4) % 2, there % 2, which],
            out.at[source, core],
            state_send.at[which, there],
            state_recv.at[which, source],
            chip_coords(there),
        )

    def quad_copy(j, source):
        number = (local + j) % 4
        there = quad_base + 4 * (number // 2) + number % 2
        return remote(
            moments.at[number // 2],
            moments_out.at[source],
            quad_send.at[number],
            quad_recv.at[source],
            chip_coords(there),
        )

    def grad_copy(j, source):
        there = (chip + j) % 16
        return remote(
            total.at[(there // 4) % 2],
            grad_out.at[source, core],
            grad_send.at[there],
            grad_recv.at[source],
            chip_coords(there),
        )

    loop(1, 8, lambda j: dp_copy(j, me).start())
    mine = pltpu.make_async_copy(slot_grads.at[me], parts.at[me], own.at[0])
    mine.start()
    k, s = (chip // 4) % 2, chip % 2
    keep = [
        pltpu.make_async_copy(state.at[k, s, 0], stat_out.at[chip, core], own.at[1]),
        pltpu.make_async_copy(state.at[k, s, 1], basis_out.at[chip, core], own.at[2]),
        pltpu.make_async_copy(moments.at[k], moments_out.at[local], own.at[3]),
    ]
    for copy in keep:
        copy.start()
    loop(1, 16, lambda j: state_copy(0, stat_out, j, chip).start())
    loop(1, 16, lambda j: state_copy(1, basis_out, j, chip).start())
    loop(1, 4, lambda j: quad_copy(j, local).start())

    mine.wait()
    loop(1, 8, lambda j: dp_copy(j, (me + 8 - j) % 8).wait_recv())
    for slot in range(2):
        acc = parts[0, slot].astype(F32)
        for d in range(1, 8):
            acc = acc + parts[d, slot].astype(F32)
        total[slot] = acc.astype(BF)
    loop(1, 16, lambda j: grad_copy(j, chip).start())
    last = pltpu.make_async_copy(total.at[k], grad_out.at[chip, core], own.at[4])
    last.start()

    def share(out, n):
        return remote(out.at[:, core], out.at[:, core], pair_send.at[n], pair_recv.at[n], pair)

    def shared(out, n):
        return remote(out.at[:, 1 - core], out.at[:, 1 - core], pair_send.at[n], pair_recv.at[n], pair)

    for copy in keep:
        copy.wait()
    loop(1, 16, lambda j: state_copy(0, stat_out, j, (chip + 16 - j) % 16).wait_recv())
    share(stat_out, 0).start()
    loop(1, 16, lambda j: state_copy(1, basis_out, j, (chip + 16 - j) % 16).wait_recv())
    share(basis_out, 1).start()
    last.wait()
    loop(1, 16, lambda j: grad_copy(j, (chip + 16 - j) % 16).wait_recv())
    share(grad_out, 2).start()
    loop(1, 4, lambda j: quad_copy(j, (local + 4 - j) % 4).wait_recv())
    for n, out in enumerate((stat_out, basis_out, grad_out)):
        shared(out, n).wait_recv()
        share(out, n).wait_send()
    loop(1, 8, lambda j: dp_copy(j, me).wait_send())
    loop(1, 16, lambda j: state_copy(0, stat_out, j, chip).wait_send())
    loop(1, 16, lambda j: state_copy(1, basis_out, j, chip).wait_send())
    loop(1, 16, lambda j: grad_copy(j, chip).wait_send())
    loop(1, 4, lambda j: quad_copy(j, local).wait_send())


def gather_inputs(slot_grads, state, moments):
    rows, width = state.shape[-2:]
    full = jax.ShapeDtypeStruct((16, 2, rows, width), BF)
    dma = pltpu.SemaphoreType.DMA
    return pl.pallas_call(
        gather_kernel,
        out_shape=(full, full, full, jax.ShapeDtypeStruct((4, 2, rows, width), BF)),
        in_specs=[ANY] * 3,
        out_specs=(ANY,) * 4,
        scratch_shapes=[
            pltpu.VMEM((8, 2, rows, width), BF),
            pltpu.VMEM((2, rows, width), BF),
            dma((8,)), dma((8,)), dma((2, 16)), dma((2, 16)), dma((4,)), dma((4,)),
            dma((16,)), dma((16,)), dma((3,)), dma((3,)), dma((5,)),
        ],
        compiler_params=pltpu.CompilerParams(
            collective_id=0, has_side_effects=True, vmem_limit_bytes=16 * 2**20
        ),
    )(slot_grads, state, moments)


def home_kernel(
    owned, payload, term, q, home_out, terms_out, bases_out,
    box, pieces, parts, total, dp_send, dp_recv, box_send, box_recv, row_send, row_recv,
    home_send, home_recv, pair_send, pair_recv, own,
):
    me = lax.axis_index("dp")
    chip, core = place()
    quad_base = chip - 4 * ((chip // 4) % 2) - chip % 2
    local = 2 * ((chip // 4) % 2) + chip % 2
    rows = payload.shape[1]
    pair = {"c": 1 - core}
    greet(me, chip, core)

    def member(number):
        return quad_base + 4 * (number // 2) + number % 2

    def box_copy(j, source):
        number = (local + j) % 4
        return remote(
            payload.at[number], box.at[source], box_send.at[number], box_recv.at[source],
            chip_coords(member(number)),
        )

    def row_copy(which, j, source):
        number = (local + j) % 4
        there = member(number)
        src, out = ((term, terms_out), (q, bases_out))[which]
        return remote(
            src.at[2 * there + core], out.at[source], row_send.at[which, number],
            row_recv.at[which, source], chip_coords(there),
        )

    def dp_copy(j, source):
        there = (me + j) % 8
        return remote(
            pieces.at[there], parts.at[source], dp_send.at[there], dp_recv.at[source], {"dp": there}
        )

    def home_copy(j, source):
        there = (chip + j) % 16
        return remote(
            total, home_out.at[:, source, core], home_send.at[there], home_recv.at[source],
            chip_coords(there),
        )

    loop(1, 4, lambda j: box_copy(j, local).start())
    mine = pltpu.make_async_copy(payload.at[local], box.at[local], own.at[0])
    mine.start()
    mine.wait()
    loop(1, 4, lambda j: box_copy(j, (local + 4 - j) % 4).wait_recv())

    def piece(b):
        first, second = owned[2 * b], owned[2 * b + 1]
        for which in range(2):
            pieces[b, which] = (
                box[which].astype(F32) * first + box[2 + which].astype(F32) * second
            ).astype(BF)

    def send_piece(j):
        piece((me + j) % 8)
        dp_copy(j, me).start()

    loop(1, 8, send_piece)
    piece(me)
    keep = [
        pltpu.make_async_copy(pieces.at[me], parts.at[me], own.at[1]),
        pltpu.make_async_copy(term.at[2 * chip + core], terms_out.at[local], own.at[2]),
        pltpu.make_async_copy(q.at[2 * chip + core], bases_out.at[local], own.at[3]),
    ]
    for copy in keep:
        copy.start()
    loop(1, 4, lambda j: row_copy(0, j, local).start())
    loop(1, 4, lambda j: row_copy(1, j, local).start())
    for copy in keep:
        copy.wait()
    loop(1, 8, lambda j: dp_copy(j, (me + 8 - j) % 8).wait_recv())
    for which in range(2):
        acc = parts[0, which].astype(F32)
        for d in range(1, 8):
            acc = acc + parts[d, which].astype(F32)
        total[which] = acc.astype(BF)
    loop(1, 16, lambda j: home_copy(j, chip).start())
    last = pltpu.make_async_copy(total, home_out.at[:, chip, core], own.at[4])
    last.start()
    last.wait()
    loop(1, 16, lambda j: home_copy(j, (chip + 16 - j) % 16).wait_recv())
    share = remote(
        home_out.at[:, :, core], home_out.at[:, :, core], pair_send.at[0], pair_recv.at[0], pair
    )
    share.start()
    other = 1 - core
    remote(
        home_out.at[:, :, other], home_out.at[:, :, other], pair_send.at[0], pair_recv.at[0], pair
    ).wait_recv()
    share.wait_send()
    for which in range(2):
        loop(1, 4, lambda j: row_copy(which, j, (local + 4 - j) % 4).wait_recv())
        loop(1, 4, lambda j: row_copy(which, j, local).wait_send())
    loop(1, 4, lambda j: box_copy(j, local).wait_send())
    loop(1, 8, lambda j: dp_copy(j, me).wait_send())
    loop(1, 16, lambda j: home_copy(j, chip).wait_send())


def bring_home(owned, payload, term, q):
    rows, width = payload.shape[-2:]
    dma = pltpu.SemaphoreType.DMA
    return pl.pallas_call(
        home_kernel,
        out_shape=(
            jax.ShapeDtypeStruct((2, 16, 2, rows, width), BF),
            jax.ShapeDtypeStruct((4, rows, width), F32),
            jax.ShapeDtypeStruct((4, rows, width), BF),
        ),
        in_specs=[pl.BlockSpec(memory_space=pltpu.SMEM), ANY, ANY, ANY],
        out_specs=(ANY,) * 3,
        scratch_shapes=[
            pltpu.VMEM((4, rows, width), BF),
            pltpu.VMEM((8, 2, rows, width), BF),
            pltpu.VMEM((8, 2, rows, width), BF),
            pltpu.VMEM((2, rows, width), BF),
            dma((8,)), dma((8,)), dma((4,)), dma((4,)), dma((2, 4)), dma((2, 4)),
            dma((16,)), dma((16,)), dma((1,)), dma((1,)), dma((5,)),
        ],
        compiler_params=pltpu.CompilerParams(
            collective_id=1, has_side_effects=True, vmem_limit_bytes=16 * 2**20
        ),
    )(owned, payload, term, q)


def per_device(
    grads, block_slot, left_stats, right_stats, left_basis, right_basis, first_moment, second_moment
):
    capacity, rows, width = left_stats.shape
    group_size = lax.axis_size("dp")
    block_total = block_slot.shape[0]
    slot_total = capacity * group_size
    side = lax.axis_index("s")
    slot_ids = lax.axis_index("dp") * capacity + jnp.arange(capacity, dtype=jnp.int32)
    owns = block_slot[:, None] == slot_ids[None, :]
    held_mask = jnp.any(owns, axis=0)[:, None, None]

    placing = (
        block_slot[:, None] == lax.broadcasted_iota(jnp.int32, (block_total, slot_total), 1)
    ).astype(BF)
    slot_grads = jnp.einsum("bs,brc->src", placing, grads[0], preferred_element_type=F32).astype(BF)
    stats = jnp.stack([left_stats, right_stats], axis=1).astype(BF)
    bases = jnp.stack([left_basis, right_basis], axis=1)
    grad, old_stat, old_basis, moments = gather_inputs(
        slot_grads.reshape(group_size, capacity, rows, width),
        jnp.stack([stats, bases], axis=2),
        jnp.stack([first_moment, second_moment], axis=1).astype(BF),
    )
    grad, old_stat, old_basis = (
        x.reshape(width, width) for x in (grad, old_stat, old_basis)
    )
    first_old = moments[:, 0].astype(F32).reshape(4 * rows, width)
    second_old = moments[:, 1].astype(F32).reshape(4 * rows, width)

    term = lax.cond(side == 0, lambda g: dot(g, g, 1, 1), lambda g: dot(g, g, 0, 0), grad)
    stat = (BETA_STATS * old_stat.astype(F32) + (1.0 - BETA_STATS) * term).astype(BF)
    power_t = dot(old_basis, stat, 0, 0).astype(BF)
    gram = dot(power_t, power_t, 1, 1)
    q_t = orthogonal(gram, power_t).astype(BF)

    yh, xh, core = (lax.axis_index(a) for a in ("yh", "xh", "c"))
    parts = q_t.reshape(2, 2, 2, 2, 2, rows, width)
    parts = lax.dynamic_index_in_dim(parts, yh, 0, keepdims=False)
    parts = lax.dynamic_index_in_dim(parts, xh, 1, keepdims=False)
    parts = lax.dynamic_index_in_dim(parts, core, 2, keepdims=False)
    q_part = parts.reshape(4 * rows, width)
    left_part = lax.ppermute(q_part, "s", [(0, 1), (1, 0)])
    moved = dot(grad, q_t, 1, 1).astype(BF)
    rotated = dot(left_part, moved, 1, 0)
    first_next = BETA_FIRST * first_old + (1.0 - BETA_FIRST) * rotated
    second_next = BETA_SECOND * second_old + (1.0 - BETA_SECOND) * rotated * rotated
    normed = first_next / (jnp.sqrt(second_next) + EPSILON)
    half = dot(normed.astype(BF), q_t, 1, 0).astype(BF)

    payload = jnp.where(side == 0, q_part, half).reshape(4, rows, width)
    home, terms, new_bases = bring_home(
        owns.astype(F32).reshape(block_total * capacity),
        payload,
        term.reshape(width // rows, rows, width),
        q_t.T.reshape(width // rows, rows, width),
    )
    home = home.reshape(2, width, width)
    update = dot(home[0], home[1], 0, 0).astype(BF)

    def merged(new, old):
        return jnp.where(held_mask, new, old)

    terms = terms.reshape(2, 2, rows, width)
    new_bases = new_bases.reshape(2, 2, rows, width)
    return (
        update[None],
        merged(BETA_STATS * left_stats + (1.0 - BETA_STATS) * terms[:, 0], left_stats),
        merged(BETA_STATS * right_stats + (1.0 - BETA_STATS) * terms[:, 1], right_stats),
        merged(new_bases[:, 0], left_basis),
        merged(new_bases[:, 1], right_basis),
    )


def solution(mesh):
    groups = mesh.shape["dp"]
    fine = Mesh(mesh.devices.reshape(groups, 2, 2, 2, 2, 2), ("dp",) + MP)
    rows = P("dp", MP, None)
    return jax.shard_map(
        per_device,
        mesh=fine,
        in_specs=(P("dp", None, MP, None), P()) + (rows,) * 6,
        out_specs=(P("dp", None, None),) + (rows,) * 4,
        check_vma=False,
    )
```

```python
import functools

import jax
import jax.numpy as jnp
from jax import lax
from jax.experimental import pallas as pl
from jax.experimental.pallas import tpu as pltpu
from jax.sharding import Mesh
from jax.sharding import PartitionSpec as P

BETA_STATS = 0.95
BETA_FIRST = 0.9
BETA_SECOND = 0.95
EPSILON = 1e-08
F32 = jnp.float32
BF = jnp.bfloat16
T = 128
MP = ("yh", "k", "xh", "s", "c")
MESH = pl.DeviceIdType.MESH
ANY = pl.BlockSpec(memory_space=pl.ANY)


def split(x):
    high = x.astype(BF)
    return high, (x - high.astype(F32)).astype(BF)


def dot(a, b, a_dim, b_dim):
    return lax.dot_general(a, b, (((a_dim,), (b_dim,)), ((), ())), preferred_element_type=F32)


def reciprocal(x):
    r = pl.reciprocal(x, approx=True)
    return r * (2.0 - x * r)


def tree(terms):
    while len(terms) > 1:
        terms = [a + b for a, b in zip(terms[::2], terms[1::2])]
    return terms[0]


def base_factor(block, hook):
    sub = lax.broadcasted_iota(jnp.int32, (8, T), 0)
    lane = lax.broadcasted_iota(jnp.int32, (8, T), 1)
    groups = T // 8

    def spread(x, q):
        return jnp.broadcast_to(x[q : q + 1, :], (8, T))

    def column(x, at):
        return jnp.broadcast_to(x[:, at : at + 1], (8, T))

    eye = lax.broadcasted_iota(jnp.int32, (T, T), 0) == lax.broadcasted_iota(jnp.int32, (T, T), 1)
    diag = jnp.where(eye, block, 0.0)
    across = lax.rsqrt(jnp.sum(diag, axis=0, keepdims=True))
    down = jnp.sum(jnp.where(eye, jnp.broadcast_to(across, (T, T)), 0.0), axis=1, keepdims=True)
    block = block * across * down
    rows = [block[8 * g : 8 * g + 8, :] for g in range(groups)]
    inv = [(lane == sub + 8 * g).astype(F32) for g in range(groups)]
    out = []
    for g in range(groups):
        r, e = rows[g], inv[g]
        f = e
        cols = [column(r, 8 * g + q) for q in range(8)]
        scale = jnp.zeros((8, T), F32)
        coef = jnp.zeros((8, T), F32)
        for q in range(0, 8, 2):
            x, y = cols[q], cols[q + 1]
            a, b, c = spread(x, q), spread(x, q + 1), spread(y, q + 1)
            det = a * c - b * b
            rd = reciprocal(det)
            i11, i22, i12 = c * rd, a * rd, -(b * rd)
            root = lax.rsqrt(a)
            scale = jnp.where(sub == q, root, scale)
            scale = jnp.where(sub == q + 1, a * root * lax.rsqrt(det), scale)
            coef = jnp.where(sub == q + 1, b * root * root, coef)
            m0 = x * i11 + y * i12
            m1 = x * i12 + y * i22
            if q < 6:
                f = f - (
                    jnp.where(sub > q + 1, m0, 0.0) * spread(f, q)
                    + jnp.where(sub > q + 1, m1, 0.0) * spread(f, q + 1)
                )
            m0 = jnp.where(sub == q, 1.0 - i11, jnp.where(sub == q + 1, -i12, m0))
            m1 = jnp.where(sub == q, -i12, jnp.where(sub == q + 1, 1.0 - i22, m1))
            for p in range(q + 2, 8):
                cols[p] = cols[p] - (m0 * spread(cols[p], q) + m1 * spread(cols[p], q + 1))
            if g < groups - 1:
                r = r - (m0 * spread(r, q) + m1 * spread(r, q + 1))
                e = e - (m0 * spread(e, q) + m1 * spread(e, q + 1))
        out.append((f - coef * pltpu.roll(f, 1, 0)) * scale * across)
        hook(g)
        if g < groups - 1:
            rr = [spread(r, q) for q in range(8)]
            ee = [spread(e, q) for q in range(8)]
            for h in range(g + 1, groups):
                m = [column(rows[h], 8 * g + q) for q in range(8)]
                rows[h] = rows[h] - tree([m[q] * rr[q] for q in range(8)])
                inv[h] = inv[h] - tree([m[q] * ee[q] for q in range(8)])
    return jnp.concatenate(out, axis=0)


def loop(low, high, body):
    def step(j, carry):
        body(j)
        return carry

    lax.fori_loop(low, high, step, 0)


def core_kernel(
    where, grad, old_stat, basis, q_t, q_part, q_rows, term_rows, a, q, stat, mul, cat, d_ref, turned
):
    width = grad.shape[0]
    rows = q_part.shape[1]
    half = width // 4
    side, core, corner = where[0], where[1], where[2]

    def tile(j):
        return pl.ds(pl.multiple_of(j * half, half), half)

    @pl.when(side == 0)
    def _():
        def body(j):
            a[tile(j), :] = dot(grad[tile(j), :], grad[...], 1, 1)

        loop(0, 4, body)

    @pl.when(side != 0)
    def _():
        def body(j):
            a[tile(j), :] = dot(grad[:, tile(j)], grad[...], 0, 0)

        loop(0, 4, body)

    def owned_rows(n):
        chip = corner + 4 * (n // 2) + n % 2
        return pl.ds(pl.multiple_of((2 * chip + core) * rows, rows), rows)

    for n in range(4):
        term_rows[n] = a[owned_rows(n), :]

    def mix(j):
        stat[tile(j), :] = (
            BETA_STATS * old_stat[tile(j), :].astype(F32) + (1.0 - BETA_STATS) * a[tile(j), :]
        ).astype(BF)

    loop(0, 4, mix)

    def power(j):
        q[tile(j), :] = dot(basis[:, tile(j)], stat[...], 0, 0).astype(BF).astype(F32)

    loop(0, 4, power)

    def keep(j):
        stat[tile(j), :] = q[tile(j), :].astype(BF)

    loop(0, 4, keep)

    def gram(j):
        a[tile(j), :] = dot(stat[tile(j), :], stat[...], 1, 1)

    loop(0, 4, gram)

    mul[...] = jnp.zeros_like(mul)
    cat[...] = jnp.zeros_like(cat)
    d_ref[...] = a[0:T, 0:T]
    lane = lax.broadcasted_iota(jnp.int32, (T, width), 1)

    def trail(g):
        if g % 2 == 0:
            return
        start = g // 2 * T
        there = slice(start, start + T)
        m = mul[:, there]
        a[there, start:width] -= dot(m, cat[:, start:width], 0, 0)
        q[there, :] -= dot(m, cat[:, width : 2 * width], 0, 0)

    def panel(i):
        here = pl.ds(pl.multiple_of(i * T, T), T)
        high, low = split(base_factor(d_ref[...], trail))
        inverse = jnp.concatenate([high, low, high], axis=1)
        for ref, start in ((a, 0), (q, width)):
            high, low = split(ref[here, :])
            u = dot(inverse, jnp.concatenate([high, high, low], axis=0), 1, 0)
            high, low = split(u)
            part = slice(start, start + width)
            cat[0:T, part], cat[T : 2 * T, part], cat[2 * T : 3 * T, part] = high, high, low
            if start == 0:
                high, low = split(jnp.where(lane >= (i + 1) * T, u, 0.0))
                mul[0:T, :], mul[T : 2 * T, :], mul[2 * T : 3 * T, :] = high, low, high
            else:
                q[here, :] = u
        following = pl.ds(pl.multiple_of(jnp.minimum(i + 1, width // T - 1) * T, T), T)
        d_ref[...] = a[following, following] - dot(mul[:, following], cat[:, following], 0, 0)

    loop(0, width // T, panel)

    def out(j):
        q_t[tile(j), :] = q[tile(j), :].astype(BF)

    loop(0, 4, out)
    for n in range(4):
        q_part[n] = q[owned_rows(n), :].astype(BF)
    for k in range(2):
        columns = pl.ds(pl.multiple_of((corner + 4 * k) // 2 * T, T), T)
        turned[...] = q[:, columns].T
        for side_to in range(2):
            these = pl.ds(pl.multiple_of((2 * side_to + core) * rows, rows), rows)
            q_rows[2 * k + side_to] = turned[these, :].astype(BF)


def factored(where, grad, old_stat, basis, rows):
    width = grad.shape[0]
    vmem = pl.BlockSpec(memory_space=pltpu.VMEM)
    return pl.pallas_call(
        core_kernel,
        out_shape=(
            jax.ShapeDtypeStruct((width, width), BF),
            jax.ShapeDtypeStruct((4, rows, width), BF),
            jax.ShapeDtypeStruct((4, rows, width), BF),
            jax.ShapeDtypeStruct((4, rows, width), F32),
        ),
        in_specs=[pl.BlockSpec(memory_space=pltpu.SMEM), vmem, vmem, vmem],
        out_specs=(vmem,) * 4,
        scratch_shapes=[
            pltpu.VMEM((width, width), F32),
            pltpu.VMEM((width, width), F32),
            pltpu.VMEM((width, width), BF),
            pltpu.VMEM((3 * T, width), BF),
            pltpu.VMEM((3 * T, 2 * width), BF),
            pltpu.VMEM((T, T), F32),
            pltpu.VMEM((T, width), F32),
        ],
        compiler_params=pltpu.CompilerParams(vmem_limit_bytes=48 * 2**20),
    )(where, grad, old_stat, basis)


def chip_coords(t):
    return {"yh": t // 8, "k": (t // 4) % 2, "xh": (t // 2) % 2, "s": t % 2}


def place():
    yh, k, xh, s, c = (lax.axis_index(a) for a in MP)
    return ((yh * 2 + k) * 2 + xh) * 2 + s, c


def remote(src, dst, send, recv, coords):
    return pltpu.make_async_remote_copy(
        src_ref=src, dst_ref=dst, send_sem=send, recv_sem=recv, device_id=coords, device_id_type=MESH
    )


def greet(me, chip, core):
    barrier = pltpu.get_barrier_semaphore()

    def to_dp(j, carry):
        pl.semaphore_signal(barrier, inc=1, device_id={"dp": (me + j) % 8}, device_id_type=MESH)
        return carry

    def to_chip(j, carry):
        pl.semaphore_signal(
            barrier, inc=1, device_id=chip_coords((chip + j) % 16), device_id_type=MESH
        )
        return carry

    lax.fori_loop(1, 8, to_dp, 0)
    lax.fori_loop(1, 16, to_chip, 0)
    pl.semaphore_signal(barrier, inc=1, device_id={"c": 1 - core}, device_id_type=MESH)
    pl.semaphore_wait(barrier, 7 + 15 + 1)


def gather_kernel(
    slot_grads, state, moments, grad_out, stat_out, basis_out, moments_out,
    parts, total, dp_send, dp_recv, state_send, state_recv, quad_send, quad_recv,
    grad_send, grad_recv, pair_send, pair_recv, own,
):
    me = lax.axis_index("dp")
    chip, core = place()
    quad_base = chip - 4 * ((chip // 4) % 2) - chip % 2
    local = 2 * ((chip // 4) % 2) + chip % 2
    pair = {"c": 1 - core}
    greet(me, chip, core)

    def dp_copy(j, source):
        there = (me + j) % 8
        return remote(
            slot_grads.at[there], parts.at[source], dp_send.at[there], dp_recv.at[source], {"dp": there}
        )

    def state_copy(which, out, j, source):
        there = (chip + j) % 16
        return remote(
            state.at[(there // 4) % 2, there % 2, which],
            out.at[source, core],
            state_send.at[which, there],
            state_recv.at[which, source],
            chip_coords(there),
        )

    def quad_copy(j, source):
        number = (local + j) % 4
        there = quad_base + 4 * (number // 2) + number % 2
        return remote(
            moments.at[number // 2],
            moments_out.at[source],
            quad_send.at[number],
            quad_recv.at[source],
            chip_coords(there),
        )

    def grad_copy(j, source):
        there = (chip + j) % 16
        return remote(
            total.at[(there // 4) % 2],
            grad_out.at[source, core],
            grad_send.at[there],
            grad_recv.at[source],
            chip_coords(there),
        )

    loop(1, 8, lambda j: dp_copy(j, me).start())
    mine = pltpu.make_async_copy(slot_grads.at[me], parts.at[me], own.at[0])
    mine.start()
    k, s = (chip // 4) % 2, chip % 2
    keep = [
        pltpu.make_async_copy(state.at[k, s, 0], stat_out.at[chip, core], own.at[1]),
        pltpu.make_async_copy(state.at[k, s, 1], basis_out.at[chip, core], own.at[2]),
        pltpu.make_async_copy(moments.at[k], moments_out.at[local], own.at[3]),
    ]
    for copy in keep:
        copy.start()
    loop(1, 16, lambda j: state_copy(0, stat_out, j, chip).start())
    loop(1, 16, lambda j: state_copy(1, basis_out, j, chip).start())
    loop(1, 4, lambda j: quad_copy(j, local).start())

    mine.wait()
    loop(1, 8, lambda j: dp_copy(j, (me + 8 - j) % 8).wait_recv())
    for slot in range(2):
        acc = parts[0, slot].astype(F32)
        for d in range(1, 8):
            acc = acc + parts[d, slot].astype(F32)
        total[slot] = acc.astype(BF)
    loop(1, 16, lambda j: grad_copy(j, chip).start())
    last = pltpu.make_async_copy(total.at[k], grad_out.at[chip, core], own.at[4])
    last.start()

    def share(out, n):
        return remote(out.at[:, core], out.at[:, core], pair_send.at[n], pair_recv.at[n], pair)

    def shared(out, n):
        return remote(out.at[:, 1 - core], out.at[:, 1 - core], pair_send.at[n], pair_recv.at[n], pair)

    for copy in keep:
        copy.wait()
    loop(1, 16, lambda j: state_copy(0, stat_out, j, (chip + 16 - j) % 16).wait_recv())
    share(stat_out, 0).start()
    loop(1, 16, lambda j: state_copy(1, basis_out, j, (chip + 16 - j) % 16).wait_recv())
    share(basis_out, 1).start()
    last.wait()
    loop(1, 16, lambda j: grad_copy(j, (chip + 16 - j) % 16).wait_recv())
    share(grad_out, 2).start()
    loop(1, 4, lambda j: quad_copy(j, (local + 4 - j) % 4).wait_recv())
    for n, out in enumerate((stat_out, basis_out, grad_out)):
        shared(out, n).wait_recv()
        share(out, n).wait_send()
    loop(1, 8, lambda j: dp_copy(j, me).wait_send())
    loop(1, 16, lambda j: state_copy(0, stat_out, j, chip).wait_send())
    loop(1, 16, lambda j: state_copy(1, basis_out, j, chip).wait_send())
    loop(1, 16, lambda j: grad_copy(j, chip).wait_send())
    loop(1, 4, lambda j: quad_copy(j, local).wait_send())


def gather_inputs(slot_grads, state, moments):
    rows, width = state.shape[-2:]
    full = jax.ShapeDtypeStruct((16, 2, rows, width), BF)
    dma = pltpu.SemaphoreType.DMA
    return pl.pallas_call(
        gather_kernel,
        out_shape=(full, full, full, jax.ShapeDtypeStruct((4, 2, rows, width), BF)),
        in_specs=[ANY] * 3,
        out_specs=(ANY,) * 4,
        scratch_shapes=[
            pltpu.VMEM((8, 2, rows, width), BF),
            pltpu.VMEM((2, rows, width), BF),
            dma((8,)), dma((8,)), dma((2, 16)), dma((2, 16)), dma((4,)), dma((4,)),
            dma((16,)), dma((16,)), dma((3,)), dma((3,)), dma((5,)),
        ],
        compiler_params=pltpu.CompilerParams(
            collective_id=0, has_side_effects=True, vmem_limit_bytes=16 * 2**20
        ),
    )(slot_grads, state, moments)


def tail_kernel(
    owned, q_part, q_rows, term_rows, q_t, grad, moments, update, terms_out, bases_out,
    moved, left, half, box, pieces, parts, total, home,
    left_sem, box_send, box_recv, row_send, row_recv, dp_send, dp_recv, home_send, home_recv,
    pair_send, pair_recv, own,
):
    me = lax.axis_index("dp")
    chip, core = place()
    quad_base = chip - 4 * ((chip // 4) % 2) - chip % 2
    local = 2 * ((chip // 4) % 2) + chip % 2
    side = chip % 2
    width = grad.shape[0]
    rows = q_part.shape[1]
    greet(me, chip, core)

    def member(number):
        return quad_base + 4 * (number // 2) + number % 2

    def payload(which):
        return half if which else q_part

    def box_copy(which, number, source):
        return remote(
            payload(which).at[number], box.at[which, source], box_send.at[which, number],
            box_recv.at[which, source], chip_coords(member(number)),
        )

    def row_copy(which, j, source):
        number = (local + j) % 4
        src, out = ((term_rows, terms_out), (q_rows, bases_out))[which]
        return remote(
            src.at[number], out.at[source], row_send.at[which, number],
            row_recv.at[which, source], chip_coords(member(number)),
        )

    def dp_copy(which, j, source):
        there = (me + j) % 8
        return remote(
            pieces.at[which, there], parts.at[which, source], dp_send.at[which, there],
            dp_recv.at[which, source], {"dp": there},
        )

    def home_copy(which, j, source):
        there = (chip + j) % 16
        return remote(
            total.at[which], home.at[which, source, core], home_send.at[which, there],
            home_recv.at[which, source], chip_coords(there),
        )

    def share(which, part):
        return remote(
            home.at[which, :, part], home.at[which, :, part], pair_send.at[which],
            pair_recv.at[which], {"c": 1 - core},
        )

    left_copy = remote(q_part, left, left_sem.at[0], left_sem.at[1], {"s": 1 - side})

    def send_box(which):
        @pl.when(side == which)
        def _():
            loop(1, 4, lambda j: box_copy(which, (local + j) % 4, local).start())
            mine = pltpu.make_async_copy(payload(which).at[local], box.at[which, local], own.at[which])
            mine.start()
            mine.wait()

    def receive_box(which):
        for source in (which, which + 2):
            @pl.when(local != source)
            def _():
                box_copy(which, local, source).wait_recv()

        def piece(b):
            pieces[which, b] = (
                box[which, which].astype(F32) * owned[2 * b]
                + box[which, which + 2].astype(F32) * owned[2 * b + 1]
            ).astype(BF)

        def send_piece(j):
            piece((me + j) % 8)
            dp_copy(which, j, me).start()

        loop(1, 8, send_piece)
        piece(me)
        mine = pltpu.make_async_copy(pieces.at[which, me], parts.at[which, me], own.at[2 + which])
        mine.start()
        mine.wait()

    def gather_home(which):
        loop(1, 8, lambda j: dp_copy(which, j, (me + 8 - j) % 8).wait_recv())
        acc = parts[which, 0].astype(F32)
        for d in range(1, 8):
            acc = acc + parts[which, d].astype(F32)
        total[which] = acc.astype(BF)
        loop(1, 16, lambda j: home_copy(which, j, chip).start())
        mine = pltpu.make_async_copy(total.at[which], home.at[which, chip, core], own.at[4 + which])
        mine.start()
        mine.wait()

    @pl.when(side == 0)
    def _():
        left_copy.start()

    send_box(0)

    @pl.when(side == 1)
    def _():
        def body(j):
            tile = pl.ds(pl.multiple_of(j * (width // 4), width // 4), width // 4)
            moved[tile, :] = dot(grad[tile, :], q_t[...], 1, 1).astype(BF)

        loop(0, 4, body)

    receive_box(0)

    @pl.when(side == 1)
    def _():
        left_copy.wait_recv()
        for n in range(4):
            rotated = dot(left[n], moved[...], 1, 0)
            first = BETA_FIRST * moments[n, 0].astype(F32) + (1.0 - BETA_FIRST) * rotated
            second = (
                BETA_SECOND * moments[n, 1].astype(F32) + (1.0 - BETA_SECOND) * rotated * rotated
            )
            left[n] = (first / (jnp.sqrt(second) + EPSILON)).astype(BF)
        normed = left[...].reshape(4 * rows, width)
        half[...] = dot(normed, q_t[...], 1, 0).astype(BF).reshape(4, rows, width)

    send_box(1)
    receive_box(1)
    keep = [
        pltpu.make_async_copy(term_rows.at[local], terms_out.at[local], own.at[6]),
        pltpu.make_async_copy(q_rows.at[local], bases_out.at[local], own.at[7]),
    ]
    for copy in keep:
        copy.start()
    for which in range(2):
        loop(1, 4, lambda j: row_copy(which, j, local).start())
    for which in range(2):
        gather_home(which)
    for which in range(2):
        loop(1, 16, lambda j: home_copy(which, j, (chip + 16 - j) % 16).wait_recv())
        share(which, core).start()
    for which in range(2):
        share(which, 1 - core).wait_recv()
    n_tiles = 4
    step = width // n_tiles
    for j in range(n_tiles):
        tile = slice(j * step, (j + 1) * step)
        update[tile, :] = dot(
            home[0, :, :, :, tile].reshape(width, step), home[1].reshape(width, width), 0, 0
        ).astype(BF)

    for copy in keep:
        copy.wait()
    for which in range(2):
        loop(1, 4, lambda j: row_copy(which, j, (local + 4 - j) % 4).wait_recv())
        loop(1, 4, lambda j: row_copy(which, j, local).wait_send())
        loop(1, 8, lambda j: dp_copy(which, j, me).wait_send())
        loop(1, 16, lambda j: home_copy(which, j, chip).wait_send())
        share(which, core).wait_send()

        @pl.when(side == which)
        def _():
            loop(1, 4, lambda j: box_copy(which, (local + j) % 4, local).wait_send())

    @pl.when(side == 0)
    def _():
        left_copy.wait_send()


def rotate_and_gather(owned, q_part, q_rows, term_rows, q_t, grad, moments):
    rows, width = q_part.shape[-2:]
    dma = pltpu.SemaphoreType.DMA
    vmem = pl.BlockSpec(memory_space=pltpu.VMEM)
    return pl.pallas_call(
        tail_kernel,
        out_shape=(
            jax.ShapeDtypeStruct((width, width), BF),
            jax.ShapeDtypeStruct((4, rows, width), F32),
            jax.ShapeDtypeStruct((4, rows, width), BF),
        ),
        in_specs=[pl.BlockSpec(memory_space=pltpu.SMEM), ANY, ANY, ANY, vmem, vmem, vmem],
        out_specs=(vmem, ANY, ANY),
        scratch_shapes=[
            pltpu.VMEM((width, width), BF),
            pltpu.VMEM((4, rows, width), BF),
            pltpu.VMEM((4, rows, width), BF),
            pltpu.VMEM((2, 4, rows, width), BF),
            pltpu.VMEM((2, 8, rows, width), BF),
            pltpu.VMEM((2, 8, rows, width), BF),
            pltpu.VMEM((2, rows, width), BF),
            pltpu.VMEM((2, 16, 2, rows, width), BF),
            dma((2,)), dma((2, 4)), dma((2, 4)), dma((2, 4)), dma((2, 4)), dma((2, 8)), dma((2, 8)),
            dma((2, 16)), dma((2, 16)), dma((2,)), dma((2,)), dma((8,)),
        ],
        compiler_params=pltpu.CompilerParams(
            collective_id=1, has_side_effects=True, vmem_limit_bytes=40 * 2**20
        ),
    )(owned, q_part, q_rows, term_rows, q_t, grad, moments)


def per_device(
    grads, block_slot, left_stats, right_stats, left_basis, right_basis, first_moment, second_moment
):
    capacity, rows, width = left_stats.shape
    group_size = lax.axis_size("dp")
    block_total = block_slot.shape[0]
    slot_total = capacity * group_size
    side = lax.axis_index("s")
    slot_ids = lax.axis_index("dp") * capacity + jnp.arange(capacity, dtype=jnp.int32)
    owns = block_slot[:, None] == slot_ids[None, :]
    held_mask = jnp.any(owns, axis=0)[:, None, None]

    placing = (
        block_slot[:, None] == lax.broadcasted_iota(jnp.int32, (block_total, slot_total), 1)
    ).astype(BF)
    slot_grads = jnp.einsum("bs,brc->src", placing, grads[0], preferred_element_type=F32).astype(BF)
    stats = jnp.stack([left_stats, right_stats], axis=1).astype(BF)
    bases = jnp.stack([left_basis, right_basis], axis=1)
    grad, old_stat, old_basis, moments = gather_inputs(
        slot_grads.reshape(group_size, capacity, rows, width),
        jnp.stack([stats, bases], axis=2),
        jnp.stack([first_moment, second_moment], axis=1).astype(BF),
    )
    grad, old_stat, old_basis = (
        x.reshape(width, width) for x in (grad, old_stat, old_basis)
    )

    yh, xh, core = (lax.axis_index(axis) for axis in ("yh", "xh", "c"))
    where = jnp.stack([side, core, 8 * yh + 2 * xh]).astype(jnp.int32)
    q_t, q_part, q_rows, term_rows = factored(where, grad, old_stat, old_basis, rows)
    update, terms, new_bases = rotate_and_gather(
        owns.astype(F32).reshape(block_total * capacity), q_part, q_rows, term_rows, q_t, grad, moments
    )

    def merged(new, old):
        return jnp.where(held_mask, new, old)

    terms = terms.reshape(2, 2, rows, width)
    new_bases = new_bases.reshape(2, 2, rows, width)
    return (
        update[None],
        merged(BETA_STATS * left_stats + (1.0 - BETA_STATS) * terms[:, 0], left_stats),
        merged(BETA_STATS * right_stats + (1.0 - BETA_STATS) * terms[:, 1], right_stats),
        merged(new_bases[:, 0], left_basis),
        merged(new_bases[:, 1], right_basis),
    )


def solution(mesh):
    groups = mesh.shape["dp"]
    fine = Mesh(mesh.devices.reshape(groups, 2, 2, 2, 2, 2), ("dp",) + MP)
    rows = P("dp", MP, None)
    return jax.shard_map(
        per_device,
        mesh=fine,
        in_specs=(P("dp", None, MP, None), P()) + (rows,) * 6,
        out_specs=(P("dp", None, None),) + (rows,) * 4,
        check_vma=False,
    )
```

```python
import functools

import jax
import jax.numpy as jnp
from jax import lax
from jax.experimental import pallas as pl
from jax.experimental.pallas import tpu as pltpu
from jax.sharding import Mesh
from jax.sharding import PartitionSpec as P

BETA_STATS = 0.95
BETA_FIRST = 0.9
BETA_SECOND = 0.95
EPSILON = 1e-08
F32 = jnp.float32
BF = jnp.bfloat16
T = 128
MP = ("yh", "k", "xh", "s", "c")
MESH = pl.DeviceIdType.MESH
ANY = pl.BlockSpec(memory_space=pl.ANY)


def split(x):
    high = x.astype(BF)
    return high, (x - high.astype(F32)).astype(BF)


def dot(a, b, a_dim, b_dim):
    return lax.dot_general(a, b, (((a_dim,), (b_dim,)), ((), ())), preferred_element_type=F32)


def reciprocal(x):
    r = pl.reciprocal(x, approx=True)
    return r * (2.0 - x * r)


def tree(terms):
    while len(terms) > 1:
        terms = [a + b for a, b in zip(terms[::2], terms[1::2])]
    return terms[0]


def base_factor(block, hook):
    sub = lax.broadcasted_iota(jnp.int32, (8, T), 0)
    lane = lax.broadcasted_iota(jnp.int32, (8, T), 1)
    groups = T // 8

    def spread(x, q):
        return jnp.broadcast_to(x[q : q + 1, :], (8, T))

    def column(x, at):
        return jnp.broadcast_to(x[:, at : at + 1], (8, T))

    eye = lax.broadcasted_iota(jnp.int32, (T, T), 0) == lax.broadcasted_iota(jnp.int32, (T, T), 1)
    diag = jnp.where(eye, block, 0.0)
    across = lax.rsqrt(jnp.sum(diag, axis=0, keepdims=True))
    down = jnp.sum(jnp.where(eye, jnp.broadcast_to(across, (T, T)), 0.0), axis=1, keepdims=True)
    block = block * across * down
    rows = [block[8 * g : 8 * g + 8, :] for g in range(groups)]
    inv = [(lane == sub + 8 * g).astype(F32) for g in range(groups)]
    out = []
    for g in range(groups):
        r, e = rows[g], inv[g]
        f = e
        cols = [column(r, 8 * g + q) for q in range(8)]
        scale = jnp.zeros((8, T), F32)
        coef = jnp.zeros((8, T), F32)
        for q in range(0, 8, 2):
            x, y = cols[q], cols[q + 1]
            a, b, c = spread(x, q), spread(x, q + 1), spread(y, q + 1)
            det = a * c - b * b
            rd = reciprocal(det)
            i11, i22, i12 = c * rd, a * rd, -(b * rd)
            root = lax.rsqrt(a)
            scale = jnp.where(sub == q, root, scale)
            scale = jnp.where(sub == q + 1, a * root * lax.rsqrt(det), scale)
            coef = jnp.where(sub == q + 1, b * root * root, coef)
            m0 = x * i11 + y * i12
            m1 = x * i12 + y * i22
            if q < 6:
                f = f - (
                    jnp.where(sub > q + 1, m0, 0.0) * spread(f, q)
                    + jnp.where(sub > q + 1, m1, 0.0) * spread(f, q + 1)
                )
            m0 = jnp.where(sub == q, 1.0 - i11, jnp.where(sub == q + 1, -i12, m0))
            m1 = jnp.where(sub == q, -i12, jnp.where(sub == q + 1, 1.0 - i22, m1))
            for p in range(q + 2, 8):
                cols[p] = cols[p] - (m0 * spread(cols[p], q) + m1 * spread(cols[p], q + 1))
            if g < groups - 1:
                r = r - (m0 * spread(r, q) + m1 * spread(r, q + 1))
                e = e - (m0 * spread(e, q) + m1 * spread(e, q + 1))
        out.append((f - coef * pltpu.roll(f, 1, 0)) * scale * across)
        hook(g)
        if g < groups - 1:
            rr = [spread(r, q) for q in range(8)]
            ee = [spread(e, q) for q in range(8)]
            for h in range(g + 1, groups):
                m = [column(rows[h], 8 * g + q) for q in range(8)]
                rows[h] = rows[h] - tree([m[q] * rr[q] for q in range(8)])
                inv[h] = inv[h] - tree([m[q] * ee[q] for q in range(8)])
    return jnp.concatenate(out, axis=0)


def loop(low, high, body):
    def step(j, carry):
        body(j)
        return carry

    lax.fori_loop(low, high, step, 0)


def chip_coords(t):
    return {"yh": t // 8, "k": (t // 4) % 2, "xh": (t // 2) % 2, "s": t % 2}


def place():
    yh, k, xh, s, c = (lax.axis_index(a) for a in MP)
    return ((yh * 2 + k) * 2 + xh) * 2 + s, c


def remote(src, dst, send, recv, coords):
    return pltpu.make_async_remote_copy(
        src_ref=src, dst_ref=dst, send_sem=send, recv_sem=recv, device_id=coords, device_id_type=MESH
    )


def greet(me, chip, core):
    barrier = pltpu.get_barrier_semaphore()

    def to_dp(j, carry):
        pl.semaphore_signal(barrier, inc=1, device_id={"dp": (me + j) % 8}, device_id_type=MESH)
        return carry

    def to_chip(j, carry):
        pl.semaphore_signal(
            barrier, inc=1, device_id=chip_coords((chip + j) % 16), device_id_type=MESH
        )
        return carry

    lax.fori_loop(1, 8, to_dp, 0)
    lax.fori_loop(1, 16, to_chip, 0)
    pl.semaphore_signal(barrier, inc=1, device_id={"c": 1 - core}, device_id_type=MESH)
    pl.semaphore_wait(barrier, 7 + 15 + 1)


def step_kernel(
    owned, slot_grads, state, moments, update, terms_out, bases_out,
    parts, total, grad, old_stat, basis, olds, a, q, stat, mul, cat, d_ref, turned,
    q_part, q_rows, term_rows, q_t, left, half, box, pieces, arrived, home_rows, home,
    dp_send, dp_recv, state_send, state_recv, quad_send, quad_recv, grad_send, grad_recv,
    left_sem, box_send, box_recv, row_send, row_recv, piece_send, piece_recv, home_send, home_recv,
    pair_send, pair_recv, own,
):
    me = lax.axis_index("dp")
    chip, core = place()
    k, side = (chip // 4) % 2, chip % 2
    corner = chip - 4 * k - side
    local = 2 * k + side
    rows, width = q_part.shape[1:]
    quarter = width // 4
    greet(me, chip, core)

    def member(number):
        return corner + 4 * (number // 2) + number % 2

    def dp_copy(j, source):
        there = (me + j) % 8
        return remote(
            slot_grads.at[there], parts.at[source], dp_send.at[there], dp_recv.at[source], {"dp": there}
        )

    def state_copy(which, j, source):
        there = (chip + j) % 16
        return remote(
            state.at[(there // 4) % 2, there % 2, which],
            (old_stat, basis)[which].at[source, core],
            state_send.at[which, there],
            state_recv.at[which, source],
            chip_coords(there),
        )

    def quad_copy(j, source):
        number = (local + j) % 4
        return remote(
            moments.at[number // 2], olds.at[source], quad_send.at[number], quad_recv.at[source],
            chip_coords(member(number)),
        )

    def grad_copy(j, source):
        there = (chip + j) % 16
        return remote(
            total.at[(there // 4) % 2], grad.at[source, core], grad_send.at[there],
            grad_recv.at[source], chip_coords(there),
        )

    def share(ref, part, n):
        return remote(
            ref.at[:, part], ref.at[:, part], pair_send.at[n], pair_recv.at[n], {"c": 1 - core}
        )

    loop(1, 8, lambda j: dp_copy(j, me).start())
    mine = pltpu.make_async_copy(slot_grads.at[me], parts.at[me], own.at[0])
    mine.start()
    keep = [
        pltpu.make_async_copy(state.at[k, side, 0], old_stat.at[chip, core], own.at[1]),
        pltpu.make_async_copy(state.at[k, side, 1], basis.at[chip, core], own.at[2]),
        pltpu.make_async_copy(moments.at[k], olds.at[local], own.at[3]),
    ]
    for copy in keep:
        copy.start()
    loop(1, 16, lambda j: state_copy(0, j, chip).start())
    loop(1, 16, lambda j: state_copy(1, j, chip).start())
    mine.wait()
    loop(1, 8, lambda j: dp_copy(j, (me + 8 - j) % 8).wait_recv())
    for slot in range(2):
        acc = parts[0, slot].astype(F32)
        for d in range(1, 8):
            acc = acc + parts[d, slot].astype(F32)
        total[slot] = acc.astype(BF)
    loop(1, 16, lambda j: grad_copy(j, chip).start())
    grad[chip, core] = total[k]
    loop(1, 4, lambda j: quad_copy(j, local).start())
    for copy in keep:
        copy.wait()
    for which, ref in enumerate((old_stat, basis)):
        loop(1, 16, lambda j: state_copy(which, j, (chip + 16 - j) % 16).wait_recv())
        share(ref, core, which).start()
    loop(1, 16, lambda j: grad_copy(j, (chip + 16 - j) % 16).wait_recv())
    share(grad, core, 2).start()
    for n, ref in ((2, grad), (0, old_stat), (1, basis)):
        share(ref, 1 - core, n).wait_recv()

    def tile(j):
        return pl.ds(pl.multiple_of(j * quarter, quarter), quarter)

    def row_tile(ref, j):
        return ref[pl.ds(j * 4, 4)].reshape(quarter, width)

    def column_tile(ref, j):
        return ref[:, :, :, tile(j)].reshape(width, quarter)

    def whole(ref):
        return ref[...].reshape(width, width)

    @pl.when(side == 0)
    def _():
        def body(j):
            a[tile(j), :] = dot(row_tile(grad, j), whole(grad), 1, 1)

        loop(0, 4, body)

    @pl.when(side != 0)
    def _():
        def body(j):
            a[tile(j), :] = dot(column_tile(grad, j), whole(grad), 0, 0)

        loop(0, 4, body)

    def owned_rows(n):
        return pl.ds(pl.multiple_of((2 * member(n) + core) * rows, rows), rows)

    def row_copy(which, j, source):
        number = (local + j) % 4
        src, out = ((term_rows, terms_out), (q_rows, bases_out))[which]
        return remote(
            src.at[number], out.at[source], row_send.at[which, number],
            row_recv.at[which, source], chip_coords(member(number)),
        )

    for n in range(4):
        term_rows[n] = a[owned_rows(n), :]
    loop(1, 4, lambda j: row_copy(0, j, local).start())
    kept_terms = pltpu.make_async_copy(term_rows.at[local], terms_out.at[local], own.at[4])
    kept_terms.start()

    def mix(j):
        stat[tile(j), :] = (
            BETA_STATS * row_tile(old_stat, j).astype(F32) + (1.0 - BETA_STATS) * a[tile(j), :]
        ).astype(BF)

    loop(0, 4, mix)

    def power(j):
        q[tile(j), :] = dot(column_tile(basis, j), stat[...], 0, 0).astype(BF).astype(F32)

    loop(0, 4, power)

    def keep_power(j):
        stat[tile(j), :] = q[tile(j), :].astype(BF)

    loop(0, 4, keep_power)

    def gram(j):
        a[tile(j), :] = dot(stat[tile(j), :], stat[...], 1, 1)

    loop(0, 4, gram)

    mul[...] = jnp.zeros_like(mul)
    cat[...] = jnp.zeros_like(cat)
    d_ref[...] = a[0:T, 0:T]
    lane = lax.broadcasted_iota(jnp.int32, (T, width), 1)

    def trail(g):
        if g % 2 == 0:
            return
        start = g // 2 * T
        there = slice(start, start + T)
        m = mul[:, there]
        a[there, start:width] -= dot(m, cat[:, start:width], 0, 0)
        q[there, :] -= dot(m, cat[:, width : 2 * width], 0, 0)

    def panel(i):
        here = pl.ds(pl.multiple_of(i * T, T), T)
        high, low = split(base_factor(d_ref[...], trail))
        inverse = jnp.concatenate([high, low, high], axis=1)
        for ref, start in ((a, 0), (q, width)):
            high, low = split(ref[here, :])
            u = dot(inverse, jnp.concatenate([high, high, low], axis=0), 1, 0)
            high, low = split(u)
            part = slice(start, start + width)
            cat[0:T, part], cat[T : 2 * T, part], cat[2 * T : 3 * T, part] = high, high, low
            if start == 0:
                high, low = split(jnp.where(lane >= (i + 1) * T, u, 0.0))
                mul[0:T, :], mul[T : 2 * T, :], mul[2 * T : 3 * T, :] = high, low, high
            else:
                q[here, :] = u
        following = pl.ds(pl.multiple_of(jnp.minimum(i + 1, width // T - 1) * T, T), T)
        d_ref[...] = a[following, following] - dot(mul[:, following], cat[:, following], 0, 0)

    loop(0, width // T, panel)

    def payload(which):
        return half if which else q_part

    def box_copy(which, number, source):
        return remote(
            payload(which).at[number], box.at[which, source], box_send.at[which, number],
            box_recv.at[which, source], chip_coords(member(number)),
        )

    def piece_copy(which, j, source):
        there = (me + j) % 8
        return remote(
            pieces.at[which, there], arrived.at[which, source], piece_send.at[which, there],
            piece_recv.at[which, source], {"dp": there},
        )

    def home_copy(which, j, source):
        there = (chip + j) % 16
        return remote(
            home_rows.at[which], home.at[which, source, core], home_send.at[which, there],
            home_recv.at[which, source], chip_coords(there),
        )

    left_copy = remote(q_part, left, left_sem.at[0], left_sem.at[1], {"s": 1 - side})

    def send_box(which):
        @pl.when(side == which)
        def _():
            loop(1, 4, lambda j: box_copy(which, (local + j) % 4, local).start())
            box[which, local] = payload(which)[local]

    def receive_box(which):
        for source in (which, which + 2):
            @pl.when(local != source)
            def _():
                box_copy(which, local, source).wait_recv()

        def piece(b):
            return (
                box[which, which].astype(F32) * owned[2 * b]
                + box[which, which + 2].astype(F32) * owned[2 * b + 1]
            ).astype(BF)

        def send_piece(j):
            there = (me + j) % 8
            pieces[which, there] = piece(there)
            piece_copy(which, j, me).start()

        loop(1, 8, send_piece)
        arrived[which, me] = piece(me)

    def gather_home(which):
        loop(1, 8, lambda j: piece_copy(which, j, (me + 8 - j) % 8).wait_recv())
        acc = arrived[which, 0].astype(F32)
        for d in range(1, 8):
            acc = acc + arrived[which, d].astype(F32)
        home_rows[which] = acc.astype(BF)
        loop(1, 16, lambda j: home_copy(which, j, chip).start())
        home[which, chip, core] = home_rows[which]

    for n in range(4):
        q_part[n] = q[owned_rows(n), :].astype(BF)

    @pl.when(side == 0)
    def _():
        left_copy.start()

    send_box(0)

    @pl.when(side == 1)
    def _():
        def cast(j):
            q_t[tile(j), :] = q[tile(j), :].astype(BF)

        def move(j):
            stat[tile(j), :] = dot(row_tile(grad, j), q_t[...], 1, 1).astype(BF)

        loop(0, 4, cast)
        loop(0, 4, move)

    receive_box(0)

    @pl.when(side == 1)
    def _():
        left_copy.wait_recv()

    loop(1, 4, lambda j: quad_copy(j, (local + 4 - j) % 4).wait_recv())

    @pl.when(side == 1)
    def _():
        def normalize(n):
            rotated = dot(left[n], stat[...], 1, 0)
            first = BETA_FIRST * olds[n, 0].astype(F32) + (1.0 - BETA_FIRST) * rotated
            second = (
                BETA_SECOND * olds[n, 1].astype(F32) + (1.0 - BETA_SECOND) * rotated * rotated
            )
            left[n] = (first / (jnp.sqrt(second) + EPSILON)).astype(BF)

        loop(0, 4, normalize)
        normed = left[...].reshape(4 * rows, width)
        half[...] = dot(normed, q_t[...], 1, 0).astype(BF).reshape(4, rows, width)

    send_box(1)
    receive_box(1)
    for slot in range(2):
        columns = pl.ds(pl.multiple_of((corner + 4 * slot) // 2 * T, T), T)
        turned[...] = q[:, columns].T
        for side_to in range(2):
            these = pl.ds(pl.multiple_of((2 * side_to + core) * rows, rows), rows)
            q_rows[2 * slot + side_to] = turned[these, :].astype(BF)
    gather_home(0)
    loop(1, 4, lambda j: row_copy(1, j, local).start())
    kept_bases = pltpu.make_async_copy(q_rows.at[local], bases_out.at[local], own.at[5])
    kept_bases.start()
    gather_home(1)
    for which in range(2):
        loop(1, 16, lambda j: home_copy(which, j, (chip + 16 - j) % 16).wait_recv())
        share(home.at[which], core, 3 + which).start()
    for which in range(2):
        share(home.at[which], 1 - core, 3 + which).wait_recv()

    def multiply(j):
        update[tile(j), :] = dot(
            home[0, :, :, :, tile(j)].reshape(width, quarter), home[1].reshape(width, width), 0, 0
        ).astype(BF)

    loop(0, 4, multiply)

    kept_terms.wait()
    kept_bases.wait()
    for which in range(2):
        loop(1, 4, lambda j: row_copy(which, j, (local + 4 - j) % 4).wait_recv())
        loop(1, 4, lambda j: row_copy(which, j, local).wait_send())
        loop(1, 8, lambda j: piece_copy(which, j, me).wait_send())
        loop(1, 16, lambda j: home_copy(which, j, chip).wait_send())
        loop(1, 16, lambda j: state_copy(which, j, chip).wait_send())
        share(home.at[which], core, 3 + which).wait_send()

        @pl.when(side == which)
        def _():
            loop(1, 4, lambda j: box_copy(which, (local + j) % 4, local).wait_send())

    for n, ref in enumerate((old_stat, basis, grad)):
        share(ref, core, n).wait_send()
    loop(1, 8, lambda j: dp_copy(j, me).wait_send())
    loop(1, 16, lambda j: grad_copy(j, chip).wait_send())
    loop(1, 4, lambda j: quad_copy(j, local).wait_send())

    @pl.when(side == 0)
    def _():
        left_copy.wait_send()


def optimizer_step(owned, slot_grads, state, moments):
    rows, width = state.shape[-2:]
    dma = pltpu.SemaphoreType.DMA
    vmem = pltpu.VMEM
    full = vmem((16, 2, rows, width), BF)
    return pl.pallas_call(
        step_kernel,
        out_shape=(
            jax.ShapeDtypeStruct((width, width), BF),
            jax.ShapeDtypeStruct((4, rows, width), F32),
            jax.ShapeDtypeStruct((4, rows, width), BF),
        ),
        in_specs=[pl.BlockSpec(memory_space=pltpu.SMEM), ANY, ANY, ANY],
        out_specs=(pl.BlockSpec(memory_space=vmem), ANY, ANY),
        scratch_shapes=[
            vmem((8, 2, rows, width), BF),
            vmem((2, rows, width), BF),
            full, full, full,
            vmem((4, 2, rows, width), BF),
            vmem((width, width), F32), vmem((width, width), F32), vmem((width, width), BF),
            vmem((3 * T, width), BF), vmem((3 * T, 2 * width), BF),
            vmem((T, T), F32), vmem((T, width), F32),
            vmem((4, rows, width), BF), vmem((4, rows, width), BF), vmem((4, rows, width), F32),
            vmem((width, width), BF),
            vmem((4, rows, width), BF), vmem((4, rows, width), BF),
            vmem((2, 4, rows, width), BF),
            vmem((2, 8, rows, width), BF), vmem((2, 8, rows, width), BF),
            vmem((2, rows, width), BF), vmem((2, 16, 2, rows, width), BF),
            dma((8,)), dma((8,)), dma((2, 16)), dma((2, 16)), dma((4,)), dma((4,)), dma((16,)), dma((16,)),
            dma((2,)), dma((2, 4)), dma((2, 4)), dma((2, 4)), dma((2, 4)), dma((2, 8)), dma((2, 8)),
            dma((2, 16)), dma((2, 16)), dma((5,)), dma((5,)), dma((6,)),
        ],
        compiler_params=pltpu.CompilerParams(
            collective_id=0, has_side_effects=True, vmem_limit_bytes=56 * 2**20
        ),
    )(owned, slot_grads, state, moments)


def per_device(
    grads, block_slot, left_stats, right_stats, left_basis, right_basis, first_moment, second_moment
):
    capacity, rows, width = left_stats.shape
    group_size = lax.axis_size("dp")
    block_total = block_slot.shape[0]
    slot_total = capacity * group_size
    slot_ids = lax.axis_index("dp") * capacity + jnp.arange(capacity, dtype=jnp.int32)
    owns = block_slot[:, None] == slot_ids[None, :]
    held_mask = jnp.any(owns, axis=0)[:, None, None]

    placing = (
        block_slot[:, None] == lax.broadcasted_iota(jnp.int32, (block_total, slot_total), 1)
    ).astype(BF)
    slot_grads = jnp.einsum("bs,brc->src", placing, grads[0], preferred_element_type=F32).astype(BF)
    stats = jnp.stack([left_stats, right_stats], axis=1).astype(BF)
    bases = jnp.stack([left_basis, right_basis], axis=1)
    update, terms, new_bases = optimizer_step(
        owns.astype(F32).reshape(block_total * capacity),
        slot_grads.reshape(group_size, capacity, rows, width),
        jnp.stack([stats, bases], axis=2),
        jnp.stack([first_moment, second_moment], axis=1).astype(BF),
    )

    def merged(new, old):
        return jnp.where(held_mask, new, old)

    terms = terms.reshape(2, 2, rows, width)
    new_bases = new_bases.reshape(2, 2, rows, width)
    return (
        update[None],
        merged(BETA_STATS * left_stats + (1.0 - BETA_STATS) * terms[:, 0], left_stats),
        merged(BETA_STATS * right_stats + (1.0 - BETA_STATS) * terms[:, 1], right_stats),
        merged(new_bases[:, 0], left_basis),
        merged(new_bases[:, 1], right_basis),
    )


def solution(mesh):
    groups = mesh.shape["dp"]
    fine = Mesh(mesh.devices.reshape(groups, 2, 2, 2, 2, 2), ("dp",) + MP)
    rows = P("dp", MP, None)
    return jax.shard_map(
        per_device,
        mesh=fine,
        in_specs=(P("dp", None, MP, None), P()) + (rows,) * 6,
        out_specs=(P("dp", None, None),) + (rows,) * 4,
        check_vma=False,
    )
```

```python
import functools

import jax
import jax.numpy as jnp
from jax import lax
from jax.experimental import pallas as pl
from jax.experimental.pallas import tpu as pltpu
from jax.sharding import Mesh
from jax.sharding import PartitionSpec as P

BETA_STATS = 0.95
BETA_FIRST = 0.9
BETA_SECOND = 0.95
EPSILON = 1e-08
F32 = jnp.float32
BF = jnp.bfloat16
T = 128
MP = ("yh", "k", "xh", "s", "c")
MESH = pl.DeviceIdType.MESH
ANY = pl.BlockSpec(memory_space=pl.ANY)


def split(x):
    high = x.astype(BF)
    return high, (x - high.astype(F32)).astype(BF)


def dot(a, b, a_dim, b_dim):
    return lax.dot_general(a, b, (((a_dim,), (b_dim,)), ((), ())), preferred_element_type=F32)


def reciprocal(x):
    r = pl.reciprocal(x, approx=True)
    return r * (2.0 - x * r)


def tree(terms):
    while len(terms) > 1:
        terms = [a + b for a, b in zip(terms[::2], terms[1::2])]
    return terms[0]


def base_factor(block, hook):
    sub = lax.broadcasted_iota(jnp.int32, (8, T), 0)
    lane = lax.broadcasted_iota(jnp.int32, (8, T), 1)
    groups = T // 8

    def spread(x, q):
        return jnp.broadcast_to(x[q : q + 1, :], (8, T))

    def column(x, at):
        return jnp.broadcast_to(x[:, at : at + 1], (8, T))

    eye = lax.broadcasted_iota(jnp.int32, (T, T), 0) == lax.broadcasted_iota(jnp.int32, (T, T), 1)
    diag = jnp.where(eye, block, 0.0)
    across = lax.rsqrt(jnp.sum(diag, axis=0, keepdims=True))
    down = jnp.sum(jnp.where(eye, jnp.broadcast_to(across, (T, T)), 0.0), axis=1, keepdims=True)
    block = block * across * down
    rows = [block[8 * g : 8 * g + 8, :] for g in range(groups)]
    inv = [(lane == sub + 8 * g).astype(F32) for g in range(groups)]
    out = []
    for g in range(groups):
        r, e = rows[g], inv[g]
        f = e
        cols = [column(r, 8 * g + q) for q in range(8)]
        scale = jnp.zeros((8, T), F32)
        coef = jnp.zeros((8, T), F32)
        for q in range(0, 8, 2):
            x, y = cols[q], cols[q + 1]
            a, b, c = spread(x, q), spread(x, q + 1), spread(y, q + 1)
            det = a * c - b * b
            rd = reciprocal(det)
            i11, i22, i12 = c * rd, a * rd, -(b * rd)
            root = lax.rsqrt(a)
            scale = jnp.where(sub == q, root, scale)
            scale = jnp.where(sub == q + 1, a * root * lax.rsqrt(det), scale)
            coef = jnp.where(sub == q + 1, b * root * root, coef)
            m0 = x * i11 + y * i12
            m1 = x * i12 + y * i22
            if q < 6:
                f = f - (
                    jnp.where(sub > q + 1, m0, 0.0) * spread(f, q)
                    + jnp.where(sub > q + 1, m1, 0.0) * spread(f, q + 1)
                )
            m0 = jnp.where(sub == q, 1.0 - i11, jnp.where(sub == q + 1, -i12, m0))
            m1 = jnp.where(sub == q, -i12, jnp.where(sub == q + 1, 1.0 - i22, m1))
            for p in range(q + 2, 8):
                cols[p] = cols[p] - (m0 * spread(cols[p], q) + m1 * spread(cols[p], q + 1))
            if g < groups - 1:
                r = r - (m0 * spread(r, q) + m1 * spread(r, q + 1))
                e = e - (m0 * spread(e, q) + m1 * spread(e, q + 1))
        out.append((f - coef * pltpu.roll(f, 1, 0)) * scale * across)
        if g < groups - 1:
            rr = [spread(r, q) for q in range(8)]
            ee = [spread(e, q) for q in range(8)]
            m = [column(rows[g + 1], 8 * g + q) for q in range(8)]
            if g < groups - 2:
                x = jnp.concatenate(rows[g + 2 :], axis=0)
                xh, xl = split(x)
                both = jnp.concatenate([r, e], axis=1)
                rh = both.astype(BF).astype(F32)
                above = [jnp.zeros((8 * g, 2 * T), F32)] * (g > 0)
                under = [jnp.zeros((T - 8 * g - 8, 2 * T), F32)]
                yh = jnp.concatenate(above + [rh] + under, axis=0).astype(BF)
                yl = jnp.concatenate(above + [both - rh] + under, axis=0).astype(BF)
                z = dot(xh, yh, 1, 0) + (dot(xl, yh, 1, 0) + dot(xh, yl, 1, 0))
                for h in range(g + 2, groups):
                    at = 8 * (h - g - 2)
                    rows[h] = rows[h] - z[at : at + 8, :T]
                    inv[h] = inv[h] - z[at : at + 8, T:]
            rows[g + 1] = rows[g + 1] - tree([m[q] * rr[q] for q in range(8)])
            inv[g + 1] = inv[g + 1] - tree([m[q] * ee[q] for q in range(8)])
        hook(g)
    return jnp.concatenate(out, axis=0)


def loop(low, high, body):
    def step(j, carry):
        body(j)
        return carry

    lax.fori_loop(low, high, step, 0)


def chip_coords(t):
    return {"yh": t // 8, "k": (t // 4) % 2, "xh": (t // 2) % 2, "s": t % 2}


def place():
    yh, k, xh, s, c = (lax.axis_index(a) for a in MP)
    return ((yh * 2 + k) * 2 + xh) * 2 + s, c


def remote(src, dst, send, recv, coords):
    return pltpu.make_async_remote_copy(
        src_ref=src, dst_ref=dst, send_sem=send, recv_sem=recv, device_id=coords, device_id_type=MESH
    )


def greet(me, chip, core):
    barrier = pltpu.get_barrier_semaphore()

    def to_dp(j, carry):
        pl.semaphore_signal(barrier, inc=1, device_id={"dp": (me + j) % 8}, device_id_type=MESH)
        return carry

    def to_chip(j, carry):
        pl.semaphore_signal(
            barrier, inc=1, device_id=chip_coords((chip + j) % 16), device_id_type=MESH
        )
        return carry

    lax.fori_loop(1, 8, to_dp, 0)
    lax.fori_loop(1, 16, to_chip, 0)
    pl.semaphore_signal(barrier, inc=1, device_id={"c": 1 - core}, device_id_type=MESH)
    return lambda: pl.semaphore_wait(barrier, 7 + 15 + 1)


def step_kernel(
    named, owned, grads, left_stats, right_stats, first, second, left_basis, right_basis,
    update, terms_out, bases_out, slot_grads, stats, moments,
    parts, total, grad, old_stat, basis, olds, a, q, stat, mul, cat, d_ref, turned,
    q_part, q_rows, term_rows, q_t, left, half, box, pieces, arrived, home_rows, home,
    dp_send, dp_recv, state_send, state_recv, quad_send, quad_recv, grad_send, grad_recv,
    left_sem, box_send, box_recv, row_send, row_recv, piece_send, piece_recv, home_send, home_recv,
    pair_send, pair_recv, own,
):
    me = lax.axis_index("dp")
    chip, core = place()
    k, side = (chip // 4) % 2, chip % 2
    corner = chip - 4 * k - side
    local = 2 * k + side
    rows, width = q_part.shape[1:]
    quarter = width // 4
    slot_total = 16
    all_here = greet(me, chip, core)
    for slot in range(2):
        stats[slot, 0] = left_stats[slot].astype(BF)
        stats[slot, 1] = right_stats[slot].astype(BF)
        moments[slot, 0] = first[slot].astype(BF)
        moments[slot, 1] = second[slot].astype(BF)

    def place_grads(d):
        for slot in range(2):
            present = named[slot_total + 2 * d + slot].astype(F32)
            rows_of = grads[named[2 * d + slot]].astype(F32)
            slot_grads[d, slot] = (rows_of * present).astype(BF)

    loop(0, 8, place_grads)
    all_here()

    def member(number):
        return corner + 4 * (number // 2) + number % 2

    def dp_copy(j, source):
        there = (me + j) % 8
        return remote(
            slot_grads.at[there], parts.at[source], dp_send.at[there], dp_recv.at[source], {"dp": there}
        )

    def state_copy(which, j, source):
        there = (chip + j) % 16
        return remote(
            stats.at[(there // 4) % 2, there % 2],
            (old_stat, basis)[which].at[source, core],
            state_send.at[which, there],
            state_recv.at[which, source],
            chip_coords(there),
        )

    def basis_copy(to_side, j):
        there = 2 * ((chip // 2 + j) % 8) + to_side
        return remote(
            (left_basis, right_basis)[to_side].at[(there // 4) % 2],
            basis.at[chip, core],
            state_send.at[1, there],
            state_recv.at[1, chip],
            chip_coords(there),
        )

    def quad_copy(j, source):
        number = (local + j) % 4
        return remote(
            moments.at[number // 2], olds.at[source], quad_send.at[number], quad_recv.at[source],
            chip_coords(member(number)),
        )

    def grad_copy(j, source):
        there = (chip + j) % 16
        return remote(
            total.at[(there // 4) % 2], grad.at[source, core], grad_send.at[there],
            grad_recv.at[source], chip_coords(there),
        )

    def share(ref, part, n):
        return remote(
            ref.at[:, part], ref.at[:, part], pair_send.at[n], pair_recv.at[n], {"c": 1 - core}
        )

    loop(1, 8, lambda j: dp_copy(j, me).start())
    parts[me] = slot_grads[me]
    loop(1, 16, lambda j: state_copy(0, j, chip).start())
    for to_side, ref in enumerate((left_basis, right_basis)):
        loop(jnp.where(side == to_side, 1, 0), 8, lambda j: basis_copy(to_side, j).start())

        @pl.when(side == to_side)
        def _():
            pltpu.make_async_copy(ref.at[k], basis.at[chip, core], own.at[2]).start()

    old_stat[chip, core] = stats[k, side]
    olds[local] = moments[k]
    loop(1, 8, lambda j: dp_copy(j, (me + 8 - j) % 8).wait_recv())
    for slot in range(2):
        acc = parts[0, slot].astype(F32)
        for d in range(1, 8):
            acc = acc + parts[d, slot].astype(F32)
        total[slot] = acc.astype(BF)
    loop(1, 16, lambda j: grad_copy(j, chip).start())
    grad[chip, core] = total[k]
    loop(1, 4, lambda j: quad_copy(j, local).start())
    pltpu.make_async_copy(left_basis.at[k], basis.at[chip, core], own.at[2]).wait()
    for which, ref in enumerate((old_stat, basis)):
        loop(1, 16, lambda j: state_copy(which, j, (chip + 16 - j) % 16).wait_recv())
        share(ref, core, which).start()
    loop(1, 16, lambda j: grad_copy(j, (chip + 16 - j) % 16).wait_recv())
    share(grad, core, 2).start()
    for n, ref in ((2, grad), (0, old_stat), (1, basis)):
        share(ref, 1 - core, n).wait_recv()

    def tile(j):
        return pl.ds(pl.multiple_of(j * quarter, quarter), quarter)

    def row_tile(ref, j):
        return ref[pl.ds(j * 4, 4)].reshape(quarter, width)

    def column_tile(ref, j):
        return ref[:, :, :, tile(j)].reshape(width, quarter)

    def whole(ref):
        return ref[...].reshape(width, width)

    @pl.when(side == 0)
    def _():
        def body(j):
            a[tile(j), :] = dot(row_tile(grad, j), whole(grad), 1, 1)

        loop(0, 4, body)

    @pl.when(side != 0)
    def _():
        def body(j):
            a[tile(j), :] = dot(column_tile(grad, j), whole(grad), 0, 0)

        loop(0, 4, body)

    def owned_rows(n):
        return pl.ds(pl.multiple_of((2 * member(n) + core) * rows, rows), rows)

    def row_copy(which, j, source):
        number = (local + j) % 4
        src, out = ((term_rows, terms_out), (q_rows, bases_out))[which]
        return remote(
            src.at[number], out.at[source], row_send.at[which, number],
            row_recv.at[which, source], chip_coords(member(number)),
        )

    for n in range(4):
        term_rows[n] = a[owned_rows(n), :]
    loop(1, 4, lambda j: row_copy(0, j, local).start())
    kept_terms = pltpu.make_async_copy(term_rows.at[local], terms_out.at[local], own.at[4])
    kept_terms.start()

    def mix(j):
        stat[tile(j), :] = (
            BETA_STATS * row_tile(old_stat, j).astype(F32) + (1.0 - BETA_STATS) * a[tile(j), :]
        ).astype(BF)

    loop(0, 4, mix)

    def power(j):
        q[tile(j), :] = dot(column_tile(basis, j), stat[...], 0, 0).astype(BF).astype(F32)

    loop(0, 4, power)

    def keep_power(j):
        stat[tile(j), :] = q[tile(j), :].astype(BF)

    loop(0, 4, keep_power)

    def gram(j):
        a[tile(j), :] = dot(stat[tile(j), :], stat[...], 1, 1)

    loop(0, 4, gram)

    mul[...] = jnp.zeros_like(mul)
    cat[...] = jnp.zeros_like(cat)
    d_ref[...] = a[0:T, 0:T]
    lane = lax.broadcasted_iota(jnp.int32, (T, width), 1)

    def trail(g):
        if g % 2 == 0:
            return
        start = g // 2 * T
        there = slice(start, start + T)
        m = mul[:, there]
        a[there, start:width] -= dot(m, cat[:, start:width], 0, 0)
        q[there, :] -= dot(m, cat[:, width : 2 * width], 0, 0)

    def panel(i):
        here = pl.ds(pl.multiple_of(i * T, T), T)
        high, low = split(base_factor(d_ref[...], trail))
        inverse = jnp.concatenate([high, low, high], axis=1)
        for ref, start in ((a, 0), (q, width)):
            high, low = split(ref[here, :])
            u = dot(inverse, jnp.concatenate([high, high, low], axis=0), 1, 0)
            high, low = split(u)
            part = slice(start, start + width)
            cat[0:T, part], cat[T : 2 * T, part], cat[2 * T : 3 * T, part] = high, high, low
            if start == 0:
                high, low = split(jnp.where(lane >= (i + 1) * T, u, 0.0))
                mul[0:T, :], mul[T : 2 * T, :], mul[2 * T : 3 * T, :] = high, low, high
            else:
                q[here, :] = u
        following = pl.ds(pl.multiple_of(jnp.minimum(i + 1, width // T - 1) * T, T), T)
        d_ref[...] = a[following, following] - dot(mul[:, following], cat[:, following], 0, 0)

    loop(0, width // T, panel)

    def payload(which):
        return half if which else q_part

    def box_copy(which, number, source):
        return remote(
            payload(which).at[number], box.at[which, source], box_send.at[which, number],
            box_recv.at[which, source], chip_coords(member(number)),
        )

    def piece_copy(which, j, source):
        there = (me + j) % 8
        return remote(
            pieces.at[which, there], arrived.at[which, source], piece_send.at[which, there],
            piece_recv.at[which, source], {"dp": there},
        )

    def home_copy(which, j, source):
        there = (chip + j) % 16
        return remote(
            home_rows.at[which], home.at[which, source, core], home_send.at[which, there],
            home_recv.at[which, source], chip_coords(there),
        )

    left_copy = remote(q_part, left, left_sem.at[0], left_sem.at[1], {"s": 1 - side})

    def send_box(which):
        @pl.when(side == which)
        def _():
            loop(1, 4, lambda j: box_copy(which, (local + j) % 4, local).start())
            box[which, local] = payload(which)[local]

    def receive_box(which):
        for source in (which, which + 2):
            @pl.when(local != source)
            def _():
                box_copy(which, local, source).wait_recv()

        def piece(b):
            return (
                box[which, which].astype(F32) * owned[2 * b]
                + box[which, which + 2].astype(F32) * owned[2 * b + 1]
            ).astype(BF)

        def send_piece(j):
            there = (me + j) % 8
            pieces[which, there] = piece(there)
            piece_copy(which, j, me).start()

        loop(1, 8, send_piece)
        arrived[which, me] = piece(me)

    def gather_home(which):
        loop(1, 8, lambda j: piece_copy(which, j, (me + 8 - j) % 8).wait_recv())
        acc = arrived[which, 0].astype(F32)
        for d in range(1, 8):
            acc = acc + arrived[which, d].astype(F32)
        home_rows[which] = acc.astype(BF)
        loop(1, 16, lambda j: home_copy(which, j, chip).start())
        home[which, chip, core] = home_rows[which]

    for n in range(4):
        q_part[n] = q[owned_rows(n), :].astype(BF)

    @pl.when(side == 0)
    def _():
        left_copy.start()

    send_box(0)

    @pl.when(side == 1)
    def _():
        def cast(j):
            q_t[tile(j), :] = q[tile(j), :].astype(BF)

        def move(j):
            stat[tile(j), :] = dot(row_tile(grad, j), q_t[...], 1, 1).astype(BF)

        loop(0, 4, cast)
        loop(0, 4, move)

    receive_box(0)

    @pl.when(side == 1)
    def _():
        left_copy.wait_recv()

    loop(1, 4, lambda j: quad_copy(j, (local + 4 - j) % 4).wait_recv())

    @pl.when(side == 1)
    def _():
        def normalize(n):
            rotated = dot(left[n], stat[...], 1, 0)
            first = BETA_FIRST * olds[n, 0].astype(F32) + (1.0 - BETA_FIRST) * rotated
            second = (
                BETA_SECOND * olds[n, 1].astype(F32) + (1.0 - BETA_SECOND) * rotated * rotated
            )
            left[n] = (first / (jnp.sqrt(second) + EPSILON)).astype(BF)

        loop(0, 4, normalize)
        normed = left[...].reshape(4 * rows, width)
        half[...] = dot(normed, q_t[...], 1, 0).astype(BF).reshape(4, rows, width)

    send_box(1)
    receive_box(1)
    for slot in range(2):
        columns = pl.ds(pl.multiple_of((corner + 4 * slot) // 2 * T, T), T)
        turned[...] = q[:, columns].T
        for side_to in range(2):
            these = pl.ds(pl.multiple_of((2 * side_to + core) * rows, rows), rows)
            q_rows[2 * slot + side_to] = turned[these, :].astype(BF)
    gather_home(0)
    loop(1, 4, lambda j: row_copy(1, j, local).start())
    kept_bases = pltpu.make_async_copy(q_rows.at[local], bases_out.at[local], own.at[5])
    kept_bases.start()
    gather_home(1)
    for which in range(2):
        loop(1, 16, lambda j: home_copy(which, j, (chip + 16 - j) % 16).wait_recv())
        share(home.at[which], core, 3 + which).start()
    for which in range(2):
        share(home.at[which], 1 - core, 3 + which).wait_recv()

    def multiply(j):
        update[tile(j), :] = dot(
            home[0, :, :, :, tile(j)].reshape(width, quarter), home[1].reshape(width, width), 0, 0
        ).astype(BF)

    loop(0, 4, multiply)

    kept_terms.wait()
    kept_bases.wait()
    for which in range(2):
        loop(1, 4, lambda j: row_copy(which, j, (local + 4 - j) % 4).wait_recv())
        loop(1, 4, lambda j: row_copy(which, j, local).wait_send())
        loop(1, 8, lambda j: piece_copy(which, j, me).wait_send())
        loop(1, 16, lambda j: home_copy(which, j, chip).wait_send())
        loop(1, 16, lambda j: state_copy(which, j, chip).wait_send())
        share(home.at[which], core, 3 + which).wait_send()

        @pl.when(side == which)
        def _():
            loop(1, 4, lambda j: box_copy(which, (local + j) % 4, local).wait_send())

    for n, ref in enumerate((old_stat, basis, grad)):
        share(ref, core, n).wait_send()
    loop(1, 8, lambda j: dp_copy(j, me).wait_send())
    loop(1, 16, lambda j: grad_copy(j, chip).wait_send())
    loop(1, 4, lambda j: quad_copy(j, local).wait_send())

    @pl.when(side == 0)
    def _():
        left_copy.wait_send()


def optimizer_step(named, owned, grads, left_stats, right_stats, first, second, left_basis, right_basis):
    rows, width = grads.shape[-2:]
    dma = pltpu.SemaphoreType.DMA
    vmem = pltpu.VMEM
    full = vmem((16, 2, rows, width), BF)
    return pl.pallas_call(
        step_kernel,
        out_shape=(
            jax.ShapeDtypeStruct((width, width), BF),
            jax.ShapeDtypeStruct((4, rows, width), F32),
            jax.ShapeDtypeStruct((4, rows, width), BF),
        ),
        in_specs=[pl.BlockSpec(memory_space=pltpu.SMEM)] * 2 + [pl.BlockSpec(memory_space=vmem)] * 5 + [ANY] * 2,
        out_specs=(pl.BlockSpec(memory_space=vmem), ANY, ANY),
        scratch_shapes=[
            vmem((8, 2, rows, width), BF),
            vmem((2, 2, rows, width), BF), vmem((2, 2, rows, width), BF),
            vmem((8, 2, rows, width), BF),
            vmem((2, rows, width), BF),
            full, full, full,
            vmem((4, 2, rows, width), BF),
            vmem((width, width), F32), vmem((width, width), F32), vmem((width, width), BF),
            vmem((3 * T, width), BF), vmem((3 * T, 2 * width), BF),
            vmem((T, T), F32), vmem((T, width), F32),
            vmem((4, rows, width), BF), vmem((4, rows, width), BF), vmem((4, rows, width), F32),
            vmem((width, width), BF),
            vmem((4, rows, width), BF), vmem((4, rows, width), BF),
            vmem((2, 4, rows, width), BF),
            vmem((2, 8, rows, width), BF), vmem((2, 8, rows, width), BF),
            vmem((2, rows, width), BF), vmem((2, 16, 2, rows, width), BF),
            dma((8,)), dma((8,)), dma((2, 16)), dma((2, 16)), dma((4,)), dma((4,)), dma((16,)), dma((16,)),
            dma((2,)), dma((2, 4)), dma((2, 4)), dma((2, 4)), dma((2, 4)), dma((2, 8)), dma((2, 8)),
            dma((2, 16)), dma((2, 16)), dma((5,)), dma((5,)), dma((6,)),
        ],
        compiler_params=pltpu.CompilerParams(
            collective_id=0, has_side_effects=True, vmem_limit_bytes=56 * 2**20
        ),
    )(named, owned, grads, left_stats, right_stats, first, second, left_basis, right_basis)


def per_device(
    grads, block_slot, left_stats, right_stats, left_basis, right_basis, first_moment, second_moment
):
    capacity, rows, width = left_stats.shape
    block_total = block_slot.shape[0]
    slot_total = capacity * lax.axis_size("dp")
    slot_ids = lax.axis_index("dp") * capacity + jnp.arange(capacity, dtype=jnp.int32)
    owns = block_slot[:, None] == slot_ids[None, :]
    held_mask = jnp.any(owns, axis=0)[:, None, None]

    naming = block_slot[None, :] == jnp.arange(slot_total, dtype=jnp.int32)[:, None]
    numbers = jnp.arange(block_total, dtype=jnp.int32)[None, :]
    named = jnp.concatenate(
        [jnp.sum(jnp.where(naming, numbers, 0), axis=1), jnp.any(naming, axis=1).astype(jnp.int32)]
    )
    update, terms, new_bases = optimizer_step(
        named,
        owns.astype(F32).reshape(block_total * capacity),
        grads[0],
        left_stats,
        right_stats,
        first_moment,
        second_moment,
        left_basis,
        right_basis,
    )

    def merged(new, old):
        return jnp.where(held_mask, new, old)

    terms = terms.reshape(2, 2, rows, width)
    new_bases = new_bases.reshape(2, 2, rows, width)
    return (
        update[None],
        merged(BETA_STATS * left_stats + (1.0 - BETA_STATS) * terms[:, 0], left_stats),
        merged(BETA_STATS * right_stats + (1.0 - BETA_STATS) * terms[:, 1], right_stats),
        merged(new_bases[:, 0], left_basis),
        merged(new_bases[:, 1], right_basis),
    )


def solution(mesh):
    groups = mesh.shape["dp"]
    fine = Mesh(mesh.devices.reshape(groups, 2, 2, 2, 2, 2), ("dp",) + MP)
    rows = P("dp", MP, None)
    return jax.shard_map(
        per_device,
        mesh=fine,
        in_specs=(P("dp", None, MP, None), P()) + (rows,) * 6,
        out_specs=(P("dp", None, None),) + (rows,) * 4,
        check_vma=False,
    )
```

```python
import functools

import jax
import jax.numpy as jnp
from jax import lax
from jax.experimental import pallas as pl
from jax.experimental.pallas import tpu as pltpu
from jax.sharding import Mesh
from jax.sharding import PartitionSpec as P

BETA_STATS = 0.95
BETA_FIRST = 0.9
BETA_SECOND = 0.95
EPSILON = 1e-08
F32 = jnp.float32
BF = jnp.bfloat16
T = 128
MP = ("yh", "k", "xh", "s", "c")
MESH = pl.DeviceIdType.MESH
ANY = pl.BlockSpec(memory_space=pl.ANY)


def split(x):
    high = x.astype(BF)
    return high, (x - high.astype(F32)).astype(BF)


def dot(a, b, a_dim, b_dim):
    return lax.dot_general(a, b, (((a_dim,), (b_dim,)), ((), ())), preferred_element_type=F32)


def reciprocal(x):
    r = pl.reciprocal(x, approx=True)
    return r * (2.0 - x * r)


def tree(terms):
    while len(terms) > 1:
        terms = [a + b for a, b in zip(terms[::2], terms[1::2])]
    return terms[0]


def base_factor(block, hook):
    sub = lax.broadcasted_iota(jnp.int32, (8, T), 0)
    lane = lax.broadcasted_iota(jnp.int32, (8, T), 1)
    groups = T // 8

    def spread(x, q):
        return jnp.broadcast_to(x[q : q + 1, :], (8, T))

    def column(x, at):
        return jnp.broadcast_to(x[:, at : at + 1], (8, T))

    eye = lax.broadcasted_iota(jnp.int32, (T, T), 0) == lax.broadcasted_iota(jnp.int32, (T, T), 1)
    diag = jnp.where(eye, block, 0.0)
    across = lax.rsqrt(jnp.sum(diag, axis=0, keepdims=True))
    down = jnp.sum(jnp.where(eye, jnp.broadcast_to(across, (T, T)), 0.0), axis=1, keepdims=True)
    block = block * across * down
    rows = [block[8 * g : 8 * g + 8, :] for g in range(groups)]
    inv = [(lane == sub + 8 * g).astype(F32) for g in range(groups)]
    out = []
    for g in range(groups):
        r, e = rows[g], inv[g]
        f = e
        cols = [column(r, 8 * g + q) for q in range(8)]
        scale = jnp.zeros((8, T), F32)
        coef = jnp.zeros((8, T), F32)
        for q in range(0, 8, 2):
            x, y = cols[q], cols[q + 1]
            a, b, c = spread(x, q), spread(x, q + 1), spread(y, q + 1)
            det = a * c - b * b
            rd = reciprocal(det)
            i11, i22, i12 = c * rd, a * rd, -(b * rd)
            root = lax.rsqrt(a)
            scale = jnp.where(sub == q, root, scale)
            scale = jnp.where(sub == q + 1, a * root * lax.rsqrt(det), scale)
            coef = jnp.where(sub == q + 1, b * root * root, coef)
            m0 = x * i11 + y * i12
            m1 = x * i12 + y * i22
            if q < 6:
                f = f - (
                    jnp.where(sub > q + 1, m0, 0.0) * spread(f, q)
                    + jnp.where(sub > q + 1, m1, 0.0) * spread(f, q + 1)
                )
            m0 = jnp.where(sub == q, 1.0 - i11, jnp.where(sub == q + 1, -i12, m0))
            m1 = jnp.where(sub == q, -i12, jnp.where(sub == q + 1, 1.0 - i22, m1))
            for p in range(q + 2, 8):
                cols[p] = cols[p] - (m0 * spread(cols[p], q) + m1 * spread(cols[p], q + 1))
            if g < groups - 1:
                r = r - (m0 * spread(r, q) + m1 * spread(r, q + 1))
                e = e - (m0 * spread(e, q) + m1 * spread(e, q + 1))
        out.append((f - coef * pltpu.roll(f, 1, 0)) * scale * across)
        if g < groups - 1:
            rr = [spread(r, q) for q in range(8)]
            ee = [spread(e, q) for q in range(8)]
            m = [column(rows[g + 1], 8 * g + q) for q in range(8)]
            if g < groups - 2:
                x = jnp.concatenate(rows[g + 2 :], axis=0)
                xh, xl = split(x)
                both = jnp.concatenate([r, e], axis=1)
                rh = both.astype(BF).astype(F32)
                above = [jnp.zeros((8 * g, 2 * T), F32)] * (g > 0)
                under = [jnp.zeros((T - 8 * g - 8, 2 * T), F32)]
                yh = jnp.concatenate(above + [rh] + under, axis=0).astype(BF)
                yl = jnp.concatenate(above + [both - rh] + under, axis=0).astype(BF)
                z = dot(xh, yh, 1, 0) + (dot(xl, yh, 1, 0) + dot(xh, yl, 1, 0))
                for h in range(g + 2, groups):
                    at = 8 * (h - g - 2)
                    rows[h] = rows[h] - z[at : at + 8, :T]
                    inv[h] = inv[h] - z[at : at + 8, T:]
            rows[g + 1] = rows[g + 1] - tree([m[q] * rr[q] for q in range(8)])
            inv[g + 1] = inv[g + 1] - tree([m[q] * ee[q] for q in range(8)])
        hook(g)
    return jnp.concatenate(out, axis=0)


def loop(low, high, body):
    def step(j, carry):
        body(j)
        return carry

    lax.fori_loop(low, high, step, 0)


def chip_coords(t):
    return {"yh": t // 8, "k": (t // 4) % 2, "xh": (t // 2) % 2, "s": t % 2}


def place():
    yh, k, xh, s, c = (lax.axis_index(a) for a in MP)
    return ((yh * 2 + k) * 2 + xh) * 2 + s, c


def remote(src, dst, send, recv, coords):
    return pltpu.make_async_remote_copy(
        src_ref=src, dst_ref=dst, send_sem=send, recv_sem=recv, device_id=coords, device_id_type=MESH
    )


def greet(me, chip, core):
    barrier = pltpu.get_barrier_semaphore()

    def to_dp(j, carry):
        pl.semaphore_signal(barrier, inc=1, device_id={"dp": (me + j) % 8}, device_id_type=MESH)
        return carry

    def to_chip(j, carry):
        pl.semaphore_signal(
            barrier, inc=1, device_id=chip_coords((chip + j) % 16), device_id_type=MESH
        )
        return carry

    lax.fori_loop(1, 8, to_dp, 0)
    lax.fori_loop(1, 16, to_chip, 0)
    pl.semaphore_signal(barrier, inc=1, device_id={"c": 1 - core}, device_id_type=MESH)
    return lambda: pl.semaphore_wait(barrier, 7 + 15 + 1)


def step_kernel(
    block_slot, grads, left_stats, right_stats, first, second, left_basis, right_basis,
    update, terms_out, bases_out, slot_grads, stats, moments,
    parts, total, grad, old_stat, basis, olds, a, q, stat, mul, cat, d_ref, turned,
    q_part, q_rows, term_rows, q_t, left, half, box, pieces, arrived, home_rows, home,
    dp_send, dp_recv, state_send, state_recv, quad_send, quad_recv, grad_send, grad_recv,
    left_sem, box_send, box_recv, row_send, row_recv, piece_send, piece_recv, home_send, home_recv,
    pair_send, pair_recv, own,
):
    me = lax.axis_index("dp")
    chip, core = place()
    k, side = (chip // 4) % 2, chip % 2
    corner = chip - 4 * k - side
    local = 2 * k + side
    rows, width = q_part.shape[1:]
    quarter = width // 4
    all_here = greet(me, chip, core)
    for slot in range(2):
        stats[slot, 0] = left_stats[slot].astype(BF)
        stats[slot, 1] = right_stats[slot].astype(BF)
        moments[slot, 0] = first[slot].astype(BF)
        moments[slot, 1] = second[slot].astype(BF)

    def place_grads(d):
        for slot in range(2):
            present, block = jnp.float32(0.0), jnp.int32(0)
            for b in range(grads.shape[0]):
                hit = block_slot[b] == 2 * d + slot
                present = jnp.where(hit, jnp.float32(1.0), present)
                block = jnp.where(hit, jnp.int32(b), block)
            rows_of = grads[block].astype(F32)
            slot_grads[d, slot] = (rows_of * present).astype(BF)

    loop(0, 8, place_grads)
    all_here()

    def member(number):
        return corner + 4 * (number // 2) + number % 2

    def dp_copy(j, source):
        there = (me + j) % 8
        return remote(
            slot_grads.at[there], parts.at[source], dp_send.at[there], dp_recv.at[source], {"dp": there}
        )

    def state_copy(which, j, source):
        there = (chip + j) % 16
        return remote(
            stats.at[(there // 4) % 2, there % 2],
            (old_stat, basis)[which].at[source, core],
            state_send.at[which, there],
            state_recv.at[which, source],
            chip_coords(there),
        )

    def basis_copy(to_side, j):
        there = 2 * ((chip // 2 + j) % 8) + to_side
        return remote(
            (left_basis, right_basis)[to_side].at[(there // 4) % 2],
            basis.at[chip, core],
            state_send.at[1, there],
            state_recv.at[1, chip],
            chip_coords(there),
        )

    def quad_copy(j, source):
        number = (local + j) % 4
        return remote(
            moments.at[number // 2], olds.at[source], quad_send.at[number], quad_recv.at[source],
            chip_coords(member(number)),
        )

    def grad_copy(j, source):
        there = (chip + j) % 16
        return remote(
            total.at[(there // 4) % 2], grad.at[source, core], grad_send.at[there],
            grad_recv.at[source], chip_coords(there),
        )

    def share(ref, part, n):
        return remote(
            ref.at[:, part], ref.at[:, part], pair_send.at[n], pair_recv.at[n], {"c": 1 - core}
        )

    def share_rows(ref, source, n):
        rows_of = ref.at[source, core]
        return remote(rows_of, rows_of, pair_send.at[n], pair_recv.at[n], {"c": 1 - core})

    loop(1, 8, lambda j: dp_copy(j, me).start())
    parts[me] = slot_grads[me]
    loop(1, 16, lambda j: state_copy(0, j, chip).start())
    for to_side, ref in enumerate((left_basis, right_basis)):
        loop(jnp.where(side == to_side, 1, 0), 8, lambda j: basis_copy(to_side, j).start())

        @pl.when(side == to_side)
        def _():
            pltpu.make_async_copy(ref.at[k], basis.at[chip, core], own.at[2]).start()

    old_stat[chip, core] = stats[k, side]
    olds[local] = moments[k]
    loop(1, 8, lambda j: dp_copy(j, (me + 8 - j) % 8).wait_recv())
    for slot in range(2):
        acc = parts[0, slot].astype(F32)
        for d in range(1, 8):
            acc = acc + parts[d, slot].astype(F32)
        total[slot] = acc.astype(BF)
    loop(1, 16, lambda j: grad_copy(j, chip).start())
    grad[chip, core] = total[k]
    loop(1, 4, lambda j: quad_copy(j, local).start())
    pltpu.make_async_copy(left_basis.at[k], basis.at[chip, core], own.at[2]).wait()
    for which, ref in enumerate((old_stat, basis)):
        loop(1, 16, lambda j: state_copy(which, j, (chip + 16 - j) % 16).wait_recv())
        share(ref, core, which).start()
    share_rows(grad, chip, 2).start()

    def take_grad(j):
        source = (chip + 16 - j) % 16
        grad_copy(j, source).wait_recv()
        share_rows(grad, source, 2).start()

    loop(1, 16, take_grad)
    for n, ref in ((2, grad), (0, old_stat), (1, basis)):
        share(ref, 1 - core, n).wait_recv()

    def tile(j):
        return pl.ds(pl.multiple_of(j * quarter, quarter), quarter)

    def row_tile(ref, j):
        return ref[pl.ds(j * 4, 4)].reshape(quarter, width)

    def column_tile(ref, j):
        return ref[:, :, :, tile(j)].reshape(width, quarter)

    def whole(ref):
        return ref[...].reshape(width, width)

    @pl.when(side == 0)
    def _():
        def body(j):
            a[tile(j), :] = dot(row_tile(grad, j), whole(grad), 1, 1)

        loop(0, 4, body)

    @pl.when(side != 0)
    def _():
        def body(j):
            a[tile(j), :] = dot(column_tile(grad, j), whole(grad), 0, 0)

        loop(0, 4, body)

    def owned_rows(n):
        return pl.ds(pl.multiple_of((2 * member(n) + core) * rows, rows), rows)

    def row_copy(which, j, source):
        number = (local + j) % 4
        src, out = ((term_rows, terms_out), (q_rows, bases_out))[which]
        return remote(
            src.at[number], out.at[source], row_send.at[which, number],
            row_recv.at[which, source], chip_coords(member(number)),
        )

    for n in range(4):
        term_rows[n] = a[owned_rows(n), :]
    loop(1, 4, lambda j: row_copy(0, j, local).start())
    kept_terms = pltpu.make_async_copy(term_rows.at[local], terms_out.at[local], own.at[4])
    kept_terms.start()

    def mix(j):
        stat[tile(j), :] = (
            BETA_STATS * row_tile(old_stat, j).astype(F32) + (1.0 - BETA_STATS) * a[tile(j), :]
        ).astype(BF)

    loop(0, 4, mix)

    def power(j):
        q[tile(j), :] = dot(column_tile(basis, j), stat[...], 0, 0).astype(BF).astype(F32)

    loop(0, 4, power)

    def keep_power(j):
        stat[tile(j), :] = q[tile(j), :].astype(BF)

    loop(0, 4, keep_power)

    def gram(j):
        a[tile(j), :] = dot(stat[tile(j), :], stat[...], 1, 1)

    loop(0, 4, gram)

    mul[...] = jnp.zeros_like(mul)
    cat[...] = jnp.zeros_like(cat)
    d_ref[...] = a[0:T, 0:T]
    lane = lax.broadcasted_iota(jnp.int32, (T, width), 1)

    def trail(g):
        if g % 2 == 0:
            return
        start = g // 2 * T
        there = slice(start, start + T)
        m = mul[:, there]
        a[there, start:width] -= dot(m, cat[:, start:width], 0, 0)
        q[there, :] -= dot(m, cat[:, width : 2 * width], 0, 0)

    def panel(i):
        here = pl.ds(pl.multiple_of(i * T, T), T)
        high, low = split(base_factor(d_ref[...], trail))
        inverse = jnp.concatenate([high, low, high], axis=1)
        for ref, start in ((a, 0), (q, width)):
            high, low = split(ref[here, :])
            u = dot(inverse, jnp.concatenate([high, high, low], axis=0), 1, 0)
            high, low = split(u)
            part = slice(start, start + width)
            cat[0:T, part], cat[T : 2 * T, part], cat[2 * T : 3 * T, part] = high, high, low
            if start == 0:
                high, low = split(jnp.where(lane >= (i + 1) * T, u, 0.0))
                mul[0:T, :], mul[T : 2 * T, :], mul[2 * T : 3 * T, :] = high, low, high
            else:
                q[here, :] = u
        following = pl.ds(pl.multiple_of(jnp.minimum(i + 1, width // T - 1) * T, T), T)
        d_ref[...] = a[following, following] - dot(mul[:, following], cat[:, following], 0, 0)

    loop(0, width // T, panel)

    def payload(which):
        return half if which else q_part

    def box_copy(which, number, source):
        return remote(
            payload(which).at[number], box.at[which, source], box_send.at[which, number],
            box_recv.at[which, source], chip_coords(member(number)),
        )

    def piece_copy(which, j, source):
        there = (me + j) % 8
        return remote(
            pieces.at[which, there], arrived.at[which, source], piece_send.at[which, there],
            piece_recv.at[which, source], {"dp": there},
        )

    def home_copy(which, j, source):
        there = (chip + j) % 16
        return remote(
            home_rows.at[which], home.at[which, source, core], home_send.at[which, there],
            home_recv.at[which, source], chip_coords(there),
        )

    left_copy = remote(q_part, left, left_sem.at[0], left_sem.at[1], {"s": 1 - side})

    def send_box(which):
        @pl.when(side == which)
        def _():
            loop(1, 4, lambda j: box_copy(which, (local + j) % 4, local).start())
            box[which, local] = payload(which)[local]

    def receive_box(which):
        for source in (which, which + 2):
            @pl.when(local != source)
            def _():
                box_copy(which, local, source).wait_recv()

        def piece(b):
            one, none = jnp.float32(1.0), jnp.float32(0.0)
            first_owned = jnp.where(block_slot[b] == 2 * me, one, none)
            second_owned = jnp.where(block_slot[b] == 2 * me + 1, one, none)
            return (
                box[which, which].astype(F32) * first_owned
                + box[which, which + 2].astype(F32) * second_owned
            ).astype(BF)

        def send_piece(j):
            there = (me + j) % 8
            pieces[which, there] = piece(there)
            piece_copy(which, j, me).start()

        loop(1, 8, send_piece)
        arrived[which, me] = piece(me)

    def gather_home(which):
        loop(1, 8, lambda j: piece_copy(which, j, (me + 8 - j) % 8).wait_recv())
        acc = arrived[which, 0].astype(F32)
        for d in range(1, 8):
            acc = acc + arrived[which, d].astype(F32)
        home_rows[which] = acc.astype(BF)
        loop(1, 16, lambda j: home_copy(which, j, chip).start())
        home[which, chip, core] = home_rows[which]

    for n in range(4):
        q_part[n] = q[owned_rows(n), :].astype(BF)

    send_box(0)

    @pl.when(side == 0)
    def _():
        left_copy.start()

    @pl.when(side == 1)
    def _():
        def cast(j):
            q_t[tile(j), :] = q[tile(j), :].astype(BF)

        def move(j):
            stat[tile(j), :] = dot(row_tile(grad, j), q_t[...], 1, 1).astype(BF)

        loop(0, 4, cast)
        loop(0, 4, move)

    receive_box(0)

    @pl.when(side == 1)
    def _():
        left_copy.wait_recv()

    loop(1, 4, lambda j: quad_copy(j, (local + 4 - j) % 4).wait_recv())

    @pl.when(side == 1)
    def _():
        def normalize(n):
            rotated = dot(left[n], stat[...], 1, 0)
            first = BETA_FIRST * olds[n, 0].astype(F32) + (1.0 - BETA_FIRST) * rotated
            second = (
                BETA_SECOND * olds[n, 1].astype(F32) + (1.0 - BETA_SECOND) * rotated * rotated
            )
            left[n] = (first / (jnp.sqrt(second) + EPSILON)).astype(BF)

        loop(0, 4, normalize)
        normed = left[...].reshape(4 * rows, width)
        half[...] = dot(normed, q_t[...], 1, 0).astype(BF).reshape(4, rows, width)

    send_box(1)
    receive_box(1)
    for slot in range(2):
        columns = pl.ds(pl.multiple_of((corner + 4 * slot) // 2 * T, T), T)
        turned[...] = q[:, columns].T
        for side_to in range(2):
            these = pl.ds(pl.multiple_of((2 * side_to + core) * rows, rows), rows)
            q_rows[2 * slot + side_to] = turned[these, :].astype(BF)
    gather_home(0)
    loop(1, 4, lambda j: row_copy(1, j, local).start())
    kept_bases = pltpu.make_async_copy(q_rows.at[local], bases_out.at[local], own.at[5])
    kept_bases.start()
    gather_home(1)
    for which in range(2):
        share_rows(home.at[which], chip, 3 + which).start()

        def take_home(j):
            source = (chip + 16 - j) % 16
            home_copy(which, j, source).wait_recv()
            share_rows(home.at[which], source, 3 + which).start()

        loop(1, 16, take_home)
    for which in range(2):
        share(home.at[which], 1 - core, 3 + which).wait_recv()

    def multiply(j):
        update[tile(j), :] = dot(
            home[0, :, :, :, tile(j)].reshape(width, quarter), home[1].reshape(width, width), 0, 0
        ).astype(BF)

    loop(0, 4, multiply)

    kept_terms.wait()
    kept_bases.wait()
    for which in range(2):
        loop(1, 4, lambda j: row_copy(which, j, (local + 4 - j) % 4).wait_recv())
        loop(1, 4, lambda j: row_copy(which, j, local).wait_send())
        loop(1, 8, lambda j: piece_copy(which, j, me).wait_send())
        loop(1, 16, lambda j: home_copy(which, j, chip).wait_send())
        loop(1, 16, lambda j: state_copy(which, j, chip).wait_send())
        share(home.at[which], core, 3 + which).wait_send()

        @pl.when(side == which)
        def _():
            loop(1, 4, lambda j: box_copy(which, (local + j) % 4, local).wait_send())

    for n, ref in enumerate((old_stat, basis, grad)):
        share(ref, core, n).wait_send()
    loop(1, 8, lambda j: dp_copy(j, me).wait_send())
    loop(1, 16, lambda j: grad_copy(j, chip).wait_send())
    loop(1, 4, lambda j: quad_copy(j, local).wait_send())

    @pl.when(side == 0)
    def _():
        left_copy.wait_send()


def optimizer_step(block_slot, grads, left_stats, right_stats, first, second, left_basis, right_basis):
    rows, width = grads.shape[-2:]
    dma = pltpu.SemaphoreType.DMA
    vmem = pltpu.VMEM
    full = vmem((16, 2, rows, width), BF)
    return pl.pallas_call(
        step_kernel,
        out_shape=(
            jax.ShapeDtypeStruct((width, width), BF),
            jax.ShapeDtypeStruct((4, rows, width), F32),
            jax.ShapeDtypeStruct((4, rows, width), BF),
        ),
        in_specs=[pl.BlockSpec(memory_space=pltpu.SMEM)] + [pl.BlockSpec(memory_space=vmem)] * 5 + [ANY] * 2,
        out_specs=(pl.BlockSpec(memory_space=vmem), ANY, ANY),
        scratch_shapes=[
            vmem((8, 2, rows, width), BF),
            vmem((2, 2, rows, width), BF), vmem((2, 2, rows, width), BF),
            vmem((8, 2, rows, width), BF),
            vmem((2, rows, width), BF),
            full, full, full,
            vmem((4, 2, rows, width), BF),
            vmem((width, width), F32), vmem((width, width), F32), vmem((width, width), BF),
            vmem((3 * T, width), BF), vmem((3 * T, 2 * width), BF),
            vmem((T, T), F32), vmem((T, width), F32),
            vmem((4, rows, width), BF), vmem((4, rows, width), BF), vmem((4, rows, width), F32),
            vmem((width, width), BF),
            vmem((4, rows, width), BF), vmem((4, rows, width), BF),
            vmem((2, 4, rows, width), BF),
            vmem((2, 8, rows, width), BF), vmem((2, 8, rows, width), BF),
            vmem((2, rows, width), BF), vmem((2, 16, 2, rows, width), BF),
            dma((8,)), dma((8,)), dma((2, 16)), dma((2, 16)), dma((4,)), dma((4,)), dma((16,)), dma((16,)),
            dma((2,)), dma((2, 4)), dma((2, 4)), dma((2, 4)), dma((2, 4)), dma((2, 8)), dma((2, 8)),
            dma((2, 16)), dma((2, 16)), dma((5,)), dma((5,)), dma((6,)),
        ],
        compiler_params=pltpu.CompilerParams(
            collective_id=0, has_side_effects=True, vmem_limit_bytes=56 * 2**20
        ),
    )(block_slot, grads, left_stats, right_stats, first, second, left_basis, right_basis)


def per_device(
    grads, block_slot, left_stats, right_stats, left_basis, right_basis, first_moment, second_moment
):
    capacity, rows, width = left_stats.shape
    slot_ids = lax.axis_index("dp") * capacity + jnp.arange(capacity, dtype=jnp.int32)
    owns = block_slot[:, None] == slot_ids[None, :]
    held_mask = jnp.any(owns, axis=0)[:, None, None]

    update, terms, new_bases = optimizer_step(
        block_slot,
        grads[0],
        left_stats,
        right_stats,
        first_moment,
        second_moment,
        left_basis,
        right_basis,
    )

    def merged(new, old):
        return jnp.where(held_mask, new, old)

    terms = terms.reshape(2, 2, rows, width)
    new_bases = new_bases.reshape(2, 2, rows, width)
    return (
        update[None],
        merged(BETA_STATS * left_stats + (1.0 - BETA_STATS) * terms[:, 0], left_stats),
        merged(BETA_STATS * right_stats + (1.0 - BETA_STATS) * terms[:, 1], right_stats),
        merged(new_bases[:, 0], left_basis),
        merged(new_bases[:, 1], right_basis),
    )


def solution(mesh):
    groups = mesh.shape["dp"]
    fine = Mesh(mesh.devices.reshape(groups, 2, 2, 2, 2, 2), ("dp",) + MP)
    rows = P("dp", MP, None)
    return jax.shard_map(
        per_device,
        mesh=fine,
        in_specs=(P("dp", None, MP, None), P()) + (rows,) * 6,
        out_specs=(P("dp", None, None),) + (rows,) * 4,
        check_vma=False,
    )
```

```python
import functools

import jax
import jax.numpy as jnp
from jax import lax
from jax.experimental import pallas as pl
from jax.experimental.pallas import tpu as pltpu
from jax.sharding import Mesh
from jax.sharding import PartitionSpec as P

BETA_STATS = 0.95
BETA_FIRST = 0.9
BETA_SECOND = 0.95
EPSILON = 1e-08
F32 = jnp.float32
BF = jnp.bfloat16
T = 128
MP = ("yh", "k", "xh", "s", "c")
MESH = pl.DeviceIdType.MESH
ANY = pl.BlockSpec(memory_space=pl.ANY)


def split(x):
    high = x.astype(BF)
    return high, (x - high.astype(F32)).astype(BF)


def dot(a, b, a_dim, b_dim):
    return lax.dot_general(a, b, (((a_dim,), (b_dim,)), ((), ())), preferred_element_type=F32)


def reciprocal(x):
    r = pl.reciprocal(x, approx=True)
    return r * (2.0 - x * r)


def tree(terms):
    while len(terms) > 1:
        terms = [a + b for a, b in zip(terms[::2], terms[1::2])]
    return terms[0]


def base_factor(block, hook):
    sub = lax.broadcasted_iota(jnp.int32, (8, T), 0)
    lane = lax.broadcasted_iota(jnp.int32, (8, T), 1)
    groups = T // 8

    def spread(x, q):
        return jnp.broadcast_to(x[q : q + 1, :], (8, T))

    def column(x, at):
        return jnp.broadcast_to(x[:, at : at + 1], (8, T))

    eye = lax.broadcasted_iota(jnp.int32, (T, T), 0) == lax.broadcasted_iota(jnp.int32, (T, T), 1)
    diag = jnp.where(eye, block, 0.0)
    across = lax.rsqrt(jnp.sum(diag, axis=0, keepdims=True))
    down = jnp.sum(jnp.where(eye, jnp.broadcast_to(across, (T, T)), 0.0), axis=1, keepdims=True)
    block = block * across * down
    rows = [block[8 * g : 8 * g + 8, :] for g in range(groups)]
    inv = [(lane == sub + 8 * g).astype(F32) for g in range(groups)]
    out = []
    for g in range(groups):
        r, e = rows[g], inv[g]
        f = e
        cols = [column(r, 8 * g + q) for q in range(8)]
        scale = jnp.zeros((8, T), F32)
        coef = jnp.zeros((8, T), F32)
        for q in range(0, 8, 2):
            x, y = cols[q], cols[q + 1]
            a, b, c = spread(x, q), spread(x, q + 1), spread(y, q + 1)
            det = a * c - b * b
            rd = reciprocal(det)
            i11, i22, i12 = c * rd, a * rd, -(b * rd)
            root = lax.rsqrt(a)
            scale = jnp.where(sub == q, root, scale)
            scale = jnp.where(sub == q + 1, a * root * lax.rsqrt(det), scale)
            coef = jnp.where(sub == q + 1, b * root * root, coef)
            m0 = x * i11 + y * i12
            m1 = x * i12 + y * i22
            if q < 6:
                f = f - (
                    jnp.where(sub > q + 1, m0, 0.0) * spread(f, q)
                    + jnp.where(sub > q + 1, m1, 0.0) * spread(f, q + 1)
                )
            m0 = jnp.where(sub == q, 1.0 - i11, jnp.where(sub == q + 1, -i12, m0))
            m1 = jnp.where(sub == q, -i12, jnp.where(sub == q + 1, 1.0 - i22, m1))
            for p in range(q + 2, 8):
                cols[p] = cols[p] - (m0 * spread(cols[p], q) + m1 * spread(cols[p], q + 1))
            if g < groups - 1:
                r = r - (m0 * spread(r, q) + m1 * spread(r, q + 1))
                e = e - (m0 * spread(e, q) + m1 * spread(e, q + 1))
        out.append((f - coef * pltpu.roll(f, 1, 0)) * scale * across)
        if g < groups - 1:
            rr = [spread(r, q) for q in range(8)]
            ee = [spread(e, q) for q in range(8)]
            m = [column(rows[g + 1], 8 * g + q) for q in range(8)]
            if g < groups - 2:
                x = jnp.concatenate(rows[g + 2 :], axis=0)
                xh, xl = split(x)
                both = jnp.concatenate([r, e], axis=1)
                rh = both.astype(BF).astype(F32)
                above = [jnp.zeros((8 * g, 2 * T), F32)] * (g > 0)
                under = [jnp.zeros((T - 8 * g - 8, 2 * T), F32)]
                yh = jnp.concatenate(above + [rh] + under, axis=0).astype(BF)
                yl = jnp.concatenate(above + [both - rh] + under, axis=0).astype(BF)
                z = dot(xh, yh, 1, 0) + (dot(xl, yh, 1, 0) + dot(xh, yl, 1, 0))
                for h in range(g + 2, groups):
                    at = 8 * (h - g - 2)
                    rows[h] = rows[h] - z[at : at + 8, :T]
                    inv[h] = inv[h] - z[at : at + 8, T:]
            rows[g + 1] = rows[g + 1] - tree([m[q] * rr[q] for q in range(8)])
            inv[g + 1] = inv[g + 1] - tree([m[q] * ee[q] for q in range(8)])
        hook(g)
    return jnp.concatenate(out, axis=0)


def loop(low, high, body):
    def step(j, carry):
        body(j)
        return carry

    lax.fori_loop(low, high, step, 0)


def chip_coords(t):
    return {"yh": t // 8, "k": (t // 4) % 2, "xh": (t // 2) % 2, "s": t % 2}


def place():
    yh, k, xh, s, c = (lax.axis_index(a) for a in MP)
    return ((yh * 2 + k) * 2 + xh) * 2 + s, c


def remote(src, dst, send, recv, coords):
    return pltpu.make_async_remote_copy(
        src_ref=src, dst_ref=dst, send_sem=send, recv_sem=recv, device_id=coords, device_id_type=MESH
    )


def greet(me, chip, core):
    barrier = pltpu.get_barrier_semaphore()

    def to_dp(j, carry):
        pl.semaphore_signal(barrier, inc=1, device_id={"dp": (me + j) % 8}, device_id_type=MESH)
        return carry

    def to_chip(j, carry):
        pl.semaphore_signal(
            barrier, inc=1, device_id=chip_coords((chip + j) % 16), device_id_type=MESH
        )
        return carry

    lax.fori_loop(1, 8, to_dp, 0)
    lax.fori_loop(1, 16, to_chip, 0)
    pl.semaphore_signal(barrier, inc=1, device_id={"c": 1 - core}, device_id_type=MESH)
    return lambda: pl.semaphore_wait(barrier, 7 + 15 + 1)


def step_kernel(
    block_slot, grads, left_stats, right_stats, first, second, left_basis, right_basis,
    update, terms_out, bases_out, slot_grads, stats, moments,
    parts, total, grad, old_stat, basis, olds, a, q, stat, mul, cat, d_ref, turned,
    q_part, q_rows, term_rows, q_t, left, half, box, pieces, arrived, home_rows, home,
    dp_send, dp_recv, state_send, state_recv, quad_send, quad_recv, grad_send, grad_recv,
    left_sem, box_send, box_recv, row_send, row_recv, piece_send, piece_recv, home_send, home_recv,
    pair_send, pair_recv, own,
):
    me = lax.axis_index("dp")
    chip, core = place()
    k, side = (chip // 4) % 2, chip % 2
    corner = chip - 4 * k - side
    local = 2 * k + side
    rows, width = q_part.shape[1:]
    quarter = width // 4
    all_here = greet(me, chip, core)
    for slot in range(2):
        stats[slot, 0] = left_stats[slot].astype(BF)
        stats[slot, 1] = right_stats[slot].astype(BF)
        moments[slot, 0] = first[slot].astype(BF)
        moments[slot, 1] = second[slot].astype(BF)

    def place_grads(d):
        for slot in range(2):
            present, block = jnp.float32(0.0), jnp.int32(0)
            for b in range(grads.shape[0]):
                hit = block_slot[b] == 2 * d + slot
                present = jnp.where(hit, jnp.float32(1.0), present)
                block = jnp.where(hit, jnp.int32(b), block)
            rows_of = grads[block].astype(F32)
            slot_grads[d, slot] = (rows_of * present).astype(BF)

    loop(0, 8, place_grads)
    all_here()

    def member(number):
        return corner + 4 * (number // 2) + number % 2

    def dp_copy(j, source):
        there = (me + j) % 8
        return remote(
            slot_grads.at[there], parts.at[source], dp_send.at[there], dp_recv.at[source], {"dp": there}
        )

    def state_copy(which, j, source):
        there = (chip + j) % 16
        return remote(
            stats.at[(there // 4) % 2, there % 2],
            (old_stat, basis)[which].at[source, core],
            state_send.at[which, there],
            state_recv.at[which, source],
            chip_coords(there),
        )

    def basis_copy(to_side, j):
        there = 2 * ((chip // 2 + j) % 8) + to_side
        return remote(
            (left_basis, right_basis)[to_side].at[(there // 4) % 2],
            basis.at[chip, core],
            state_send.at[1, there],
            state_recv.at[1, chip],
            chip_coords(there),
        )

    def quad_copy(j, source):
        number = (local + j) % 4
        return remote(
            moments.at[number // 2], olds.at[source], quad_send.at[number], quad_recv.at[source],
            chip_coords(member(number)),
        )

    def grad_copy(j, source):
        there = (chip + j) % 16
        return remote(
            total.at[(there // 4) % 2], grad.at[source, core], grad_send.at[there],
            grad_recv.at[source], chip_coords(there),
        )

    def share(ref, part, n):
        return remote(
            ref.at[:, part], ref.at[:, part], pair_send.at[n], pair_recv.at[n], {"c": 1 - core}
        )

    def share_rows(ref, source, n):
        rows_of = ref.at[source, core]
        return remote(rows_of, rows_of, pair_send.at[n], pair_recv.at[n], {"c": 1 - core})

    loop(1, 8, lambda j: dp_copy(j, me).start())
    parts[me] = slot_grads[me]
    loop(1, 16, lambda j: state_copy(0, j, chip).start())
    for to_side, ref in enumerate((left_basis, right_basis)):
        loop(jnp.where(side == to_side, 1, 0), 8, lambda j: basis_copy(to_side, j).start())

        @pl.when(side == to_side)
        def _():
            pltpu.make_async_copy(ref.at[k], basis.at[chip, core], own.at[2]).start()

    old_stat[chip, core] = stats[k, side]
    olds[local] = moments[k]
    loop(1, 8, lambda j: dp_copy(j, (me + 8 - j) % 8).wait_recv())
    for slot in range(2):
        acc = parts[0, slot].astype(F32)
        for d in range(1, 8):
            acc = acc + parts[d, slot].astype(F32)
        total[slot] = acc.astype(BF)
    loop(1, 16, lambda j: grad_copy(j, chip).start())
    grad[chip, core] = total[k]
    loop(1, 4, lambda j: quad_copy(j, local).start())
    pltpu.make_async_copy(left_basis.at[k], basis.at[chip, core], own.at[2]).wait()
    for which, ref in enumerate((old_stat, basis)):
        loop(1, 16, lambda j: state_copy(which, j, (chip + 16 - j) % 16).wait_recv())
        share(ref, core, which).start()
    share_rows(grad, chip, 2).start()

    def take_grad(j):
        source = (chip + 16 - j) % 16
        grad_copy(j, source).wait_recv()
        share_rows(grad, source, 2).start()

    loop(1, 16, take_grad)
    for n, ref in ((2, grad), (0, old_stat), (1, basis)):
        share(ref, 1 - core, n).wait_recv()

    def tile(j):
        return pl.ds(pl.multiple_of(j * quarter, quarter), quarter)

    def row_tile(ref, j):
        return ref[pl.ds(j * 4, 4)].reshape(quarter, width)

    def column_tile(ref, j):
        return ref[:, :, :, tile(j)].reshape(width, quarter)

    def whole(ref):
        return ref[...].reshape(width, width)

    @pl.when(side == 0)
    def _():
        def body(j):
            a[tile(j), :] = dot(row_tile(grad, j), whole(grad), 1, 1)

        loop(0, 4, body)

    @pl.when(side != 0)
    def _():
        def body(j):
            a[tile(j), :] = dot(column_tile(grad, j), whole(grad), 0, 0)

        loop(0, 4, body)

    def owned_rows(n):
        return pl.ds(pl.multiple_of((2 * member(n) + core) * rows, rows), rows)

    def row_copy(which, j, source):
        number = (local + j) % 4
        src, out = ((term_rows, terms_out), (q_rows, bases_out))[which]
        return remote(
            src.at[number], out.at[source], row_send.at[which, number],
            row_recv.at[which, source], chip_coords(member(number)),
        )

    for n in range(4):
        term_rows[n] = a[owned_rows(n), :]
    loop(1, 4, lambda j: row_copy(0, j, local).start())
    kept_terms = pltpu.make_async_copy(term_rows.at[local], terms_out.at[local], own.at[4])
    kept_terms.start()

    def mix(j):
        stat[tile(j), :] = (
            BETA_STATS * row_tile(old_stat, j).astype(F32) + (1.0 - BETA_STATS) * a[tile(j), :]
        ).astype(BF)

    loop(0, 4, mix)

    def power(j):
        q[tile(j), :] = dot(column_tile(basis, j), stat[...], 0, 0).astype(BF).astype(F32)

    loop(0, 4, power)

    def keep_power(j):
        stat[tile(j), :] = q[tile(j), :].astype(BF)

    loop(0, 4, keep_power)

    def gram(j):
        a[tile(j), :] = dot(stat[tile(j), :], stat[...], 1, 1)

    loop(0, 4, gram)

    mul[...] = jnp.zeros_like(mul)
    cat[...] = jnp.zeros_like(cat)
    d_ref[...] = a[0:T, 0:T]
    lane = lax.broadcasted_iota(jnp.int32, (T, width), 1)

    def trail(g):
        if g % 2 == 0:
            return
        start = g // 2 * T
        there = slice(start, start + T)
        m = mul[:, there]
        a[there, start:width] -= dot(m, cat[:, start:width], 0, 0)
        q[there, :] -= dot(m, cat[:, width : 2 * width], 0, 0)

    def panel(i):
        here = pl.ds(pl.multiple_of(i * T, T), T)
        high, low = split(base_factor(d_ref[...], trail))
        inverse = jnp.concatenate([high, low, high], axis=1)
        for ref, start in ((a, 0), (q, width)):
            high, low = split(ref[here, :])
            u = dot(inverse, jnp.concatenate([high, high, low], axis=0), 1, 0)
            high, low = split(u)
            part = slice(start, start + width)
            cat[0:T, part], cat[T : 2 * T, part], cat[2 * T : 3 * T, part] = high, high, low
            if start == 0:
                high, low = split(jnp.where(lane >= (i + 1) * T, u, 0.0))
                mul[0:T, :], mul[T : 2 * T, :], mul[2 * T : 3 * T, :] = high, low, high
            else:
                q[here, :] = u
        following = pl.ds(pl.multiple_of(jnp.minimum(i + 1, width // T - 1) * T, T), T)
        d_ref[...] = a[following, following] - dot(mul[:, following], cat[:, following], 0, 0)

    loop(0, width // T, panel)

    def payload(which):
        return half if which else q_part

    def box_copy(which, number, source):
        return remote(
            payload(which).at[number], box.at[which, source], box_send.at[which, number],
            box_recv.at[which, source], chip_coords(member(number)),
        )

    ways = ((0, 0, rows), (1, 0, rows // 2), (1, rows // 2, rows))

    def piece_copy(way, j, source):
        there = (me + j) % 8
        which, low, high = ways[way]
        return remote(
            pieces.at[which, there, low:high], arrived.at[which, source, low:high],
            piece_send.at[way, there], piece_recv.at[way, source], {"dp": there},
        )

    def home_copy(way, j, source):
        there = (chip + j) % 16
        which, low, high = ways[way]
        return remote(
            home_rows.at[which, low:high], home.at[which, source, core, low:high],
            home_send.at[way, there], home_recv.at[way, source], chip_coords(there),
        )

    def pair_copy(way, source, part):
        which, low, high = ways[way]
        rows_of = home.at[which, source, part, low:high]
        return remote(
            rows_of, rows_of, pair_send.at[3 + way], pair_recv.at[3 + way], {"c": 1 - core}
        )

    left_copy = remote(q_part, left, left_sem.at[0], left_sem.at[1], {"s": 1 - side})

    def send_box(which):
        @pl.when(side == which)
        def _():
            loop(1, 4, lambda j: box_copy(which, (local + j) % 4, local).start())
            box[which, local] = payload(which)[local]

    def receive_box(which):
        for source in (which, which + 2):
            @pl.when(local != source)
            def _():
                box_copy(which, local, source).wait_recv()

        def piece(b):
            one, none = jnp.float32(1.0), jnp.float32(0.0)
            first_owned = jnp.where(block_slot[b] == 2 * me, one, none)
            second_owned = jnp.where(block_slot[b] == 2 * me + 1, one, none)
            return (
                box[which, which].astype(F32) * first_owned
                + box[which, which + 2].astype(F32) * second_owned
            ).astype(BF)

        def send_piece(j):
            there = (me + j) % 8
            pieces[which, there] = piece(there)
            piece_copy(which, j, me).start()

        loop(1, 8, send_piece)
        if which == 1:
            loop(1, 8, lambda j: piece_copy(2, j, me).start())
        arrived[which, me] = piece(me)

    def gather_home(way):
        which, low, high = ways[way]
        loop(1, 8, lambda j: piece_copy(way, j, (me + 8 - j) % 8).wait_recv())
        acc = arrived[which, 0, low:high].astype(F32)
        for d in range(1, 8):
            acc = acc + arrived[which, d, low:high].astype(F32)
        home_rows[which, low:high] = acc.astype(BF)
        loop(1, 16, lambda j: home_copy(way, j, chip).start())
        home[which, chip, core, low:high] = acc.astype(BF)
        pair_copy(way, chip, core).start()

    for n in range(4):
        q_part[n] = q[owned_rows(n), :].astype(BF)

    send_box(0)

    @pl.when(side == 0)
    def _():
        left_copy.start()

    @pl.when(side == 1)
    def _():
        def cast(j):
            q_t[tile(j), :] = q[tile(j), :].astype(BF)

        def move(j):
            stat[tile(j), :] = dot(row_tile(grad, j), q_t[...], 1, 1).astype(BF)

        loop(0, 4, cast)
        loop(0, 4, move)

    receive_box(0)

    @pl.when(side == 1)
    def _():
        left_copy.wait_recv()

    loop(1, 4, lambda j: quad_copy(j, (local + 4 - j) % 4).wait_recv())

    @pl.when(side == 1)
    def _():
        def normalize(n):
            rotated = dot(left[n], stat[...], 1, 0)
            first = BETA_FIRST * olds[n, 0].astype(F32) + (1.0 - BETA_FIRST) * rotated
            second = (
                BETA_SECOND * olds[n, 1].astype(F32) + (1.0 - BETA_SECOND) * rotated * rotated
            )
            left[n] = (first / (jnp.sqrt(second) + EPSILON)).astype(BF)

        loop(0, 4, normalize)
        normed = left[...].reshape(4 * rows, width)
        half[...] = dot(normed, q_t[...], 1, 0).astype(BF).reshape(4, rows, width)

    send_box(1)
    receive_box(1)
    for slot in range(2):
        columns = pl.ds(pl.multiple_of((corner + 4 * slot) // 2 * T, T), T)
        turned[...] = q[:, columns].T
        for side_to in range(2):
            these = pl.ds(pl.multiple_of((2 * side_to + core) * rows, rows), rows)
            q_rows[2 * slot + side_to] = turned[these, :].astype(BF)
    gather_home(0)
    loop(1, 4, lambda j: row_copy(1, j, local).start())
    kept_bases = pltpu.make_async_copy(q_rows.at[local], bases_out.at[local], own.at[5])
    kept_bases.start()
    gather_home(1)
    gather_home(2)

    def take_home(way):
        def take(j):
            source = (chip + 16 - j) % 16
            home_copy(way, j, source).wait_recv()
            pair_copy(way, source, core).start()

        loop(1, 16, take)

    everywhere = slice(None)
    middle = rows // 2
    take_home(0)
    take_home(1)
    for way in range(2):
        pair_copy(way, everywhere, 1 - core).wait_recv()

    def product(j, low, high):
        deep = width * (high - low) // rows
        return dot(
            home[0, :, :, low:high, tile(j)].reshape(deep, quarter),
            home[1, :, :, low:high].reshape(deep, width), 0, 0,
        )

    def multiply_first(j):
        a[tile(j), :] = product(j, 0, middle)

    def multiply_second(j):
        update[tile(j), :] = (a[tile(j), :] + product(j, middle, rows)).astype(BF)

    loop(0, 4, multiply_first)
    take_home(2)
    pair_copy(2, everywhere, 1 - core).wait_recv()
    loop(0, 4, multiply_second)

    kept_terms.wait()
    kept_bases.wait()
    for which in range(2):
        loop(1, 4, lambda j: row_copy(which, j, (local + 4 - j) % 4).wait_recv())
        loop(1, 4, lambda j: row_copy(which, j, local).wait_send())
        loop(1, 16, lambda j: state_copy(which, j, chip).wait_send())

        @pl.when(side == which)
        def _():
            loop(1, 4, lambda j: box_copy(which, (local + j) % 4, local).wait_send())

    for way in range(3):
        loop(1, 8, lambda j: piece_copy(way, j, me).wait_send())
        loop(1, 16, lambda j: home_copy(way, j, chip).wait_send())
        pair_copy(way, everywhere, core).wait_send()
    for n, ref in enumerate((old_stat, basis, grad)):
        share(ref, core, n).wait_send()
    loop(1, 8, lambda j: dp_copy(j, me).wait_send())
    loop(1, 16, lambda j: grad_copy(j, chip).wait_send())
    loop(1, 4, lambda j: quad_copy(j, local).wait_send())

    @pl.when(side == 0)
    def _():
        left_copy.wait_send()


def optimizer_step(block_slot, grads, left_stats, right_stats, first, second, left_basis, right_basis):
    rows, width = grads.shape[-2:]
    dma = pltpu.SemaphoreType.DMA
    vmem = pltpu.VMEM
    full = vmem((16, 2, rows, width), BF)
    return pl.pallas_call(
        step_kernel,
        out_shape=(
            jax.ShapeDtypeStruct((width, width), BF),
            jax.ShapeDtypeStruct((4, rows, width), F32),
            jax.ShapeDtypeStruct((4, rows, width), BF),
        ),
        in_specs=[pl.BlockSpec(memory_space=pltpu.SMEM)] + [pl.BlockSpec(memory_space=vmem)] * 5 + [ANY] * 2,
        out_specs=(pl.BlockSpec(memory_space=vmem), ANY, ANY),
        scratch_shapes=[
            vmem((8, 2, rows, width), BF),
            vmem((2, 2, rows, width), BF), vmem((2, 2, rows, width), BF),
            vmem((8, 2, rows, width), BF),
            vmem((2, rows, width), BF),
            full, full, full,
            vmem((4, 2, rows, width), BF),
            vmem((width, width), F32), vmem((width, width), F32), vmem((width, width), BF),
            vmem((3 * T, width), BF), vmem((3 * T, 2 * width), BF),
            vmem((T, T), F32), vmem((T, width), F32),
            vmem((4, rows, width), BF), vmem((4, rows, width), BF), vmem((4, rows, width), F32),
            vmem((width, width), BF),
            vmem((4, rows, width), BF), vmem((4, rows, width), BF),
            vmem((2, 4, rows, width), BF),
            vmem((2, 8, rows, width), BF), vmem((2, 8, rows, width), BF),
            vmem((2, rows, width), BF), vmem((2, 16, 2, rows, width), BF),
            dma((8,)), dma((8,)), dma((2, 16)), dma((2, 16)), dma((4,)), dma((4,)), dma((16,)), dma((16,)),
            dma((2,)), dma((2, 4)), dma((2, 4)), dma((2, 4)), dma((2, 4)), dma((3, 8)), dma((3, 8)),
            dma((3, 16)), dma((3, 16)), dma((6,)), dma((6,)), dma((6,)),
        ],
        compiler_params=pltpu.CompilerParams(
            collective_id=0, has_side_effects=True, vmem_limit_bytes=56 * 2**20
        ),
    )(block_slot, grads, left_stats, right_stats, first, second, left_basis, right_basis)


def per_device(
    grads, block_slot, left_stats, right_stats, left_basis, right_basis, first_moment, second_moment
):
    capacity, rows, width = left_stats.shape
    slot_ids = lax.axis_index("dp") * capacity + jnp.arange(capacity, dtype=jnp.int32)
    owns = block_slot[:, None] == slot_ids[None, :]
    held_mask = jnp.any(owns, axis=0)[:, None, None]

    update, terms, new_bases = optimizer_step(
        block_slot,
        grads[0],
        left_stats,
        right_stats,
        first_moment,
        second_moment,
        left_basis,
        right_basis,
    )

    def merged(new, old):
        return jnp.where(held_mask, new, old)

    terms = terms.reshape(2, 2, rows, width)
    new_bases = new_bases.reshape(2, 2, rows, width)
    return (
        update[None],
        merged(BETA_STATS * left_stats + (1.0 - BETA_STATS) * terms[:, 0], left_stats),
        merged(BETA_STATS * right_stats + (1.0 - BETA_STATS) * terms[:, 1], right_stats),
        merged(new_bases[:, 0], left_basis),
        merged(new_bases[:, 1], right_basis),
    )


def solution(mesh):
    groups = mesh.shape["dp"]
    fine = Mesh(mesh.devices.reshape(groups, 2, 2, 2, 2, 2), ("dp",) + MP)
    rows = P("dp", MP, None)
    return jax.shard_map(
        per_device,
        mesh=fine,
        in_specs=(P("dp", None, MP, None), P()) + (rows,) * 6,
        out_specs=(P("dp", None, None),) + (rows,) * 4,
        check_vma=False,
    )
```

```python
import functools

import jax
import jax.numpy as jnp
from jax import lax
from jax.experimental import pallas as pl
from jax.experimental.pallas import tpu as pltpu
from jax.sharding import Mesh
from jax.sharding import PartitionSpec as P

BETA_STATS = 0.95
BETA_FIRST = 0.9
BETA_SECOND = 0.95
EPSILON = 1e-08
F32 = jnp.float32
BF = jnp.bfloat16
T = 128
MP = ("yh", "k", "xh", "s", "c")
MESH = pl.DeviceIdType.MESH
ANY = pl.BlockSpec(memory_space=pl.ANY)


def split(x):
    high = x.astype(BF)
    return high, (x - high.astype(F32)).astype(BF)


def dot(a, b, a_dim, b_dim):
    return lax.dot_general(a, b, (((a_dim,), (b_dim,)), ((), ())), preferred_element_type=F32)


def reciprocal(x):
    r = pl.reciprocal(x, approx=True)
    return r * (2.0 - x * r)


def tree(terms):
    while len(terms) > 1:
        terms = [a + b for a, b in zip(terms[::2], terms[1::2])]
    return terms[0]


def base_factor(block, hook):
    sub = lax.broadcasted_iota(jnp.int32, (8, T), 0)
    lane = lax.broadcasted_iota(jnp.int32, (8, T), 1)
    groups = T // 8

    def spread(x, q):
        return jnp.broadcast_to(x[q : q + 1, :], (8, T))

    def column(x, at):
        return jnp.broadcast_to(x[:, at : at + 1], (8, T))

    eye = lax.broadcasted_iota(jnp.int32, (T, T), 0) == lax.broadcasted_iota(jnp.int32, (T, T), 1)
    diag = jnp.where(eye, block, 0.0)
    across = lax.rsqrt(jnp.sum(diag, axis=0, keepdims=True))
    down = jnp.sum(jnp.where(eye, jnp.broadcast_to(across, (T, T)), 0.0), axis=1, keepdims=True)
    block = block * across * down
    rows = [block[8 * g : 8 * g + 8, :] for g in range(groups)]
    inv = [(lane == sub + 8 * g).astype(F32) for g in range(groups)]
    out = []
    for g in range(groups):
        r, e = rows[g], inv[g]
        f = e
        cols = [column(r, 8 * g + q) for q in range(8)]
        scale = jnp.zeros((8, T), F32)
        coef = jnp.zeros((8, T), F32)
        for q in range(0, 8, 2):
            x, y = cols[q], cols[q + 1]
            a, b, c = spread(x, q), spread(x, q + 1), spread(y, q + 1)
            det = a * c - b * b
            rd = reciprocal(det)
            i11, i22, i12 = c * rd, a * rd, -(b * rd)
            root = lax.rsqrt(a)
            scale = jnp.where(sub == q, root, scale)
            scale = jnp.where(sub == q + 1, a * root * lax.rsqrt(det), scale)
            coef = jnp.where(sub == q + 1, b * root * root, coef)
            m0 = x * i11 + y * i12
            m1 = x * i12 + y * i22
            if q < 6:
                f = f - (
                    jnp.where(sub > q + 1, m0, 0.0) * spread(f, q)
                    + jnp.where(sub > q + 1, m1, 0.0) * spread(f, q + 1)
                )
            m0 = jnp.where(sub == q, 1.0 - i11, jnp.where(sub == q + 1, -i12, m0))
            m1 = jnp.where(sub == q, -i12, jnp.where(sub == q + 1, 1.0 - i22, m1))
            for p in range(q + 2, 8):
                cols[p] = cols[p] - (m0 * spread(cols[p], q) + m1 * spread(cols[p], q + 1))
            if g < groups - 1:
                r = r - (m0 * spread(r, q) + m1 * spread(r, q + 1))
                e = e - (m0 * spread(e, q) + m1 * spread(e, q + 1))
        out.append((f - coef * pltpu.roll(f, 1, 0)) * scale * across)
        if g < groups - 1:
            rr = [spread(r, q) for q in range(8)]
            ee = [spread(e, q) for q in range(8)]
            m = [column(rows[g + 1], 8 * g + q) for q in range(8)]
            if g < groups - 2:
                x = jnp.concatenate(rows[g + 2 :], axis=0)
                xh, xl = split(x)
                both = jnp.concatenate([r, e], axis=1)
                rh = both.astype(BF).astype(F32)
                above = [jnp.zeros((8 * g, 2 * T), F32)] * (g > 0)
                under = [jnp.zeros((T - 8 * g - 8, 2 * T), F32)]
                yh = jnp.concatenate(above + [rh] + under, axis=0).astype(BF)
                yl = jnp.concatenate(above + [both - rh] + under, axis=0).astype(BF)
                z = dot(xh, yh, 1, 0) + (dot(xl, yh, 1, 0) + dot(xh, yl, 1, 0))
                for h in range(g + 2, groups):
                    at = 8 * (h - g - 2)
                    rows[h] = rows[h] - z[at : at + 8, :T]
                    inv[h] = inv[h] - z[at : at + 8, T:]
            rows[g + 1] = rows[g + 1] - tree([m[q] * rr[q] for q in range(8)])
            inv[g + 1] = inv[g + 1] - tree([m[q] * ee[q] for q in range(8)])
        hook(g)
    return jnp.concatenate(out, axis=0)


def loop(low, high, body):
    def step(j, carry):
        body(j)
        return carry

    lax.fori_loop(low, high, step, 0)


def chip_coords(t):
    return {"yh": t // 8, "k": (t // 4) % 2, "xh": (t // 2) % 2, "s": t % 2}


def place():
    yh, k, xh, s, c = (lax.axis_index(a) for a in MP)
    return ((yh * 2 + k) * 2 + xh) * 2 + s, c


def remote(src, dst, send, recv, coords):
    return pltpu.make_async_remote_copy(
        src_ref=src, dst_ref=dst, send_sem=send, recv_sem=recv, device_id=coords, device_id_type=MESH
    )


def greet(me, chip, core):
    barrier = pltpu.get_barrier_semaphore()

    def to_dp(j, carry):
        pl.semaphore_signal(barrier, inc=1, device_id={"dp": (me + j) % 8}, device_id_type=MESH)
        return carry

    def to_chip(j, carry):
        pl.semaphore_signal(
            barrier, inc=1, device_id=chip_coords((chip + j) % 16), device_id_type=MESH
        )
        return carry

    lax.fori_loop(1, 8, to_dp, 0)
    lax.fori_loop(1, 16, to_chip, 0)
    pl.semaphore_signal(barrier, inc=1, device_id={"c": 1 - core}, device_id_type=MESH)
    return lambda: pl.semaphore_wait(barrier, 7 + 15 + 1)


def step_kernel(
    block_slot, grads, left_stats, right_stats, first, second, left_basis, right_basis,
    update, terms_out, bases_out, slot_grads, stats, moments,
    parts, total, grad, old_stat, basis, olds, a, q, stat, mul, cat, d_ref, turned,
    q_part, q_rows, term_rows, q_t, left, half, box, pieces, arrived, home_rows, home,
    dp_send, dp_recv, state_send, state_recv, quad_send, quad_recv, grad_send, grad_recv,
    left_sem, box_send, box_recv, row_send, row_recv, piece_send, piece_recv, home_send, home_recv,
    pair_send, pair_recv, own,
):
    me = lax.axis_index("dp")
    chip, core = place()
    k, side = (chip // 4) % 2, chip % 2
    corner = chip - 4 * k - side
    local = 2 * k + side
    rows, width = q_part.shape[1:]
    quarter = width // 4
    all_here = greet(me, chip, core)
    for slot in range(2):
        stats[slot, 0] = left_stats[slot].astype(BF)
        stats[slot, 1] = right_stats[slot].astype(BF)
        moments[slot, 0] = first[slot].astype(BF)
        moments[slot, 1] = second[slot].astype(BF)

    def place_grads(d):
        for slot in range(2):
            present, block = jnp.float32(0.0), jnp.int32(0)
            for b in range(grads.shape[0]):
                hit = block_slot[b] == 2 * d + slot
                present = jnp.where(hit, jnp.float32(1.0), present)
                block = jnp.where(hit, jnp.int32(b), block)
            rows_of = grads[block].astype(F32)
            slot_grads[d, slot] = (rows_of * present).astype(BF)

    loop(0, 8, place_grads)
    mul[...] = jnp.zeros_like(mul)
    cat[...] = jnp.zeros_like(cat)
    all_here()

    def member(number):
        return corner + 4 * (number // 2) + number % 2

    def dp_copy(j, source):
        there = (me + j) % 8
        return remote(
            slot_grads.at[there], parts.at[source], dp_send.at[there], dp_recv.at[source], {"dp": there}
        )

    def state_copy(which, j, source):
        there = (chip + j) % 16
        return remote(
            stats.at[(there // 4) % 2, there % 2],
            (old_stat, basis)[which].at[source, core],
            state_send.at[which, there],
            state_recv.at[which, source],
            chip_coords(there),
        )

    def basis_copy(to_side, j):
        there = 2 * ((chip // 2 + j) % 8) + to_side
        return remote(
            (left_basis, right_basis)[to_side].at[(there // 4) % 2],
            basis.at[chip, core],
            state_send.at[1, there],
            state_recv.at[1, chip],
            chip_coords(there),
        )

    def quad_copy(j, source):
        number = (local + j) % 4
        return remote(
            moments.at[number // 2], olds.at[source], quad_send.at[number], quad_recv.at[source],
            chip_coords(member(number)),
        )

    def grad_copy(j, source):
        there = (chip + j) % 16
        return remote(
            total.at[(there // 4) % 2], grad.at[source, core], grad_send.at[there],
            grad_recv.at[source], chip_coords(there),
        )

    def share(ref, part, n):
        return remote(
            ref.at[:, part], ref.at[:, part], pair_send.at[n], pair_recv.at[n], {"c": 1 - core}
        )

    def share_rows(ref, source, n):
        rows_of = ref.at[source, core]
        return remote(rows_of, rows_of, pair_send.at[n], pair_recv.at[n], {"c": 1 - core})

    loop(1, 8, lambda j: dp_copy(j, me).start())
    parts[me] = slot_grads[me]
    loop(1, 16, lambda j: state_copy(0, j, chip).start())
    for to_side, ref in enumerate((left_basis, right_basis)):
        loop(jnp.where(side == to_side, 1, 0), 8, lambda j: basis_copy(to_side, j).start())

        @pl.when(side == to_side)
        def _():
            pltpu.make_async_copy(ref.at[k], basis.at[chip, core], own.at[2]).start()

    old_stat[chip, core] = stats[k, side]
    olds[local] = moments[k]
    loop(1, 8, lambda j: dp_copy(j, (me + 8 - j) % 8).wait_recv())
    for slot in range(2):
        acc = parts[0, slot].astype(F32)
        for d in range(1, 8):
            acc = acc + parts[d, slot].astype(F32)
        total[slot] = acc.astype(BF)
    loop(1, 16, lambda j: grad_copy(j, chip).start())
    grad[chip, core] = total[k]
    loop(1, 4, lambda j: quad_copy(j, local).start())
    pltpu.make_async_copy(left_basis.at[k], basis.at[chip, core], own.at[2]).wait()
    for which, ref in enumerate((old_stat, basis)):
        loop(1, 16, lambda j: state_copy(which, j, (chip + 16 - j) % 16).wait_recv())
        share(ref, core, which).start()
    share_rows(grad, chip, 2).start()

    def take_grad(j):
        source = (chip + 16 - j) % 16
        grad_copy(j, source).wait_recv()
        share_rows(grad, source, 2).start()

    loop(1, 16, take_grad)
    for n, ref in ((2, grad), (0, old_stat), (1, basis)):
        share(ref, 1 - core, n).wait_recv()

    def tile(j):
        return pl.ds(pl.multiple_of(j * quarter, quarter), quarter)

    def row_tile(ref, j):
        return ref[pl.ds(j * 4, 4)].reshape(quarter, width)

    def column_tile(ref, j):
        return ref[:, :, :, tile(j)].reshape(width, quarter)

    def whole(ref):
        return ref[...].reshape(width, width)

    @pl.when(side == 0)
    def _():
        def body(j):
            a[tile(j), :] = dot(row_tile(grad, j), whole(grad), 1, 1)

        loop(0, 4, body)

    @pl.when(side != 0)
    def _():
        def body(j):
            a[tile(j), :] = dot(column_tile(grad, j), whole(grad), 0, 0)

        loop(0, 4, body)

    def owned_rows(n):
        return pl.ds(pl.multiple_of((2 * member(n) + core) * rows, rows), rows)

    def row_copy(which, j, source):
        number = (local + j) % 4
        src, out = ((term_rows, terms_out), (q_rows, bases_out))[which]
        return remote(
            src.at[number], out.at[source], row_send.at[which, number],
            row_recv.at[which, source], chip_coords(member(number)),
        )

    for n in range(4):
        term_rows[n] = a[owned_rows(n), :]
    loop(1, 4, lambda j: row_copy(0, j, local).start())
    kept_terms = pltpu.make_async_copy(term_rows.at[local], terms_out.at[local], own.at[4])
    kept_terms.start()

    def mix(j):
        stat[tile(j), :] = (
            BETA_STATS * row_tile(old_stat, j).astype(F32) + (1.0 - BETA_STATS) * a[tile(j), :]
        ).astype(BF)

    loop(0, 4, mix)

    def power(j):
        q[tile(j), :] = dot(column_tile(basis, j), stat[...], 0, 0).astype(BF).astype(F32)

    loop(0, 4, power)

    def keep_power(j):
        stat[tile(j), :] = q[tile(j), :].astype(BF)

    loop(0, 4, keep_power)

    def gram(j):
        a[tile(j), :] = dot(stat[tile(j), :], stat[...], 1, 1)

    loop(0, 4, gram)

    d_ref[...] = a[0:T, 0:T]
    lane = lax.broadcasted_iota(jnp.int32, (T, width), 1)

    def trail(g):
        if g % 2 == 0:
            return
        start = g // 2 * T
        there = slice(start, start + T)
        m = mul[:, there]
        a[there, start:width] -= dot(m, cat[:, start:width], 0, 0)
        q[there, :] -= dot(m, cat[:, width : 2 * width], 0, 0)

    def panel(i):
        here = pl.ds(pl.multiple_of(i * T, T), T)
        high, low = split(base_factor(d_ref[...], trail))
        inverse = jnp.concatenate([high, low, high], axis=1)
        for ref, start in ((a, 0), (q, width)):
            high, low = split(ref[here, :])
            u = dot(inverse, jnp.concatenate([high, high, low], axis=0), 1, 0)
            high, low = split(u)
            part = slice(start, start + width)
            cat[0:T, part], cat[T : 2 * T, part], cat[2 * T : 3 * T, part] = high, high, low
            if start == 0:
                high, low = split(jnp.where(lane >= (i + 1) * T, u, 0.0))
                mul[0:T, :], mul[T : 2 * T, :], mul[2 * T : 3 * T, :] = high, low, high
            else:
                q[here, :] = u
        following = pl.ds(pl.multiple_of(jnp.minimum(i + 1, width // T - 1) * T, T), T)
        d_ref[...] = a[following, following] - dot(mul[:, following], cat[:, following], 0, 0)

    loop(0, width // T, panel)

    def payload(which):
        return half if which else q_part

    def box_copy(which, number, source):
        return remote(
            payload(which).at[number], box.at[which, source], box_send.at[which, number],
            box_recv.at[which, source], chip_coords(member(number)),
        )

    ways = ((0, 0, rows), (1, 0, rows // 2), (1, rows // 2, rows))

    def piece_copy(way, j, source):
        there = (me + j) % 8
        which, low, high = ways[way]
        return remote(
            pieces.at[which, there, low:high], arrived.at[which, source, low:high],
            piece_send.at[way, there], piece_recv.at[way, source], {"dp": there},
        )

    def home_copy(way, j, source):
        there = (chip + j) % 16
        which, low, high = ways[way]
        return remote(
            home_rows.at[which, low:high], home.at[which, source, core, low:high],
            home_send.at[way, there], home_recv.at[way, source], chip_coords(there),
        )

    def pair_copy(way, source, part):
        which, low, high = ways[way]
        rows_of = home.at[which, source, part, low:high]
        return remote(
            rows_of, rows_of, pair_send.at[3 + way], pair_recv.at[3 + way], {"c": 1 - core}
        )

    left_copy = remote(q_part, left, left_sem.at[0], left_sem.at[1], {"s": 1 - side})

    def send_box(which):
        @pl.when(side == which)
        def _():
            loop(1, 4, lambda j: box_copy(which, (local + j) % 4, local).start())
            box[which, local] = payload(which)[local]

    def receive_box(which):
        for source in (which, which + 2):
            @pl.when(local != source)
            def _():
                box_copy(which, local, source).wait_recv()

        def piece(b):
            one, none = jnp.float32(1.0), jnp.float32(0.0)
            first_owned = jnp.where(block_slot[b] == 2 * me, one, none)
            second_owned = jnp.where(block_slot[b] == 2 * me + 1, one, none)
            return (
                box[which, which].astype(F32) * first_owned
                + box[which, which + 2].astype(F32) * second_owned
            ).astype(BF)

        def send_piece(j):
            there = (me + j) % 8
            pieces[which, there] = piece(there)
            piece_copy(which, j, me).start()

        loop(1, 8, send_piece)
        if which == 1:
            loop(1, 8, lambda j: piece_copy(2, j, me).start())
        arrived[which, me] = piece(me)

    def gather_home(way):
        which, low, high = ways[way]
        loop(1, 8, lambda j: piece_copy(way, j, (me + 8 - j) % 8).wait_recv())
        acc = arrived[which, 0, low:high].astype(F32)
        for d in range(1, 8):
            acc = acc + arrived[which, d, low:high].astype(F32)
        home_rows[which, low:high] = acc.astype(BF)
        loop(1, 16, lambda j: home_copy(way, j, chip).start())
        home[which, chip, core, low:high] = acc.astype(BF)
        pair_copy(way, chip, core).start()

    for n in range(4):
        q_part[n] = q[owned_rows(n), :].astype(BF)

    send_box(0)

    @pl.when(side == 0)
    def _():
        left_copy.start()

    @pl.when(side == 1)
    def _():
        def cast(j):
            q_t[tile(j), :] = q[tile(j), :].astype(BF)

        def move(j):
            stat[tile(j), :] = dot(row_tile(grad, j), q_t[...], 1, 1).astype(BF)

        loop(0, 4, cast)
        loop(0, 4, move)

    receive_box(0)

    @pl.when(side == 1)
    def _():
        left_copy.wait_recv()

    loop(1, 4, lambda j: quad_copy(j, (local + 4 - j) % 4).wait_recv())

    @pl.when(side == 1)
    def _():
        def normalize(n):
            rotated = dot(left[n], stat[...], 1, 0)
            first = BETA_FIRST * olds[n, 0].astype(F32) + (1.0 - BETA_FIRST) * rotated
            second = (
                BETA_SECOND * olds[n, 1].astype(F32) + (1.0 - BETA_SECOND) * rotated * rotated
            )
            left[n] = (first / (jnp.sqrt(second) + EPSILON)).astype(BF)

        loop(0, 4, normalize)
        normed = left[...].reshape(4 * rows, width)
        half[...] = dot(normed, q_t[...], 1, 0).astype(BF).reshape(4, rows, width)

    send_box(1)
    receive_box(1)
    gather_home(0)
    for slot in range(2):
        columns = pl.ds(pl.multiple_of((corner + 4 * slot) // 2 * T, T), T)
        turned[...] = q[:, columns].T
        for side_to in range(2):
            these = pl.ds(pl.multiple_of((2 * side_to + core) * rows, rows), rows)
            q_rows[2 * slot + side_to] = turned[these, :].astype(BF)
    loop(1, 4, lambda j: row_copy(1, j, local).start())
    kept_bases = pltpu.make_async_copy(q_rows.at[local], bases_out.at[local], own.at[5])
    kept_bases.start()
    gather_home(1)
    gather_home(2)

    def take_home(way):
        def take(j):
            source = (chip + 16 - j) % 16
            home_copy(way, j, source).wait_recv()
            pair_copy(way, source, core).start()

        loop(1, 16, take)

    everywhere = slice(None)
    middle = rows // 2
    take_home(0)
    take_home(1)
    for way in range(2):
        pair_copy(way, everywhere, 1 - core).wait_recv()

    def product(j, low, high):
        deep = width * (high - low) // rows
        return dot(
            home[0, :, :, low:high, tile(j)].reshape(deep, quarter),
            home[1, :, :, low:high].reshape(deep, width), 0, 0,
        )

    def multiply_first(j):
        a[tile(j), :] = product(j, 0, middle)

    def multiply_second(j):
        update[tile(j), :] = (a[tile(j), :] + product(j, middle, rows)).astype(BF)

    loop(0, 4, multiply_first)
    take_home(2)
    pair_copy(2, everywhere, 1 - core).wait_recv()
    loop(0, 4, multiply_second)

    kept_terms.wait()
    kept_bases.wait()
    for which in range(2):
        loop(1, 4, lambda j: row_copy(which, j, (local + 4 - j) % 4).wait_recv())
        loop(1, 4, lambda j: row_copy(which, j, local).wait_send())
        loop(1, 16, lambda j: state_copy(which, j, chip).wait_send())

        @pl.when(side == which)
        def _():
            loop(1, 4, lambda j: box_copy(which, (local + j) % 4, local).wait_send())

    for way in range(3):
        loop(1, 8, lambda j: piece_copy(way, j, me).wait_send())
        loop(1, 16, lambda j: home_copy(way, j, chip).wait_send())
        pair_copy(way, everywhere, core).wait_send()
    for n, ref in enumerate((old_stat, basis, grad)):
        share(ref, core, n).wait_send()
    loop(1, 8, lambda j: dp_copy(j, me).wait_send())
    loop(1, 16, lambda j: grad_copy(j, chip).wait_send())
    loop(1, 4, lambda j: quad_copy(j, local).wait_send())

    @pl.when(side == 0)
    def _():
        left_copy.wait_send()


def optimizer_step(block_slot, grads, left_stats, right_stats, first, second, left_basis, right_basis):
    rows, width = grads.shape[-2:]
    dma = pltpu.SemaphoreType.DMA
    vmem = pltpu.VMEM
    full = vmem((16, 2, rows, width), BF)
    return pl.pallas_call(
        step_kernel,
        out_shape=(
            jax.ShapeDtypeStruct((width, width), BF),
            jax.ShapeDtypeStruct((4, rows, width), F32),
            jax.ShapeDtypeStruct((4, rows, width), BF),
        ),
        in_specs=[pl.BlockSpec(memory_space=pltpu.SMEM)] + [pl.BlockSpec(memory_space=vmem)] * 5 + [ANY] * 2,
        out_specs=(pl.BlockSpec(memory_space=vmem), ANY, ANY),
        scratch_shapes=[
            vmem((8, 2, rows, width), BF),
            vmem((2, 2, rows, width), BF), vmem((2, 2, rows, width), BF),
            vmem((8, 2, rows, width), BF),
            vmem((2, rows, width), BF),
            full, full, full,
            vmem((4, 2, rows, width), BF),
            vmem((width, width), F32), vmem((width, width), F32), vmem((width, width), BF),
            vmem((3 * T, width), BF), vmem((3 * T, 2 * width), BF),
            vmem((T, T), F32), vmem((T, width), F32),
            vmem((4, rows, width), BF), vmem((4, rows, width), BF), vmem((4, rows, width), F32),
            vmem((width, width), BF),
            vmem((4, rows, width), BF), vmem((4, rows, width), BF),
            vmem((2, 4, rows, width), BF),
            vmem((2, 8, rows, width), BF), vmem((2, 8, rows, width), BF),
            vmem((2, rows, width), BF), vmem((2, 16, 2, rows, width), BF),
            dma((8,)), dma((8,)), dma((2, 16)), dma((2, 16)), dma((4,)), dma((4,)), dma((16,)), dma((16,)),
            dma((2,)), dma((2, 4)), dma((2, 4)), dma((2, 4)), dma((2, 4)), dma((3, 8)), dma((3, 8)),
            dma((3, 16)), dma((3, 16)), dma((6,)), dma((6,)), dma((6,)),
        ],
        compiler_params=pltpu.CompilerParams(
            collective_id=0, has_side_effects=True, vmem_limit_bytes=56 * 2**20
        ),
    )(block_slot, grads, left_stats, right_stats, first, second, left_basis, right_basis)


def per_device(
    grads, block_slot, left_stats, right_stats, left_basis, right_basis, first_moment, second_moment
):
    capacity, rows, width = left_stats.shape
    slot_ids = lax.axis_index("dp") * capacity + jnp.arange(capacity, dtype=jnp.int32)
    owns = block_slot[:, None] == slot_ids[None, :]
    held_mask = jnp.any(owns, axis=0)[:, None, None]

    update, terms, new_bases = optimizer_step(
        block_slot,
        grads[0],
        left_stats,
        right_stats,
        first_moment,
        second_moment,
        left_basis,
        right_basis,
    )

    def merged(new, old):
        return jnp.where(held_mask, new, old)

    terms = terms.reshape(2, 2, rows, width)
    new_bases = new_bases.reshape(2, 2, rows, width)
    return (
        update[None],
        merged(BETA_STATS * left_stats + (1.0 - BETA_STATS) * terms[:, 0], left_stats),
        merged(BETA_STATS * right_stats + (1.0 - BETA_STATS) * terms[:, 1], right_stats),
        merged(new_bases[:, 0], left_basis),
        merged(new_bases[:, 1], right_basis),
    )


def solution(mesh):
    groups = mesh.shape["dp"]
    fine = Mesh(mesh.devices.reshape(groups, 2, 2, 2, 2, 2), ("dp",) + MP)
    rows = P("dp", MP, None)
    return jax.shard_map(
        per_device,
        mesh=fine,
        in_specs=(P("dp", None, MP, None), P()) + (rows,) * 6,
        out_specs=(P("dp", None, None),) + (rows,) * 4,
        check_vma=False,
    )
```

```python
import functools

import jax
import jax.numpy as jnp
from jax import lax
from jax.experimental import pallas as pl
from jax.experimental.pallas import tpu as pltpu
from jax.sharding import Mesh
from jax.sharding import PartitionSpec as P

BETA_STATS = 0.95
BETA_FIRST = 0.9
BETA_SECOND = 0.95
EPSILON = 1e-08
F32 = jnp.float32
BF = jnp.bfloat16
T = 128
MP = ("yh", "k", "xh", "s", "c")
MESH = pl.DeviceIdType.MESH
ANY = pl.BlockSpec(memory_space=pl.ANY)


def split(x):
    high = x.astype(BF)
    return high, (x - high.astype(F32)).astype(BF)


def dot(a, b, a_dim, b_dim):
    return lax.dot_general(a, b, (((a_dim,), (b_dim,)), ((), ())), preferred_element_type=F32)


def reciprocal(x):
    r = pl.reciprocal(x, approx=True)
    return r * (2.0 - x * r)


def tree(terms):
    while len(terms) > 1:
        terms = [a + b for a, b in zip(terms[::2], terms[1::2])]
    return terms[0]


def base_factor(block, hook):
    sub = lax.broadcasted_iota(jnp.int32, (8, T), 0)
    lane = lax.broadcasted_iota(jnp.int32, (8, T), 1)
    groups = T // 8

    def spread(x, q):
        return jnp.broadcast_to(x[q : q + 1, :], (8, T))

    def column(x, at):
        return jnp.broadcast_to(x[:, at : at + 1], (8, T))

    eye = lax.broadcasted_iota(jnp.int32, (T, T), 0) == lax.broadcasted_iota(jnp.int32, (T, T), 1)
    diag = jnp.where(eye, block, 0.0)
    across = lax.rsqrt(jnp.sum(diag, axis=0, keepdims=True))
    down = jnp.sum(jnp.where(eye, jnp.broadcast_to(across, (T, T)), 0.0), axis=1, keepdims=True)
    block = block * across * down
    rows = [block[8 * g : 8 * g + 8, :] for g in range(groups)]
    inv = [(lane == sub + 8 * g).astype(F32) for g in range(groups)]
    out = []
    for g in range(groups):
        r, e = rows[g], inv[g]
        f = e
        cols = [column(r, 8 * g + q) for q in range(8)]
        scale = jnp.zeros((8, T), F32)
        coef = jnp.zeros((8, T), F32)
        for q in range(0, 8, 2):
            x, y = cols[q], cols[q + 1]
            a, b, c = spread(x, q), spread(x, q + 1), spread(y, q + 1)
            det = a * c - b * b
            rd = reciprocal(det)
            i11, i22, i12 = c * rd, a * rd, -(b * rd)
            root = lax.rsqrt(a)
            scale = jnp.where(sub == q, root, scale)
            scale = jnp.where(sub == q + 1, a * root * lax.rsqrt(det), scale)
            coef = jnp.where(sub == q + 1, b * root * root, coef)
            m0 = x * i11 + y * i12
            m1 = x * i12 + y * i22
            if q < 6:
                f = f - (
                    jnp.where(sub > q + 1, m0, 0.0) * spread(f, q)
                    + jnp.where(sub > q + 1, m1, 0.0) * spread(f, q + 1)
                )
            m0 = jnp.where(sub == q, 1.0 - i11, jnp.where(sub == q + 1, -i12, m0))
            m1 = jnp.where(sub == q, -i12, jnp.where(sub == q + 1, 1.0 - i22, m1))
            for p in range(q + 2, 8):
                cols[p] = cols[p] - (m0 * spread(cols[p], q) + m1 * spread(cols[p], q + 1))
            if g < groups - 1:
                r = r - (m0 * spread(r, q) + m1 * spread(r, q + 1))
                e = e - (m0 * spread(e, q) + m1 * spread(e, q + 1))
        out.append((f - coef * pltpu.roll(f, 1, 0)) * scale * across)
        if g < groups - 1:
            rr = [spread(r, q) for q in range(8)]
            ee = [spread(e, q) for q in range(8)]
            m = [column(rows[g + 1], 8 * g + q) for q in range(8)]
            if g < groups - 2:
                x = jnp.concatenate(rows[g + 2 :], axis=0)
                xh, xl = split(x)
                both = jnp.concatenate([r, e], axis=1)
                rh = both.astype(BF).astype(F32)
                above = [jnp.zeros((8 * g, 2 * T), F32)] * (g > 0)
                under = [jnp.zeros((T - 8 * g - 8, 2 * T), F32)]
                yh = jnp.concatenate(above + [rh] + under, axis=0).astype(BF)
                yl = jnp.concatenate(above + [both - rh] + under, axis=0).astype(BF)
                z = dot(xh, yh, 1, 0) + (dot(xl, yh, 1, 0) + dot(xh, yl, 1, 0))
                for h in range(g + 2, groups):
                    at = 8 * (h - g - 2)
                    rows[h] = rows[h] - z[at : at + 8, :T]
                    inv[h] = inv[h] - z[at : at + 8, T:]
            rows[g + 1] = rows[g + 1] - tree([m[q] * rr[q] for q in range(8)])
            inv[g + 1] = inv[g + 1] - tree([m[q] * ee[q] for q in range(8)])
        hook(g)
    return jnp.concatenate(out, axis=0)


def loop(low, high, body):
    def step(j, carry):
        body(j)
        return carry

    lax.fori_loop(low, high, step, 0)


def chip_coords(t):
    return {"yh": t // 8, "k": (t // 4) % 2, "xh": (t // 2) % 2, "s": t % 2}


def place():
    yh, k, xh, s, c = (lax.axis_index(a) for a in MP)
    return ((yh * 2 + k) * 2 + xh) * 2 + s, c


def remote(src, dst, send, recv, coords):
    return pltpu.make_async_remote_copy(
        src_ref=src, dst_ref=dst, send_sem=send, recv_sem=recv, device_id=coords, device_id_type=MESH
    )


def greet(me, chip, core):
    barrier = pltpu.get_barrier_semaphore()

    def to_dp(j, carry):
        pl.semaphore_signal(barrier, inc=1, device_id={"dp": (me + j) % 8}, device_id_type=MESH)
        return carry

    def to_chip(j, carry):
        pl.semaphore_signal(
            barrier, inc=1, device_id=chip_coords((chip + j) % 16), device_id_type=MESH
        )
        return carry

    lax.fori_loop(1, 8, to_dp, 0)
    lax.fori_loop(1, 16, to_chip, 0)
    pl.semaphore_signal(barrier, inc=1, device_id={"c": 1 - core}, device_id_type=MESH)
    return lambda: pl.semaphore_wait(barrier, 7 + 15 + 1)


def step_kernel(
    block_slot, grads, left_stats, right_stats, first, second, left_basis, right_basis,
    update, terms_out, bases_out, slot_grads, stats, moments,
    parts, total, grad, old_stat, basis, olds, a, q, stat, mul, cat, d_ref, turned,
    q_part, q_rows, term_rows, q_t, left, half, box, pieces, arrived, home_rows, home,
    dp_send, dp_recv, state_send, state_recv, quad_send, quad_recv, grad_send, grad_recv,
    left_sem, box_send, box_recv, row_send, row_recv, piece_send, piece_recv, home_send, home_recv,
    pair_send, pair_recv, own,
):
    me = lax.axis_index("dp")
    chip, core = place()
    k, side = (chip // 4) % 2, chip % 2
    corner = chip - 4 * k - side
    local = 2 * k + side
    rows, width = q_part.shape[1:]
    quarter = width // 4
    all_here = greet(me, chip, core)
    for slot in range(2):
        stats[slot, 0] = left_stats[slot].astype(BF)
        stats[slot, 1] = right_stats[slot].astype(BF)
        moments[slot, 0] = first[slot].astype(BF)
        moments[slot, 1] = second[slot].astype(BF)

    def place_grads(d):
        for slot in range(2):
            present, block = jnp.float32(0.0), jnp.int32(0)
            for b in range(grads.shape[0]):
                hit = block_slot[b] == 2 * d + slot
                present = jnp.where(hit, jnp.float32(1.0), present)
                block = jnp.where(hit, jnp.int32(b), block)
            rows_of = grads[block].astype(F32)
            slot_grads[d, slot] = (rows_of * present).astype(BF)

    loop(0, 8, place_grads)
    mul[...] = jnp.zeros_like(mul)
    cat[...] = jnp.zeros_like(cat)
    all_here()

    def member(number):
        return corner + 4 * (number // 2) + number % 2

    def dp_copy(j, source):
        there = (me + j) % 8
        return remote(
            slot_grads.at[there], parts.at[source], dp_send.at[there], dp_recv.at[source], {"dp": there}
        )

    def state_copy(which, j, source):
        there = (chip + j) % 16
        return remote(
            stats.at[(there // 4) % 2, there % 2],
            (old_stat, basis)[which].at[source, core],
            state_send.at[which, there],
            state_recv.at[which, source],
            chip_coords(there),
        )

    def basis_copy(to_side, j):
        there = 2 * ((chip // 2 + j) % 8) + to_side
        return remote(
            (left_basis, right_basis)[to_side].at[(there // 4) % 2],
            basis.at[chip, core],
            state_send.at[1, there],
            state_recv.at[1, chip],
            chip_coords(there),
        )

    def quad_copy(j, source):
        number = (local + j) % 4
        return remote(
            moments.at[number // 2], olds.at[source], quad_send.at[number], quad_recv.at[source],
            chip_coords(member(number)),
        )

    def grad_copy(j, source):
        there = (chip + j) % 16
        return remote(
            total.at[(there // 4) % 2], grad.at[source, core], grad_send.at[there],
            grad_recv.at[source], chip_coords(there),
        )

    def share(ref, part, n):
        return remote(
            ref.at[:, part], ref.at[:, part], pair_send.at[n], pair_recv.at[n], {"c": 1 - core}
        )

    def share_rows(ref, source, n):
        rows_of = ref.at[source, core]
        return remote(rows_of, rows_of, pair_send.at[n], pair_recv.at[n], {"c": 1 - core})

    loop(1, 8, lambda j: dp_copy(j, me).start())
    parts[me] = slot_grads[me]
    loop(1, 16, lambda j: state_copy(0, j, chip).start())
    for to_side, ref in enumerate((left_basis, right_basis)):
        loop(jnp.where(side == to_side, 1, 0), 8, lambda j: basis_copy(to_side, j).start())

        @pl.when(side == to_side)
        def _():
            pltpu.make_async_copy(ref.at[k], basis.at[chip, core], own.at[2]).start()

    old_stat[chip, core] = stats[k, side]
    olds[local] = moments[k]
    loop(1, 8, lambda j: dp_copy(j, (me + 8 - j) % 8).wait_recv())
    for slot in range(2):
        acc = parts[0, slot].astype(F32)
        for d in range(1, 8):
            acc = acc + parts[d, slot].astype(F32)
        total[slot] = acc.astype(BF)
    loop(1, 16, lambda j: grad_copy(j, chip).start())
    grad[chip, core] = total[k]
    pltpu.make_async_copy(left_basis.at[k], basis.at[chip, core], own.at[2]).wait()
    for which, ref in enumerate((old_stat, basis)):
        loop(1, 16, lambda j: state_copy(which, j, (chip + 16 - j) % 16).wait_recv())
        share(ref, core, which).start()
    share_rows(grad, chip, 2).start()

    def take_grad(j):
        source = (chip + 16 - j) % 16
        grad_copy(j, source).wait_recv()
        share_rows(grad, source, 2).start()

    loop(1, 16, take_grad)
    for n, ref in ((2, grad), (0, old_stat), (1, basis)):
        share(ref, 1 - core, n).wait_recv()

    def tile(j):
        return pl.ds(pl.multiple_of(j * quarter, quarter), quarter)

    def row_tile(ref, j):
        return ref[pl.ds(j * 4, 4)].reshape(quarter, width)

    def column_tile(ref, j):
        return ref[:, :, :, tile(j)].reshape(width, quarter)

    def whole(ref):
        return ref[...].reshape(width, width)

    @pl.when(side == 0)
    def _():
        def body(j):
            a[tile(j), :] = dot(row_tile(grad, j), whole(grad), 1, 1)

        loop(0, 4, body)

    @pl.when(side != 0)
    def _():
        def body(j):
            a[tile(j), :] = dot(column_tile(grad, j), whole(grad), 0, 0)

        loop(0, 4, body)

    def owned_rows(n):
        return pl.ds(pl.multiple_of((2 * member(n) + core) * rows, rows), rows)

    def row_copy(which, j, source):
        number = (local + j) % 4
        src, out = ((term_rows, terms_out), (q_rows, bases_out))[which]
        return remote(
            src.at[number], out.at[source], row_send.at[which, number],
            row_recv.at[which, source], chip_coords(member(number)),
        )

    for n in range(4):
        term_rows[n] = a[owned_rows(n), :]
    loop(1, 4, lambda j: row_copy(0, j, local).start())
    loop(1, 4, lambda j: quad_copy(j, local).start())
    kept_terms = pltpu.make_async_copy(term_rows.at[local], terms_out.at[local], own.at[4])
    kept_terms.start()

    def mix(j):
        stat[tile(j), :] = (
            BETA_STATS * row_tile(old_stat, j).astype(F32) + (1.0 - BETA_STATS) * a[tile(j), :]
        ).astype(BF)

    loop(0, 4, mix)

    def power(j):
        q[tile(j), :] = dot(column_tile(basis, j), stat[...], 0, 0).astype(BF).astype(F32)

    loop(0, 4, power)

    def keep_power(j):
        stat[tile(j), :] = q[tile(j), :].astype(BF)

    loop(0, 4, keep_power)

    def gram(j):
        a[tile(j), :] = dot(stat[tile(j), :], stat[...], 1, 1)

    loop(0, 4, gram)

    d_ref[...] = a[0:T, 0:T]
    lane = lax.broadcasted_iota(jnp.int32, (T, width), 1)

    def trail(g):
        if g % 2 == 0:
            return
        start = g // 2 * T
        there = slice(start, start + T)
        m = mul[:, there]
        a[there, start:width] -= dot(m, cat[:, start:width], 0, 0)
        q[there, :] -= dot(m, cat[:, width : 2 * width], 0, 0)

    def panel(i):
        here = pl.ds(pl.multiple_of(i * T, T), T)
        high, low = split(base_factor(d_ref[...], trail))
        inverse = jnp.concatenate([high, low, high], axis=1)
        for ref, start in ((a, 0), (q, width)):
            high, low = split(ref[here, :])
            u = dot(inverse, jnp.concatenate([high, high, low], axis=0), 1, 0)
            high, low = split(u)
            part = slice(start, start + width)
            cat[0:T, part], cat[T : 2 * T, part], cat[2 * T : 3 * T, part] = high, high, low
            if start == 0:
                high, low = split(jnp.where(lane >= (i + 1) * T, u, 0.0))
                mul[0:T, :], mul[T : 2 * T, :], mul[2 * T : 3 * T, :] = high, low, high
            else:
                q[here, :] = u
        following = pl.ds(pl.multiple_of(jnp.minimum(i + 1, width // T - 1) * T, T), T)
        d_ref[...] = a[following, following] - dot(mul[:, following], cat[:, following], 0, 0)

    loop(0, width // T, panel)

    def payload(which):
        return half if which else q_part

    def box_copy(which, number, source):
        return remote(
            payload(which).at[number], box.at[which, source], box_send.at[which, number],
            box_recv.at[which, source], chip_coords(member(number)),
        )

    ways = ((0, 0, rows), (1, 0, rows // 2), (1, rows // 2, rows))

    def piece_copy(way, j, source):
        there = (me + j) % 8
        which, low, high = ways[way]
        return remote(
            pieces.at[which, there, low:high], arrived.at[which, source, low:high],
            piece_send.at[way, there], piece_recv.at[way, source], {"dp": there},
        )

    def home_copy(way, j, source):
        there = (chip + j) % 16
        which, low, high = ways[way]
        return remote(
            home_rows.at[which, low:high], home.at[which, source, core, low:high],
            home_send.at[way, there], home_recv.at[way, source], chip_coords(there),
        )

    def pair_copy(way, source, part):
        which, low, high = ways[way]
        rows_of = home.at[which, source, part, low:high]
        return remote(
            rows_of, rows_of, pair_send.at[3 + way], pair_recv.at[3 + way], {"c": 1 - core}
        )

    left_copy = remote(q_part, left, left_sem.at[0], left_sem.at[1], {"s": 1 - side})

    def send_box(which):
        @pl.when(side == which)
        def _():
            loop(1, 4, lambda j: box_copy(which, (local + j) % 4, local).start())
            box[which, local] = payload(which)[local]

    def receive_box(which):
        for source in (which, which + 2):
            @pl.when(local != source)
            def _():
                box_copy(which, local, source).wait_recv()

        def piece(b):
            one, none = jnp.float32(1.0), jnp.float32(0.0)
            first_owned = jnp.where(block_slot[b] == 2 * me, one, none)
            second_owned = jnp.where(block_slot[b] == 2 * me + 1, one, none)
            return (
                box[which, which].astype(F32) * first_owned
                + box[which, which + 2].astype(F32) * second_owned
            ).astype(BF)

        def send_piece(j):
            there = (me + j) % 8
            pieces[which, there] = piece(there)
            piece_copy(which, j, me).start()

        loop(1, 8, send_piece)
        if which == 1:
            loop(1, 8, lambda j: piece_copy(2, j, me).start())
        arrived[which, me] = piece(me)

    def gather_home(way):
        which, low, high = ways[way]
        loop(1, 8, lambda j: piece_copy(way, j, (me + 8 - j) % 8).wait_recv())
        acc = arrived[which, 0, low:high].astype(F32)
        for d in range(1, 8):
            acc = acc + arrived[which, d, low:high].astype(F32)
        home_rows[which, low:high] = acc.astype(BF)
        loop(1, 16, lambda j: home_copy(way, j, chip).start())
        home[which, chip, core, low:high] = acc.astype(BF)
        pair_copy(way, chip, core).start()

    for n in range(4):
        q_part[n] = q[owned_rows(n), :].astype(BF)

    send_box(0)

    @pl.when(side == 0)
    def _():
        left_copy.start()

    @pl.when(side == 1)
    def _():
        def cast(j):
            q_t[tile(j), :] = q[tile(j), :].astype(BF)

        def move(j):
            stat[tile(j), :] = dot(row_tile(grad, j), q_t[...], 1, 1).astype(BF)

        loop(0, 4, cast)
        loop(0, 4, move)

    receive_box(0)

    @pl.when(side == 1)
    def _():
        left_copy.wait_recv()

    loop(1, 4, lambda j: quad_copy(j, (local + 4 - j) % 4).wait_recv())

    @pl.when(side == 1)
    def _():
        def normalize(n):
            rotated = dot(left[n], stat[...], 1, 0)
            first = BETA_FIRST * olds[n, 0].astype(F32) + (1.0 - BETA_FIRST) * rotated
            second = (
                BETA_SECOND * olds[n, 1].astype(F32) + (1.0 - BETA_SECOND) * rotated * rotated
            )
            left[n] = (first / (jnp.sqrt(second) + EPSILON)).astype(BF)

        loop(0, 4, normalize)
        normed = left[...].reshape(4 * rows, width)
        half[...] = dot(normed, q_t[...], 1, 0).astype(BF).reshape(4, rows, width)

    send_box(1)
    receive_box(1)
    gather_home(0)
    for slot in range(2):
        columns = pl.ds(pl.multiple_of((corner + 4 * slot) // 2 * T, T), T)
        turned[...] = q[:, columns].T
        for side_to in range(2):
            these = pl.ds(pl.multiple_of((2 * side_to + core) * rows, rows), rows)
            q_rows[2 * slot + side_to] = turned[these, :].astype(BF)
    loop(1, 4, lambda j: row_copy(1, j, local).start())
    kept_bases = pltpu.make_async_copy(q_rows.at[local], bases_out.at[local], own.at[5])
    kept_bases.start()
    gather_home(1)
    gather_home(2)

    def take_home(way):
        def take(j):
            source = (chip + 16 - j) % 16
            home_copy(way, j, source).wait_recv()
            pair_copy(way, source, core).start()

        loop(1, 16, take)

    everywhere = slice(None)
    middle = rows // 2
    take_home(0)
    take_home(1)
    for way in range(2):
        pair_copy(way, everywhere, 1 - core).wait_recv()

    def product(j, low, high):
        deep = width * (high - low) // rows
        return dot(
            home[0, :, :, low:high, tile(j)].reshape(deep, quarter),
            home[1, :, :, low:high].reshape(deep, width), 0, 0,
        )

    def multiply_first(j):
        a[tile(j), :] = product(j, 0, middle)

    def multiply_second(j):
        update[tile(j), :] = (a[tile(j), :] + product(j, middle, rows)).astype(BF)

    loop(0, 4, multiply_first)
    take_home(2)
    pair_copy(2, everywhere, 1 - core).wait_recv()
    loop(0, 4, multiply_second)

    kept_terms.wait()
    kept_bases.wait()
    for which in range(2):
        loop(1, 4, lambda j: row_copy(which, j, (local + 4 - j) % 4).wait_recv())
        loop(1, 4, lambda j: row_copy(which, j, local).wait_send())
        loop(1, 16, lambda j: state_copy(which, j, chip).wait_send())

        @pl.when(side == which)
        def _():
            loop(1, 4, lambda j: box_copy(which, (local + j) % 4, local).wait_send())

    for way in range(3):
        loop(1, 8, lambda j: piece_copy(way, j, me).wait_send())
        loop(1, 16, lambda j: home_copy(way, j, chip).wait_send())
        pair_copy(way, everywhere, core).wait_send()
    for n, ref in enumerate((old_stat, basis, grad)):
        share(ref, core, n).wait_send()
    loop(1, 8, lambda j: dp_copy(j, me).wait_send())
    loop(1, 16, lambda j: grad_copy(j, chip).wait_send())
    loop(1, 4, lambda j: quad_copy(j, local).wait_send())

    @pl.when(side == 0)
    def _():
        left_copy.wait_send()


def optimizer_step(block_slot, grads, left_stats, right_stats, first, second, left_basis, right_basis):
    rows, width = grads.shape[-2:]
    dma = pltpu.SemaphoreType.DMA
    vmem = pltpu.VMEM
    full = vmem((16, 2, rows, width), BF)
    return pl.pallas_call(
        step_kernel,
        out_shape=(
            jax.ShapeDtypeStruct((width, width), BF),
            jax.ShapeDtypeStruct((4, rows, width), F32),
            jax.ShapeDtypeStruct((4, rows, width), BF),
        ),
        in_specs=[pl.BlockSpec(memory_space=pltpu.SMEM)] + [pl.BlockSpec(memory_space=vmem)] * 5 + [ANY] * 2,
        out_specs=(pl.BlockSpec(memory_space=vmem), ANY, ANY),
        scratch_shapes=[
            vmem((8, 2, rows, width), BF),
            vmem((2, 2, rows, width), BF), vmem((2, 2, rows, width), BF),
            vmem((8, 2, rows, width), BF),
            vmem((2, rows, width), BF),
            full, full, full,
            vmem((4, 2, rows, width), BF),
            vmem((width, width), F32), vmem((width, width), F32), vmem((width, width), BF),
            vmem((3 * T, width), BF), vmem((3 * T, 2 * width), BF),
            vmem((T, T), F32), vmem((T, width), F32),
            vmem((4, rows, width), BF), vmem((4, rows, width), BF), vmem((4, rows, width), F32),
            vmem((width, width), BF),
            vmem((4, rows, width), BF), vmem((4, rows, width), BF),
            vmem((2, 4, rows, width), BF),
            vmem((2, 8, rows, width), BF), vmem((2, 8, rows, width), BF),
            vmem((2, rows, width), BF), vmem((2, 16, 2, rows, width), BF),
            dma((8,)), dma((8,)), dma((2, 16)), dma((2, 16)), dma((4,)), dma((4,)), dma((16,)), dma((16,)),
            dma((2,)), dma((2, 4)), dma((2, 4)), dma((2, 4)), dma((2, 4)), dma((3, 8)), dma((3, 8)),
            dma((3, 16)), dma((3, 16)), dma((6,)), dma((6,)), dma((6,)),
        ],
        compiler_params=pltpu.CompilerParams(
            collective_id=0, has_side_effects=True, vmem_limit_bytes=56 * 2**20
        ),
    )(block_slot, grads, left_stats, right_stats, first, second, left_basis, right_basis)


def per_device(
    grads, block_slot, left_stats, right_stats, left_basis, right_basis, first_moment, second_moment
):
    capacity, rows, width = left_stats.shape
    slot_ids = lax.axis_index("dp") * capacity + jnp.arange(capacity, dtype=jnp.int32)
    owns = block_slot[:, None] == slot_ids[None, :]
    held_mask = jnp.any(owns, axis=0)[:, None, None]

    update, terms, new_bases = optimizer_step(
        block_slot,
        grads[0],
        left_stats,
        right_stats,
        first_moment,
        second_moment,
        left_basis,
        right_basis,
    )

    def merged(new, old):
        return jnp.where(held_mask, new, old)

    terms = terms.reshape(2, 2, rows, width)
    new_bases = new_bases.reshape(2, 2, rows, width)
    return (
        update[None],
        merged(BETA_STATS * left_stats + (1.0 - BETA_STATS) * terms[:, 0], left_stats),
        merged(BETA_STATS * right_stats + (1.0 - BETA_STATS) * terms[:, 1], right_stats),
        merged(new_bases[:, 0], left_basis),
        merged(new_bases[:, 1], right_basis),
    )


def solution(mesh):
    groups = mesh.shape["dp"]
    fine = Mesh(mesh.devices.reshape(groups, 2, 2, 2, 2, 2), ("dp",) + MP)
    rows = P("dp", MP, None)
    return jax.shard_map(
        per_device,
        mesh=fine,
        in_specs=(P("dp", None, MP, None), P()) + (rows,) * 6,
        out_specs=(P("dp", None, None),) + (rows,) * 4,
        check_vma=False,
    )
```
